32 devices in a mesh: dp: 8 (over z, y), expert: 4 (over x, core).
Axes of the slice: x: 2, y: 2, z: 4, core: 2. Of those that a mesh axis runs over, the one named last changes fastest.
Arguments:
- tokens: bfloat16 [128, 6144], P(('dp', 'expert')), may hold values from -6 to 6
- expert_choice_table: int32 [4, 32], P('expert'), may hold values from 0 to 1, as said below
- gate_weight: bfloat16 [6144, 16384], P(None, ('dp', 'expert')), may hold values from -0.078125 to 0.078125
- up_weight: bfloat16 [6144, 16384], P(None, ('dp', 'expert')), may hold values from -0.078125 to 0.078125
- down_weight: bfloat16 [16384, 6144], P(('dp', 'expert')), may hold values from -0.0625 to 0.0625
- adapter_down_shared: bfloat16 [6144, 64], P('dp'), may hold values from -0.078125 to 0.078125
- adapter_gate_factor: bfloat16 [64, 16384], P(None, ('dp', 'expert')), may hold values from -0.75 to 0.75
- router: bfloat16 [6144, 2], replicated, may hold values from -0.078125 to 0.078125
Outputs:
- mixed: bfloat16 [128, 6144], P(('dp', 'expert'))
- grad_a: float32 [6144, 64], P(('dp', 'expert'))
- grad_b: float32 [16384, 64], P(('dp', 'expert'))
The draws below stay inside these ranges and needn't reach their ends.
Inputs may be any that keep to these rules, and one draw needn't show every extreme that they name: Every row of expert_choice_table names every expert exactly 2 * 8 times.
All inputs are finite; a program needn't handle non-finite values.
Results may differ from the reference program's by a relative error of at most 0.014.
Values may be sent and summed in bfloat16 or wider, within the bound.
No kernel may reach another device: no remote copies, remote signals or barrier semaphores. Data moves between devices by JAX's collectives and lax.ppermute only.
A program may use at most 128 MiB of HBM per device.

```python
import math
import jax
import jax.numpy as jnp
from jax import lax

MODEL_WIDTH = 6144
WIN = 8192
ADAPTER_RANK = 64
TOK = 4
EXPERT_COUNT = 2
EXPERT_HIDDEN = 512
TOKENS = 128
N_DP = 8
N_EXPERT = 4


def draw_expert_choice_table(key, part):
    count = N_DP * TOK
    keys = jax.random.split(key, N_EXPERT)
    perms = jax.vmap(lambda k: jax.random.permutation(k, count))(keys)
    return (perms // (count // EXPERT_COUNT)).astype(jnp.int32)


def raised(result, rng, source, target, shards_of, factor):
    owner, partner = [(jnp.arange(result.shape[axis_at]) // (result.shape[axis_at] // shards_of)).reshape([-1 if axis == axis_at else 1 for axis in range(result.ndim)]) for axis_at in (source, target)]
    chosen = jax.random.permutation(rng, shards_of)[partner]
    strong = (owner == chosen) | (owner == (partner + shards_of // 2) % shards_of)
    return jnp.where(strong, factor * result, result)


def level_of(rng, dims, shards, least, top_value):
    loudness, own = 1.0, jax.random.fold_in(rng, 6)
    for dim, shards_of in shards:
        heights = jnp.exp(jax.random.uniform(jax.random.fold_in(own, dim), (shards_of,), jnp.float32, least / len(shards), top_value / len(shards)))
        loudness = loudness * jnp.repeat(heights, dims[dim] // shards_of).reshape([-1 if axis == dim else 1 for axis in range(len(dims))])
    return loudness


def gaussian(rng, dims, deviation, reach, cuts=(), kind=jnp.bfloat16):
    values = deviation * jax.random.normal(rng, dims, jnp.float32)
    if cuts:
        values = values * level_of(rng, dims, cuts, -0.22, 0.18)
    return jnp.clip(values, -reach, reach).astype(kind)


def bell_draw_with(stream_key, dims, scale, most, cuts, heavy, held_as=jnp.bfloat16):
    entries = scale * jax.random.normal(stream_key, dims, jnp.float32)
    if cuts:
        entries = entries * level_of(stream_key, dims, cuts, -0.22, 0.18)
    return jnp.clip(raised(entries, jax.random.fold_in(stream_key, 3), *heavy), -most, most).astype(held_as)


def setup_inputs(seed: int = 0) -> dict:
    splits = jax.random.split(jax.random.key(seed), 9)
    tokens = bell_draw_with(splits[0], (TOKENS, MODEL_WIDTH), 1.0, 6.0, ((0, 32),), (0, 1, 32, 2.75))
    expert_choice_table = draw_expert_choice_table(jax.random.fold_in(splits[8], 71), 0)
    gate_weight = gaussian(splits[2], (MODEL_WIDTH, N_DP * N_EXPERT * EXPERT_HIDDEN), MODEL_WIDTH ** -0.5, 0.078125, ((1, 32),))
    up_weight = gaussian(splits[3], (MODEL_WIDTH, N_DP * N_EXPERT * EXPERT_HIDDEN), MODEL_WIDTH ** -0.5, 0.078125, ((1, 32),))
    down_weight = gaussian(splits[4], (N_DP * N_EXPERT * EXPERT_HIDDEN, MODEL_WIDTH), WIN ** -0.5, 0.0625, ((0, 32),))
    adapter_down_shared = gaussian(splits[5], (MODEL_WIDTH, ADAPTER_RANK), MODEL_WIDTH ** -0.5, 0.078125, ((0, 8),))
    adapter_gate_factor = gaussian(splits[6], (ADAPTER_RANK, N_DP * N_EXPERT * EXPERT_HIDDEN), ADAPTER_RANK ** -0.5, 0.75, ((1, 32),))
    router = gaussian(splits[7], (MODEL_WIDTH, EXPERT_COUNT), MODEL_WIDTH ** -0.5, 0.078125)
    return dict(tokens=tokens, expert_choice_table=expert_choice_table, gate_weight=gate_weight, up_weight=up_weight, down_weight=down_weight, adapter_down_shared=adapter_down_shared, adapter_gate_factor=adapter_gate_factor, router=router)


adapter_scale = 0.25

def silu_slope(pre):
    sig = jax.nn.sigmoid(pre)
    return sig * (1.0 + pre * (1.0 - sig))

def expert_forward(block_index, grouped_rows, gate_weight, up_weight, down_weight, adapter_down_shared, adapter_gate_factor, router, loss_weight_factor):
    column_width = 2 * EXPERT_HIDDEN
    token_rows = lax.dynamic_index_in_dim(grouped_rows, block_index, 0, keepdims=False)
    gate_cols = lax.dynamic_index_in_dim(gate_weight.reshape(MODEL_WIDTH, N_DP, EXPERT_COUNT, column_width), block_index, 2, keepdims=False).reshape(MODEL_WIDTH, N_DP * column_width)
    up_cols = lax.dynamic_index_in_dim(up_weight.reshape(MODEL_WIDTH, N_DP, EXPERT_COUNT, column_width), block_index, 2, keepdims=False).reshape(MODEL_WIDTH, N_DP * column_width)
    latent_columns = lax.dynamic_index_in_dim(adapter_gate_factor.reshape(ADAPTER_RANK, N_DP, EXPERT_COUNT, column_width), block_index, 2, keepdims=False).reshape(ADAPTER_RANK, N_DP * column_width)
    out_rows = lax.dynamic_index_in_dim(down_weight.reshape(N_DP, EXPERT_COUNT, column_width, MODEL_WIDTH), block_index, 1, keepdims=False)
    route_col = lax.dynamic_index_in_dim(router, block_index, 1, keepdims=False)
    count = token_rows.shape[0]
    adapter_latent = jnp.dot(token_rows, adapter_down_shared, preferred_element_type=jnp.float32).astype(jnp.bfloat16)
    pre = jnp.dot(token_rows, gate_cols, preferred_element_type=jnp.float32) + adapter_scale * jnp.dot(adapter_latent, latent_columns, preferred_element_type=jnp.float32)
    lifted = jnp.dot(token_rows, up_cols, preferred_element_type=jnp.float32)
    hidden = (jax.nn.silu(pre) * lifted).astype(jnp.bfloat16)
    blocks = hidden.reshape(count, N_DP, column_width).transpose(1, 0, 2)

    def add_block(total, items):
        term = jnp.dot(items[0], items[1], preferred_element_type=jnp.float32).astype(jnp.bfloat16)
        return (total + term.astype(jnp.float32), None)
    total, unused = lax.scan(add_block, jnp.zeros((count, MODEL_WIDTH), jnp.float32), (blocks, out_rows))
    gate = jax.nn.sigmoid(jnp.dot(token_rows, route_col, preferred_element_type=jnp.float32))
    mixed = (gate[:, None] * total).astype(jnp.bfloat16)
    back_part = (loss_weight_factor * gate[:, None] * (mixed.astype(jnp.float32) - token_rows.astype(jnp.float32))).astype(jnp.bfloat16)
    flat_rows = out_rows.reshape(N_DP * column_width, MODEL_WIDTH)
    back_hidden = jnp.dot(back_part, flat_rows.T, preferred_element_type=jnp.float32)
    back_pre = (back_hidden * lifted * silu_slope(pre)).astype(jnp.bfloat16)
    back_low = adapter_scale * jnp.dot(back_pre, latent_columns.T, preferred_element_type=jnp.float32)
    grad_a = jnp.dot(token_rows.astype(jnp.float32).T, back_low, precision=lax.Precision.HIGHEST)
    grad_b = adapter_scale * jnp.dot(back_pre.T, adapter_latent, preferred_element_type=jnp.float32)
    return (mixed, grad_a, grad_b)

def reference(tokens, expert_choice_table, gate_weight, up_weight, down_weight, adapter_down_shared, adapter_gate_factor, router):
    per_expert = TOKENS // EXPERT_COUNT
    labels = expert_choice_table.reshape(N_EXPERT, N_DP, TOK).transpose(1, 0, 2).reshape(TOKENS)
    order = jnp.argsort(labels, stable=True).astype(jnp.int32)
    grouped_rows = jnp.take(tokens, order, axis=0).reshape(EXPERT_COUNT, per_expert, MODEL_WIDTH)
    loss_weight_factor = math.sqrt(EXPERT_COUNT / TOKENS)

    def one_expert(block_index):
        return expert_forward(block_index, grouped_rows, gate_weight, up_weight, down_weight, adapter_down_shared, adapter_gate_factor, router, loss_weight_factor)
    mixed, grad_a, grad_b = lax.map(one_expert, jnp.arange(EXPERT_COUNT, dtype=jnp.int32))
    output = jnp.zeros((TOKENS, MODEL_WIDTH), jnp.bfloat16).at[order].set(mixed.reshape(TOKENS, MODEL_WIDTH))
    grad_b_rows = grad_b.reshape(EXPERT_COUNT, N_DP, 2 * EXPERT_HIDDEN, ADAPTER_RANK).transpose(1, 0, 2, 3).reshape(N_DP * N_EXPERT * EXPERT_HIDDEN, ADAPTER_RANK)
    return (output, lax.optimization_barrier(jnp.sum(grad_a, axis=0)), grad_b_rows)
```

```python
import math

import jax
import jax.numpy as jnp
from jax import lax
from jax.sharding import Mesh, PartitionSpec as P

adapter_scale = 0.25
bf16, f32 = jnp.bfloat16, jnp.float32


def swap(block, axis):
    return lax.ppermute(block, axis, [(0, 1), (1, 0)])


def exchange(blocks, axis):
    return lax.all_to_all(blocks, axis, 0, 0, tiled=True)


def spread(block, axis):
    count = lax.axis_size(axis)
    return exchange(jnp.broadcast_to(block[None], (count, *block.shape)), axis)


def trade_groups(blocks, axis):
    count = lax.axis_size(axis)
    arrived = [blocks[0]]
    for step in range(1, count):
        route = [(i, (i + step) % count) for i in range(count)]
        arrived.append(lax.ppermute(blocks[step], axis, route))
    return arrived


def dot(left, right):
    return jnp.dot(left, right, preferred_element_type=f32)


def dot_last(left, right):
    return lax.dot_general(left, right, (((1,), (1,)), ((), ())), preferred_element_type=f32)


def dot_first(left, right):
    return lax.dot_general(left, right, (((0,), (0,)), ((), ())), preferred_element_type=f32)


def shards(
    tokens,
    expert_choice_table,
    gate_weight,
    up_weight,
    down_weight,
    adapter_down_shared,
    adapter_gate_factor,
    router,
):
    tok_rows, width = tokens.shape
    n_dp = lax.axis_size("dp")
    groups = lax.axis_size("x")
    place = lax.axis_index("dp")
    group = lax.axis_index("x")
    core = lax.axis_index("core")
    col_rows = n_dp * tok_rows
    capacity = col_rows // groups
    half = groups * capacity
    rank = adapter_down_shared.shape[1]
    depth = adapter_down_shared.shape[0]
    wide = width // n_dp
    share = width // (n_dp * groups * 2)
    loss_factor = math.sqrt(groups / (tok_rows * n_dp * groups * 2))

    column = spread(tokens, "dp").reshape(col_rows, width)
    labels = expert_choice_table[0]
    index = jnp.arange(col_rows, dtype=jnp.int32)
    before = (labels[None, :] == labels[:, None]) & (index[None, :] < index[:, None])
    ordinal = jnp.sum(before.astype(jnp.int32), axis=1)
    ahead = lax.rem(labels - group + groups, groups)
    target = ahead * capacity + ordinal
    placer = (index[:, None] == target[None, :]).astype(bf16)
    packed = dot(placer, column).astype(bf16).reshape(groups, capacity, width)
    own_half = jnp.concatenate(trade_groups(packed, "x"), axis=0)
    rows = jnp.concatenate([own_half, swap(own_half, "core")], axis=0)

    piece = lax.dynamic_slice_in_dim(rows, place * depth, depth, 1)
    low_part = dot(piece, adapter_down_shared)
    low = jnp.sum(spread(low_part, "dp"), axis=0).astype(bf16)

    pre = dot(rows, gate_weight) + adapter_scale * dot(low, adapter_gate_factor)
    lifted = dot(rows, up_weight)
    hidden = (jax.nn.silu(pre) * lifted).astype(bf16)
    partial = dot(hidden, down_weight)

    logits = dot(rows, router)
    picker = (jnp.arange(groups, dtype=jnp.int32) == group).astype(f32)
    gate = jax.nn.sigmoid(jnp.sum(logits * picker[None, :], axis=1))

    summed = (partial[:half] + swap(partial[half:].astype(bf16), "core").astype(f32)).astype(bf16)
    blocks = exchange(summed.reshape(half, n_dp, wide).transpose(1, 0, 2), "dp")
    total = jnp.sum(blocks.astype(f32), axis=0)
    mixed_block = (gate[:half, None] * total).astype(bf16)
    mixed_half = spread(mixed_block, "dp").transpose(1, 0, 2).reshape(half, width)
    mixed = jnp.concatenate([mixed_half, swap(mixed_half, "core")], axis=0)

    back = mixed_half.reshape(groups, capacity, width)
    returned = [back[0]] + [None] * (groups - 1)
    for step in range(1, groups):
        route = [(i, (i - step) % groups) for i in range(groups)]
        returned[step] = lax.ppermute(back[step], "x", route)
    unpacked = jnp.concatenate(returned, axis=0)
    own_target = lax.dynamic_slice_in_dim(target, place * tok_rows, tok_rows, 0)
    chooser = (own_target[:, None] == index[None, :]).astype(bf16)
    result = dot(chooser, unpacked).astype(bf16)

    back_rows = (
        loss_factor * gate[:, None] * (mixed.astype(f32) - rows.astype(f32))
    ).astype(bf16)
    back_hidden = dot_last(back_rows, down_weight)
    sig = jax.nn.sigmoid(pre)
    back_pre = (back_hidden * lifted * (sig * (1.0 + pre * (1.0 - sig)))).astype(bf16)
    back_low = adapter_scale * dot_last(back_pre, adapter_gate_factor)
    grad_b = adapter_scale * dot_first(back_pre, low)

    pieces = []
    for step in range(groups):
        to = lax.rem(group + step, groups)
        at = ((place * groups + to) * 2 + core) * share
        pieces.append(lax.dynamic_slice_in_dim(rows, at, share, 1))
    pieces = trade_groups(pieces, "x")
    gathered = spread(back_low.astype(bf16), ("dp", "x", "core"))
    parts = jnp.sum(
        gathered.reshape(n_dp, groups, 2, 2, half, rank).astype(f32), axis=0
    )
    by_core = jnp.stack([parts[:, 0, 0] + parts[:, 1, 1], parts[:, 0, 1] + parts[:, 1, 0]])
    by_core = jnp.where(core == 0, by_core, by_core[::-1])
    grad_a = jnp.zeros((share, rank), f32)
    for step in range(groups):
        source = lax.rem(group - step + groups, groups)
        low_rows = lax.dynamic_index_in_dim(by_core, source, 1, keepdims=False)
        grad_a = grad_a + lax.dot_general(
            pieces[step].astype(f32),
            low_rows.reshape(2 * half, rank),
            (((0,), (0,)), ((), ())),
            precision=lax.Precision.HIGHEST,
        )
    return (result, grad_a, grad_b)


def solution(mesh):
    n_dp, n_expert = mesh.shape["dp"], mesh.shape["expert"]
    split = Mesh(mesh.devices.reshape(n_dp, n_expert // 2, 2), ("dp", "x", "core"))
    every = ("dp", "x", "core")
    return jax.shard_map(
        shards,
        mesh=split,
        in_specs=(
            P(every, None),
            P(("x", "core"), None),
            P(None, every),
            P(None, every),
            P(every, None),
            P("dp", None),
            P(None, every),
            P(),
        ),
        out_specs=(P(every, None), P(every, None), P(every, None)),
        check_vma=False,
    )
```

```python
import functools
import math

import jax
import jax.numpy as jnp
from jax import lax
from jax.experimental import pallas as pl
from jax.experimental.pallas import tpu as pltpu
from jax.sharding import Mesh, PartitionSpec as P

adapter_scale = 0.25
bf16, f32 = jnp.bfloat16, jnp.float32
VMEM_LIMIT = 20 * 2**20
every = ("dp", "x", "core")


def swap(block, axis):
    return lax.ppermute(block, axis, [(0, 1), (1, 0)])


def exchange(blocks, axis):
    return lax.all_to_all(blocks, axis, 0, 0, tiled=True)


def dot(left, right):
    return jnp.dot(left, right, preferred_element_type=f32)


def dot_last(left, right):
    return lax.dot_general(left, right, (((1,), (1,)), ((), ())), preferred_element_type=f32)


def dot_first(left, right):
    return lax.dot_general(left, right, (((0,), (0,)), ((), ())), preferred_element_type=f32)


def sigmoid(v):
    return 1.0 / (1.0 + jnp.exp(-v))


def struct(shape, dtype):
    return jax.ShapeDtypeStruct(shape, dtype)


def vmem(count):
    return [pl.BlockSpec(memory_space=pltpu.VMEM)] * count


def params():
    return pltpu.CompilerParams(vmem_limit_bytes=VMEM_LIMIT)


def cost(flops, moved):
    return pl.CostEstimate(flops=int(flops), bytes_accessed=int(moved), transcendentals=0)


def beside(rows):
    half = rows.shape[0] // 2
    return jnp.concatenate([rows[:half], rows[half:]], axis=1)


def apart(wide):
    rank = wide.shape[1] // 2
    return jnp.concatenate([wide[:, :rank], wide[:, rank:]], axis=0)


def low_kernel(n_parts, place_ref, *refs):
    parts, factor_ref, out_ref = refs[:n_parts], refs[n_parts], refs[n_parts + 1]
    depth = factor_ref.shape[1]
    if depth < parts[0].shape[1]:
        at = pl.ds(pl.multiple_of(place_ref[0] * depth, depth), depth)
        rows = jnp.concatenate([r[:, at] for r in parts], axis=0)
    else:
        rows = jnp.concatenate([r[...] for r in parts], axis=0)
    piece = beside(dot_last(rows, factor_ref[...]))
    for i in range(out_ref.shape[0]):
        out_ref[i] = piece


def low_pieces(parts, factor, place, n_dp):
    rank, depth = factor.shape
    half = parts[0].shape[0] * len(parts) // 2
    if depth % 128:
        parts = [lax.dynamic_slice_in_dim(part, place * depth, depth, 1) for part in parts]
    return pl.pallas_call(
        functools.partial(low_kernel, len(parts)),
        in_specs=[pl.BlockSpec(memory_space=pltpu.SMEM)] + vmem(len(parts) + 1),
        out_specs=vmem(1)[0],
        out_shape=struct((n_dp, half, 2 * rank), f32),
        compiler_params=params(),
        name="low_pieces",
    )(place.reshape(1), *parts, factor)


def lift_kernel(n_parts, *refs):
    parts = refs[:n_parts]
    weight_ref, up_ref, route_ref, pre_ref, lifted_ref, gate_ref, weight, up, sems = refs[n_parts:]
    width = parts[0].shape[1]
    steps = sems.shape[1]
    chunk = width // steps
    copies = []
    for k in range(steps):
        at = pl.ds(k * chunk, chunk)
        copies.append(
            (
                pltpu.make_async_copy(weight_ref.at[at], weight.at[at], sems.at[0, k]),
                pltpu.make_async_copy(up_ref.at[at], up.at[at], sems.at[1, k]),
            )
        )
    ahead = 4
    for pair in copies[:ahead]:
        pair[0].start()
        pair[1].start()
    pre = lifted = logit = 0.0
    for k in range(steps):
        at = slice(k * chunk, (k + 1) * chunk)
        for i in (0, 1):
            copies[k][i].wait()
            if k + ahead < steps:
                copies[k + ahead][i].start()
        rows = jnp.concatenate([r[:, at] for r in parts], axis=0)
        pre = pre + dot(rows, weight[at])
        lifted = lifted + dot(rows, up[at])
        logit = logit + jnp.sum(rows.astype(f32) * route_ref[:, at], axis=1, keepdims=True)
    pre_ref[...] = pre
    lifted_ref[...] = lifted
    gate_ref[...] = sigmoid(logit)


def lift(parts, gate_weight, up_weight, route):
    capacity, width = parts[0].shape
    units = gate_weight.shape[1]
    count = capacity * len(parts)
    return pl.pallas_call(
        functools.partial(lift_kernel, len(parts)),
        in_specs=vmem(len(parts)) + [pl.BlockSpec(memory_space=pl.ANY)] * 2 + vmem(1),
        out_specs=vmem(3),
        scratch_shapes=[
            pltpu.VMEM(gate_weight.shape, bf16),
            pltpu.VMEM(up_weight.shape, bf16),
            pltpu.SemaphoreType.DMA((2, 12)),
        ],
        out_shape=(
            struct((count, units), f32),
            struct((count, units), f32),
            struct((count, 1), f32),
        ),
        cost_estimate=cost(4 * count * width * units, 4 * width * units),
        compiler_params=params(),
        name="lift",
    )(
        *parts,
        pltpu.with_memory_space_constraint(gate_weight, pltpu.HBM),
        pltpu.with_memory_space_constraint(up_weight, pltpu.HBM),
        route,
    )


def bring(source, target, sems, blocks, wide):
    copies, ahead = [], 4
    for k in range(blocks):
        at = pl.ds(k * wide, wide)
        copies.append(pltpu.make_async_copy(source.at[:, at], target.at[:, at], sems.at[k]))
    for copy in copies[:ahead]:
        copy.start()

    def arrive(k):
        copies[k].wait()
        if k + ahead < blocks:
            copies[k + ahead].start()

    return arrive


def down_kernel(
    base_ref, lifted_ref, low_ref, factor_ref, weight_ref, own_ref, other_ref, pre_ref, low_out, down_ref, sems
):
    blocks, half, wide = own_ref.shape
    arrive = bring(weight_ref, down_ref, sems, blocks, wide)
    low = apart(jnp.sum(low_ref[...], axis=0)).astype(bf16)
    pre = base_ref[...] + adapter_scale * dot(low, factor_ref[...])
    low_out[...] = low
    pre_ref[...] = pre
    hidden = (pre * sigmoid(pre) * lifted_ref[...]).astype(bf16)
    for k in range(blocks):
        arrive(k)
        partial = dot(hidden, down_ref[:, k * wide : (k + 1) * wide]).astype(bf16)
        own_ref[k] = partial[:half]
        other_ref[k] = partial[half:]


def down(base, lifted, low_parts, factor, down_weight, blocks):
    count, units = base.shape
    half, width = count // 2, down_weight.shape[1]
    shape = struct((blocks, half, width // blocks), bf16)
    return pl.pallas_call(
        down_kernel,
        in_specs=vmem(4) + [pl.BlockSpec(memory_space=pl.ANY)],
        out_specs=vmem(4),
        scratch_shapes=[pltpu.VMEM(down_weight.shape, bf16), pltpu.SemaphoreType.DMA((blocks,))],
        out_shape=(shape, shape, struct((count, units), f32), struct((count, factor.shape[0]), bf16)),
        cost_estimate=cost(2 * count * width * units, 2 * width * units),
        compiler_params=params(),
        name="down",
    )(base, lifted, low_parts, factor, pltpu.with_memory_space_constraint(down_weight, pltpu.HBM))


def mix_kernel(blocks_ref, gate_ref, out_ref):
    half = out_ref.shape[1]
    total = blocks_ref[0].astype(f32)
    for i in range(1, blocks_ref.shape[0]):
        total = total + blocks_ref[i].astype(f32)
    mixed = (gate_ref[:half] * total).astype(bf16)
    for i in range(out_ref.shape[0]):
        out_ref[i] = mixed


def mix(blocks, gate):
    return pl.pallas_call(
        mix_kernel,
        in_specs=vmem(2),
        out_specs=vmem(1)[0],
        out_shape=struct(blocks.shape, bf16),
        compiler_params=params(),
        name="mix",
    )(blocks, gate)


def back_kernel(n_parts, loss_factor, *refs):
    parts = refs[:n_parts]
    (
        own_ref,
        other_ref,
        gate_ref,
        weight_ref,
        pre_ref,
        lifted_ref,
        low_ref,
        factor_ref,
        low_out,
        grad_ref,
        down_ref,
        sems,
    ) = refs[n_parts:]
    blocks, half, wide = own_ref.shape
    arrive = bring(weight_ref, down_ref, sems, blocks, wide)
    scale = loss_factor * gate_ref[...]
    total = 0.0
    for k in range(blocks):
        at = slice(k * wide, (k + 1) * wide)
        mixed = jnp.concatenate([own_ref[k], other_ref[k]], axis=0).astype(f32)
        rows = jnp.concatenate([r[:, at] for r in parts], axis=0).astype(f32)
        back = (scale * (mixed - rows)).astype(bf16)
        arrive(k)
        total = total + dot_last(down_ref[:, at], back)
    pre = pre_ref[...]
    sig = sigmoid(pre)
    slope = sig * (1.0 + pre * (1.0 - sig))
    back_pre = (total.T * lifted_ref[...] * slope).astype(bf16)
    back_low = beside(adapter_scale * dot_last(back_pre, factor_ref[...])).astype(bf16)
    for i in range(low_out.shape[0]):
        low_out[i] = back_low
    grad_ref[...] = adapter_scale * dot_first(low_ref[...], back_pre)


def back(parts, own, other, gate, down_weight, pre, lifted, low, factor, loss_factor, copies):
    width = parts[0].shape[1]
    half = own.shape[1]
    count, units = pre.shape
    rank = factor.shape[0]
    return pl.pallas_call(
        functools.partial(back_kernel, len(parts), loss_factor),
        in_specs=vmem(len(parts) + 3) + [pl.BlockSpec(memory_space=pl.ANY)] + vmem(4),
        out_specs=vmem(2),
        scratch_shapes=[pltpu.VMEM(down_weight.shape, bf16), pltpu.SemaphoreType.DMA((own.shape[0],))],
        out_shape=(struct((copies, half, 2 * rank), bf16), struct((rank, units), f32)),
        cost_estimate=cost(2 * count * width * units, 2 * width * units),
        compiler_params=params(),
        name="back",
    )(
        *parts,
        own,
        other,
        gate,
        pltpu.with_memory_space_constraint(down_weight, pltpu.HBM),
        pre,
        lifted,
        low,
        factor,
    )


def factor_kernel(place_ref, low_ref, piece_ref, out_ref):
    rank = out_ref.shape[0]
    groups = piece_ref.shape[0]
    group, core = place_ref[0], place_ref[1]
    total = 0.0
    for g in range(groups):
        mine = jnp.sum(low_ref[:, g, core].astype(f32), axis=0)
        theirs = jnp.sum(low_ref[:, g, 1 - core].astype(f32), axis=0)
        low = jnp.concatenate(
            [mine[:, :rank] + theirs[:, rank:], mine[:, rank:] + theirs[:, :rank]], axis=0
        )
        high = low.astype(bf16)
        rest = (low - high.astype(f32)).astype(bf16)
        piece = piece_ref[lax.rem(group - g + groups, groups)]
        total = total + dot_first(high, piece) + dot_first(rest, piece)
    out_ref[...] = total


def factor_gradient(lows, pieces, group, core):
    rank, share = lows.shape[-1] // 2, pieces.shape[2]
    return pl.pallas_call(
        factor_kernel,
        in_specs=[pl.BlockSpec(memory_space=pltpu.SMEM)] + vmem(2),
        out_specs=vmem(1)[0],
        out_shape=struct((rank, share), f32),
        compiler_params=params(),
        name="factor_gradient",
    )(jnp.stack([group, core]), lows, pieces)


def shards(
    tokens,
    expert_choice_table,
    gate_weight,
    up_weight,
    down_weight,
    adapter_down_shared,
    adapter_gate_factor,
    router,
):
    tok_rows, width = tokens.shape
    n_dp = lax.axis_size("dp")
    groups = lax.axis_size("x")
    place = lax.axis_index("dp")
    group = lax.axis_index("x")
    core = lax.axis_index("core")
    col_rows = n_dp * tok_rows
    capacity = col_rows // groups
    half = groups * capacity
    wide = width // n_dp
    rank = adapter_down_shared.shape[1]
    devices = n_dp * groups * 2
    share = width // devices
    loss_factor = math.sqrt(groups / (tok_rows * devices))
    blocks = 8

    def regroup(array, pieces):
        if array.shape[0] == pieces:
            return array
        flat = array.transpose(1, 0, 2).reshape(array.shape[1], width)
        return flat.reshape(array.shape[1], pieces, width // pieces).transpose(1, 0, 2)

    column = exchange(jnp.broadcast_to(tokens[None], (n_dp, tok_rows, width)), "dp")
    column = column.reshape(col_rows, width)
    labels = expert_choice_table[0]
    index = jnp.arange(col_rows, dtype=jnp.int32)
    before = (labels[None, :] == labels[:, None]) & (index[None, :] < index[:, None])
    ordinal = jnp.sum(before.astype(jnp.int32), axis=1)
    ahead = lax.rem(labels - group + groups, groups)
    target = ahead * capacity + ordinal
    placer = (index[:, None] == target[None, :]).astype(bf16)
    packed = dot(placer, column).astype(bf16).reshape(groups, capacity, width)
    parts = [packed[0]]
    for step in range(1, groups):
        route = [(i, (i + step) % groups) for i in range(groups)]
        parts.append(lax.ppermute(packed[step], "x", route))
    parts = parts + [swap(part, "core") for part in parts]

    low_parts = exchange(low_pieces(parts, adapter_down_shared.T, place, n_dp), "dp")
    own_route = lax.dynamic_slice_in_dim(router.T, group, 1, 0).astype(f32)
    base, lifted, gate = lift(parts, gate_weight, up_weight, own_route)
    own, other, pre, low = down(base, lifted, low_parts, adapter_gate_factor, down_weight, blocks)

    summed = (own.astype(f32) + swap(other, "core").astype(f32)).astype(bf16)
    rows = jnp.concatenate(parts, axis=0)
    pieces = []
    for step in range(groups):
        to = lax.rem(group + step, groups)
        at = ((place * groups + to) * 2 + core) * share
        piece = lax.dynamic_slice_in_dim(rows, at, share, 1)
        route = [(i, (i + step) % groups) for i in range(groups)]
        pieces.append(lax.ppermute(piece, "x", route) if step else piece)
    pieces = jnp.stack(pieces)

    totals, pieces = lax.optimization_barrier((exchange(regroup(summed, n_dp), "dp"), pieces))
    mixed = mix(totals, gate)
    mixed_half = regroup(exchange(mixed, "dp"), blocks)
    mixed_other = swap(mixed_half, "core")

    back_low, grad_b = back(
        parts,
        mixed_half,
        mixed_other,
        gate,
        down_weight,
        pre,
        lifted,
        low,
        adapter_gate_factor,
        loss_factor,
        devices,
    )
    lows = exchange(back_low, every).reshape(n_dp, groups, 2, half, 2 * rank)

    returned = [mixed_half[:, :capacity]]
    for step in range(1, groups):
        route = [(i, (i - step) % groups) for i in range(groups)]
        part = mixed_half[:, step * capacity : (step + 1) * capacity]
        returned.append(lax.ppermute(part, "x", route))
    own_target = lax.dynamic_slice_in_dim(target, place * tok_rows, tok_rows, 0)
    result = jnp.zeros((tok_rows, width), f32)
    for step in range(groups):
        spot = index[step * capacity : (step + 1) * capacity]
        chooser = (own_target[:, None] == spot[None, :]).astype(bf16)
        chosen = jnp.einsum("ir,brc->ibc", chooser, returned[step], preferred_element_type=f32)
        result = result + chosen.reshape(tok_rows, width)

    grad_a = factor_gradient(lows, pieces, group, core)
    return (result.astype(bf16), grad_a.T, grad_b.T)


def solution(mesh):
    n_dp, n_expert = mesh.shape["dp"], mesh.shape["expert"]
    split = Mesh(mesh.devices.reshape(n_dp, n_expert // 2, 2), every)
    return jax.shard_map(
        shards,
        mesh=split,
        in_specs=(
            P(every, None),
            P(("x", "core"), None),
            P(None, every),
            P(None, every),
            P(every, None),
            P("dp", None),
            P(None, every),
            P(),
        ),
        out_specs=(P(every, None), P(every, None), P(every, None)),
        check_vma=False,
    )
```

```python
import functools
import math

import jax
import jax.numpy as jnp
from jax import lax
from jax.experimental import pallas as pl
from jax.experimental.pallas import tpu as pltpu
from jax.sharding import Mesh, PartitionSpec as P

adapter_scale = 0.25
bf16, f32 = jnp.bfloat16, jnp.float32
VMEM_LIMIT = 20 * 2**20
every = ("dp", "x", "core")
NEAR = (0, 2, 4, 6, 1, 3, 5, 7)


def swap(block, axis):
    return lax.ppermute(block, axis, [(0, 1), (1, 0)])


def across(block, axis, apart_by):
    count = lax.axis_size(axis)
    return lax.ppermute(block, axis, [(i, i ^ apart_by) for i in range(count)])


def gather_eight(block):
    near = across(block, "dp", 1)
    far = [across(block, "dp", bits) for bits in NEAR[1:4]]
    return [block, *far, near, *[across(other, "dp", 1) for other in far]]


def exchange(blocks, axis):
    return lax.all_to_all(blocks, axis, 0, 0, tiled=True)


def dot(left, right):
    return jnp.dot(left, right, preferred_element_type=f32)


def dot_last(left, right):
    return lax.dot_general(left, right, (((1,), (1,)), ((), ())), preferred_element_type=f32)


def dot_first(left, right):
    return lax.dot_general(left, right, (((0,), (0,)), ((), ())), preferred_element_type=f32)


def sigmoid(v):
    return 1.0 / (1.0 + jnp.exp(-v))


def struct(shape, dtype):
    return jax.ShapeDtypeStruct(shape, dtype)


def vmem(count):
    return [pl.BlockSpec(memory_space=pltpu.VMEM)] * count


def params():
    return pltpu.CompilerParams(vmem_limit_bytes=VMEM_LIMIT)


def cost(flops, moved):
    return pl.CostEstimate(flops=int(flops), bytes_accessed=int(moved), transcendentals=0)


def beside(rows):
    half = rows.shape[0] // 2
    return jnp.concatenate([rows[:half], rows[half:]], axis=1)


def apart(wide):
    rank = wide.shape[1] // 2
    return jnp.concatenate([wide[:, :rank], wide[:, rank:]], axis=0)


def pack_kernel(n_blocks, placer_ref, *refs):
    blocks = refs[:n_blocks]
    outs = refs[n_blocks:]
    capacity, width = outs[0].shape
    chunk = width // 6
    for k in range(6):
        at = slice(k * chunk, (k + 1) * chunk)
        rows = jnp.concatenate([block[:, at] for block in blocks], axis=0)
        packed = dot(placer_ref[...], rows).astype(bf16)
        for step, out in enumerate(outs):
            out[:, at] = packed[step * capacity : (step + 1) * capacity]


def pack(placer, blocks, capacity):
    count, width = placer.shape[0], blocks[0].shape[1]
    return pl.pallas_call(
        functools.partial(pack_kernel, len(blocks)),
        in_specs=vmem(1 + len(blocks)),
        out_specs=vmem(count // capacity),
        out_shape=[struct((capacity, width), bf16)] * (count // capacity),
        compiler_params=params(),
        name="pack",
    )(placer, *blocks)


def low_kernel(n_parts, place_ref, *refs):
    parts, factor_ref, out_ref = refs[:n_parts], refs[n_parts], refs[n_parts + 1]
    depth = factor_ref.shape[1]
    if depth < parts[0].shape[1]:
        at = pl.ds(pl.multiple_of(place_ref[0] * depth, depth), depth)
    else:
        at = slice(None)
    for step in range(n_parts):
        piece = beside(dot_last(parts[step][:, at], factor_ref[...]))
        group = lax.rem(place_ref[1] + step, n_parts)
        for i in range(out_ref.shape[0] // (2 * n_parts)):
            spot = (i * n_parts + group) * 2
            out_ref[spot] = piece
            out_ref[spot + 1] = piece


def low_pieces(parts, factor, place, group, n_dp):
    rank, depth = factor.shape
    capacity = parts[0].shape[0]
    if depth % 128:
        parts = [lax.dynamic_slice_in_dim(part, place * depth, depth, 1) for part in parts]
    return pl.pallas_call(
        functools.partial(low_kernel, len(parts)),
        in_specs=[pl.BlockSpec(memory_space=pltpu.SMEM)] + vmem(len(parts) + 1),
        out_specs=vmem(1)[0],
        out_shape=struct((n_dp * len(parts) * 2, capacity // 2, 2 * rank), f32),
        compiler_params=params(),
        name="low_pieces",
    )(jnp.stack([place, group]), *parts, factor)


def lift_kernel(n_parts, *refs):
    parts = refs[:n_parts]
    weight_ref, up_ref, route_ref, pre_ref, lifted_ref, gate_ref, weight, up, sems = refs[n_parts:]
    width = parts[0].shape[1]
    steps = sems.shape[1]
    chunk = width // steps
    copies = []
    for k in range(steps):
        at = pl.ds(k * chunk, chunk)
        copies.append(
            (
                pltpu.make_async_copy(weight_ref.at[at], weight.at[at], sems.at[0, k]),
                pltpu.make_async_copy(up_ref.at[at], up.at[at], sems.at[1, k]),
            )
        )
    ahead = 4
    for pair in copies[:ahead]:
        pair[0].start()
        pair[1].start()
    pre = lifted = logit = 0.0
    for k in range(steps):
        at = slice(k * chunk, (k + 1) * chunk)
        for i in (0, 1):
            copies[k][i].wait()
            if k + ahead < steps:
                copies[k + ahead][i].start()
        rows = jnp.concatenate([r[:, at] for r in parts], axis=0)
        pre = pre + dot(rows, weight[at])
        lifted = lifted + dot(rows, up[at])
        logit = logit + jnp.sum(rows.astype(f32) * route_ref[:, at], axis=1, keepdims=True)
    pre_ref[...] = pre
    lifted_ref[...] = lifted
    gate_ref[...] = sigmoid(logit)


def lift(parts, gate_weight, up_weight, route):
    capacity, width = parts[0].shape
    units = gate_weight.shape[1]
    count = capacity * len(parts)
    return pl.pallas_call(
        functools.partial(lift_kernel, len(parts)),
        in_specs=vmem(len(parts)) + [pl.BlockSpec(memory_space=pl.ANY)] * 2 + vmem(1),
        out_specs=vmem(3),
        scratch_shapes=[
            pltpu.VMEM(gate_weight.shape, bf16),
            pltpu.VMEM(up_weight.shape, bf16),
            pltpu.SemaphoreType.DMA((2, 12)),
        ],
        out_shape=(
            struct((count, units), f32),
            struct((count, units), f32),
            struct((count, 1), f32),
        ),
        cost_estimate=cost(4 * count * width * units, 4 * width * units),
        compiler_params=params(),
        name="lift",
    )(
        *parts,
        pltpu.with_memory_space_constraint(gate_weight, pltpu.HBM),
        pltpu.with_memory_space_constraint(up_weight, pltpu.HBM),
        route,
    )


def bring(source, target, sems, starts):
    copies = []
    for k, start in enumerate(starts):
        at = pl.ds(start, target.shape[2])
        copies.append(pltpu.make_async_copy(source.at[:, at], target.at[k], sems.at[k]))
    for copy in copies:
        copy.start()
    return copies


def down_kernel(
    place_ref, base_ref, lifted_ref, low_ref, factor_ref, weight_ref, own_ref, other_ref, pre_ref, low_out, down_ref, sems
):
    blocks, half, wide = own_ref.shape
    copies = bring(weight_ref, down_ref, sems, [k * wide for k in range(blocks)])
    groups = low_ref.shape[1]
    sums = []
    for core in (place_ref[1], 1 - place_ref[1]):
        for step in range(groups):
            group = lax.rem(place_ref[0] - step + groups, groups)
            sums.append(apart(jnp.sum(low_ref[:, group, core], axis=0)))
    low = jnp.concatenate(sums, axis=0).astype(bf16)
    pre = base_ref[...] + adapter_scale * dot(low, factor_ref[...])
    low_out[...] = low
    pre_ref[...] = pre
    hidden = (pre * sigmoid(pre) * lifted_ref[...]).astype(bf16)
    for k in range(blocks):
        if k % 2 == 0:
            copies[k].wait()
            copies[k + 1].wait()
        partial = dot(hidden, down_ref[k]).astype(bf16)
        own_ref[k] = partial[:half]
        other_ref[k] = partial[half:]


def down(base, lifted, low_parts, factor, down_weight, blocks, group, core):
    count, units = base.shape
    half, width = count // 2, down_weight.shape[1]
    shape = struct((blocks, half, width // blocks), bf16)
    return pl.pallas_call(
        down_kernel,
        in_specs=[pl.BlockSpec(memory_space=pltpu.SMEM)] + vmem(4) + [pl.BlockSpec(memory_space=pl.ANY)],
        out_specs=vmem(4),
        scratch_shapes=[
            pltpu.VMEM((blocks, units, width // blocks), bf16),
            pltpu.SemaphoreType.DMA((blocks,)),
        ],
        out_shape=(shape, shape, struct((count, units), f32), struct((count, factor.shape[0]), bf16)),
        cost_estimate=cost(2 * count * width * units, 2 * width * units),
        compiler_params=params(),
        name="down",
    )(
        jnp.stack([group, core]),
        base,
        lifted,
        low_parts,
        factor,
        pltpu.with_memory_space_constraint(down_weight, pltpu.HBM),
    )


def fold_core_kernel(place_ref, own_ref, got_ref, keep_ref, far_ref, near_ref):
    line, bit = place_ref[0] // 2, lax.rem(place_ref[0], 2)

    def folded(at):
        return (own_ref[at].astype(f32) + got_ref[at].astype(f32)).astype(bf16)

    for k in range(4):
        at = 2 * lax.bitwise_xor(line, k)
        keep_ref[k] = folded(at + bit)
        out_ref = near_ref if k < 2 else far_ref
        out_ref[k % 2] = folded(at + 1 - bit)


def fold_core(own, got, place):
    shapes = [struct((count, *own.shape[1:]), bf16) for count in (4, 2, 2)]
    return pl.pallas_call(
        fold_core_kernel,
        in_specs=[pl.BlockSpec(memory_space=pltpu.SMEM)] + vmem(2),
        out_specs=vmem(3),
        out_shape=shapes,
        compiler_params=params(),
        name="fold_core",
    )(place.reshape(1), own, got)


def fold_near_kernel(first, keep_ref, got_ref, *out_refs):
    for k, out_ref in enumerate(out_refs):
        out_ref[...] = (keep_ref[first + k].astype(f32) + got_ref[k].astype(f32)).astype(bf16)


def fold_near(keep, got, first):
    return pl.pallas_call(
        functools.partial(fold_near_kernel, first),
        in_specs=vmem(2),
        out_specs=vmem(2),
        out_shape=[struct(keep.shape[1:], bf16)] * 2,
        compiler_params=params(),
        name="fold_near",
    )(keep, got)


def mix_kernel(n_terms, *refs):
    gate_ref, out_ref = refs[n_terms:]
    total = refs[0][...].astype(f32)
    for term in refs[1:n_terms]:
        total = total + term[...].astype(f32)
    out_ref[...] = (gate_ref[: out_ref.shape[0]] * total).astype(bf16)


def mix(terms, gate):
    return pl.pallas_call(
        functools.partial(mix_kernel, len(terms)),
        in_specs=vmem(len(terms) + 1),
        out_specs=vmem(1)[0],
        out_shape=struct(terms[0].shape, bf16),
        compiler_params=params(),
        name="mix",
    )(*terms, gate)


def back_sum(parts, owns, others, starts, gate_ref, weight_ref, down_ref, back_ref, sems, loss_factor):
    wide = owns[0].shape[1]
    copies = bring(weight_ref, down_ref, sems, starts)
    scale = loss_factor * gate_ref[...]
    for k, (own, other) in enumerate(zip(owns, others)):
        at = pl.ds(starts[k], wide)
        mixed = jnp.concatenate([own[...], other[...]], axis=0).astype(f32)
        rows = jnp.concatenate([r[:, at] for r in parts], axis=0).astype(f32)
        back_ref[k] = (scale * (mixed - rows)).astype(bf16)
    for copy in copies:
        copy.wait()
    total = dot_last(down_ref[0], back_ref[0])
    for k in range(1, len(copies)):
        total = total + dot_last(down_ref[k], back_ref[k])
    return total


def back_first_kernel(n_parts, n_blocks, loss_factor, order_ref, *refs):
    parts, refs = refs[:n_parts], refs[n_parts:]
    owns, others, refs = refs[:n_blocks], refs[n_blocks : 2 * n_blocks], refs[2 * n_blocks :]
    gate_ref, weight_ref, out_ref, *scratch = refs
    wide = owns[0].shape[1]
    starts = [pl.multiple_of(order_ref[k] * wide, wide) for k in range(n_blocks)]
    out_ref[...] = back_sum(parts, owns, others, starts, gate_ref, weight_ref, *scratch, loss_factor)


def back_last_kernel(n_parts, n_blocks, loss_factor, order_ref, *refs):
    parts, refs = refs[:n_parts], refs[n_parts:]
    owns, refs = refs[: 2 * n_blocks], refs[2 * n_blocks :]
    others, refs = refs[:n_blocks], refs[n_blocks:]
    gate_ref, weight_ref, first_ref, pre_ref, lifted_ref, low_ref, factor_ref = refs[:7]
    low_out, grad_ref, *homes = refs[7:-3]
    half, wide = owns[0].shape
    capacity = half // len(homes)
    starts = [pl.multiple_of(order_ref[k] * wide, wide) for k in range(2 * n_blocks)]
    pre = pre_ref[...]
    sig = sigmoid(pre)
    slope = lifted_ref[...] * (sig * (1.0 + pre * (1.0 - sig)))
    total = back_sum(
        parts, owns[n_blocks:], others, starts[n_blocks:], gate_ref, weight_ref, *refs[-3:], loss_factor
    )
    back_pre = ((first_ref[...] + total).T * slope).astype(bf16)
    back_low = beside(adapter_scale * dot_last(back_pre, factor_ref[...])).astype(bf16)
    for i in range(low_out.shape[0]):
        low_out[i] = back_low
    grad_ref[...] = adapter_scale * dot_first(low_ref[...], back_pre)
    for k, own in enumerate(owns):
        for step, home in enumerate(homes):
            home[:, pl.ds(starts[k], wide)] = own[step * capacity : (step + 1) * capacity]


def back_scratch(blocks, units, count, wide):
    return [
        pltpu.VMEM((blocks, units, wide), bf16),
        pltpu.VMEM((blocks, count, wide), bf16),
        pltpu.SemaphoreType.DMA((blocks,)),
    ]


def back_first(parts, owns, others, order, gate, down_weight, loss_factor):
    units = down_weight.shape[0]
    count, blocks, wide = gate.shape[0], len(owns), owns[0].shape[1]
    return pl.pallas_call(
        functools.partial(back_first_kernel, len(parts), blocks, loss_factor),
        in_specs=[pl.BlockSpec(memory_space=pltpu.SMEM)]
        + vmem(len(parts) + 2 * blocks + 1)
        + [pl.BlockSpec(memory_space=pl.ANY)],
        out_specs=vmem(1)[0],
        out_shape=struct((units, count), f32),
        scratch_shapes=back_scratch(blocks, units, count, wide),
        cost_estimate=cost(2 * count * blocks * wide * units, 2 * blocks * wide * units),
        compiler_params=params(),
        name="back_first",
    )(order, *parts, *owns, *others, gate, pltpu.with_memory_space_constraint(down_weight, pltpu.HBM))


def back_last(parts, owns, others, order, gate, down_weight, first, pre, lifted, low, factor, loss_factor, copies):
    capacity, width = parts[0].shape
    half, wide = owns[0].shape
    count, units = pre.shape
    rank, blocks = factor.shape[0], len(others)
    homes = half // capacity
    return pl.pallas_call(
        functools.partial(back_last_kernel, len(parts), blocks, loss_factor),
        in_specs=[pl.BlockSpec(memory_space=pltpu.SMEM)]
        + vmem(len(parts) + 3 * blocks + 1)
        + [pl.BlockSpec(memory_space=pl.ANY)]
        + vmem(5),
        out_specs=vmem(2 + homes),
        out_shape=(
            struct((copies, half, 2 * rank), bf16),
            struct((rank, units), f32),
            *[struct((capacity, width), bf16)] * homes,
        ),
        scratch_shapes=back_scratch(blocks, units, count, wide),
        cost_estimate=cost(2 * count * blocks * wide * units, 2 * blocks * wide * units),
        compiler_params=params(),
        name="back_last",
    )(
        order,
        *parts,
        *owns,
        *others,
        gate,
        pltpu.with_memory_space_constraint(down_weight, pltpu.HBM),
        first,
        pre,
        lifted,
        low,
        factor,
    )


def factor_kernel(place_ref, low_ref, piece_ref, out_ref):
    rank = out_ref.shape[0]
    groups = piece_ref.shape[0]
    group, core = place_ref[0], place_ref[1]
    total = 0.0
    for g in range(groups):
        mine = jnp.sum(low_ref[:, g, core].astype(f32), axis=0)
        theirs = jnp.sum(low_ref[:, g, 1 - core].astype(f32), axis=0)
        low = jnp.concatenate(
            [mine[:, :rank] + theirs[:, rank:], mine[:, rank:] + theirs[:, :rank]], axis=0
        )
        high = low.astype(bf16)
        rest = (low - high.astype(f32)).astype(bf16)
        piece = piece_ref[lax.rem(group - g + groups, groups)]
        total = total + dot_first(high, piece) + dot_first(rest, piece)
    out_ref[...] = total


def factor_gradient(lows, pieces, group, core):
    rank, share = lows.shape[-1] // 2, pieces.shape[2]
    return pl.pallas_call(
        factor_kernel,
        in_specs=[pl.BlockSpec(memory_space=pltpu.SMEM)] + vmem(2),
        out_specs=vmem(1)[0],
        out_shape=struct((rank, share), f32),
        compiler_params=params(),
        name="factor_gradient",
    )(jnp.stack([group, core]), lows, pieces)


def shards(
    tokens,
    expert_choice_table,
    gate_weight,
    up_weight,
    down_weight,
    adapter_down_shared,
    adapter_gate_factor,
    router,
):
    tok_rows, width = tokens.shape
    n_dp = lax.axis_size("dp")
    groups = lax.axis_size("x")
    place = lax.axis_index("dp")
    group = lax.axis_index("x")
    core = lax.axis_index("core")
    col_rows = n_dp * tok_rows
    capacity = col_rows // groups
    half = groups * capacity
    wide = width // n_dp
    rank = adapter_down_shared.shape[1]
    devices = n_dp * groups * 2
    share = width // devices
    loss_factor = math.sqrt(groups / (tok_rows * devices))
    blocks = 8
    eight = n_dp == blocks

    labels = expert_choice_table[0]
    index = jnp.arange(col_rows, dtype=jnp.int32)
    before = (labels[None, :] == labels[:, None]) & (index[None, :] < index[:, None])
    ordinal = jnp.sum(before.astype(jnp.int32), axis=1)
    ahead = lax.rem(labels - group + groups, groups)
    target = ahead * capacity + ordinal
    if eight:
        order = lax.bitwise_xor(jnp.array(NEAR, jnp.int32), place)
        column = gather_eight(tokens)
        spread_out = target.reshape(n_dp, tok_rows)
        arrived = jnp.sum(
            jnp.where(order[:, None, None] == jnp.arange(n_dp)[None, :, None], spread_out[None], 0), axis=1
        ).reshape(col_rows)
    else:
        order = jnp.arange(blocks, dtype=jnp.int32)
        column = exchange(jnp.broadcast_to(tokens[None], (n_dp, tok_rows, width)), "dp")
        column = [column.reshape(col_rows, width)]
        arrived = target
    placer = (index[:, None] == arrived[None, :]).astype(bf16)
    own_route = lax.dynamic_slice_in_dim(router.T, group, 1, 0).astype(f32)
    column, placer, own_route = lax.optimization_barrier((column, placer, own_route))
    packed = pack(placer, column, capacity)
    parts = [packed[0]]
    for step in range(1, groups):
        route = [(i, (i + step) % groups) for i in range(groups)]
        parts.append(lax.ppermute(packed[step], "x", route))
    parts = parts + [swap(part, "core") for part in parts]

    low_parts = low_pieces(packed, adapter_down_shared.T, place, group, n_dp)
    low_parts = exchange(low_parts, every).reshape(n_dp, groups, 2, capacity // 2, 2 * rank)
    base, lifted, gate = lift(parts, gate_weight, up_weight, own_route)
    low_parts, gate = lax.optimization_barrier((low_parts, gate))
    own, other, pre, low = down(
        base, lifted, low_parts, adapter_gate_factor, down_weight, blocks, group, core
    )

    rows = jnp.concatenate(parts, axis=0)
    pieces = []
    for step in range(groups):
        to = lax.rem(group + step, groups)
        at = ((place * groups + to) * 2 + core) * share
        piece = lax.dynamic_slice_in_dim(rows, at, share, 1)
        route = [(i, (i + step) % groups) for i in range(groups)]
        pieces.append(lax.ppermute(piece, "x", route) if step else piece)
    pieces = jnp.stack(pieces)

    got = swap(other, "core")
    if eight:
        keep, far, near = fold_core(own, got, place)
        far, near = across(far, "dp", 1), across(near, "dp", 1)
        two, three = fold_near(keep, far, 2)
        mine, one = fold_near(keep, near, 0)
        terms = [mine, across(one, "dp", 2), across(two, "dp", 4), across(three, "dp", 6)]
        terms, pieces = lax.optimization_barrier((terms, pieces))
        owns = gather_eight(mix(terms, gate))
    else:
        summed = (own.astype(f32) + got.astype(f32)).astype(bf16)
        summed = summed.transpose(1, 0, 2).reshape(half, n_dp, wide).transpose(1, 0, 2)
        summed = exchange(summed, "dp")
        mixed = mix([summed[i] for i in range(n_dp)], gate)
        mixed = exchange(jnp.broadcast_to(mixed[None], (n_dp, half, wide)), "dp")
        mixed = mixed.transpose(1, 0, 2).reshape(half, width)
        owns = [mixed[:, i * (width // blocks) : (i + 1) * (width // blocks)] for i in range(blocks)]
    others = [swap(block, "core") for block in owns]

    first = back_first(
        parts, owns[: blocks // 2], others[: blocks // 2], order, gate, down_weight, loss_factor
    )
    back_low, grad_b, *homes = back_last(
        parts,
        owns,
        others[blocks // 2 :],
        order,
        gate,
        down_weight,
        first,
        pre,
        lifted,
        low,
        adapter_gate_factor,
        loss_factor,
        devices,
    )
    lows = exchange(back_low, every).reshape(n_dp, groups, 2, half, 2 * rank)

    own_target = lax.dynamic_slice_in_dim(target, place * tok_rows, tok_rows, 0)
    result = jnp.zeros((tok_rows, width), f32)
    for step in range(groups):
        route = [(i, (i - step) % groups) for i in range(groups)]
        returned = lax.ppermute(homes[step], "x", route) if step else homes[0]
        spot = index[step * capacity : (step + 1) * capacity]
        chooser = (own_target[:, None] == spot[None, :]).astype(bf16)
        result = result + dot(chooser, returned)

    grad_a = factor_gradient(lows, pieces, group, core)
    return (result.astype(bf16), grad_a.T, grad_b.T)


def solution(mesh):
    n_dp, n_expert = mesh.shape["dp"], mesh.shape["expert"]
    split = Mesh(mesh.devices.reshape(n_dp, n_expert // 2, 2), every)
    return jax.shard_map(
        shards,
        mesh=split,
        in_specs=(
            P(every, None),
            P(("x", "core"), None),
            P(None, every),
            P(None, every),
            P(every, None),
            P("dp", None),
            P(None, every),
            P(),
        ),
        out_specs=(P(every, None), P(every, None), P(every, None)),
        check_vma=False,
    )
```

```python
import functools
import math

import jax
import jax.numpy as jnp
from jax import lax
from jax.experimental import pallas as pl
from jax.experimental.pallas import tpu as pltpu
from jax.sharding import Mesh, PartitionSpec as P

adapter_scale = 0.25
bf16, f32 = jnp.bfloat16, jnp.float32
VMEM_LIMIT = 20 * 2**20
every = ("dp", "x", "core")
NEAR = (0, 2, 4, 6, 1, 3, 5, 7)


def swap(block, axis):
    return lax.ppermute(block, axis, [(0, 1), (1, 0)])


def across(block, axis, apart_by):
    count = lax.axis_size(axis)
    return lax.ppermute(block, axis, [(i, i ^ apart_by) for i in range(count)])


def gather_eight(block, *meanwhile):
    near = across(block, "dp", 1)
    far = [across(block, "dp", bits) for bits in NEAR[1:4]]
    far, meanwhile = lax.optimization_barrier((far, meanwhile))
    return [block, *far, near, *[across(other, "dp", 1) for other in far]], *meanwhile


def order_of(place, blocks, eight):
    return [lax.bitwise_xor(place, NEAR[k]) if eight else k for k in range(blocks)]


def exchange(blocks, axis):
    return lax.all_to_all(blocks, axis, 0, 0, tiled=True)


def dot(left, right):
    return jnp.dot(left, right, preferred_element_type=f32)


def dot_last(left, right):
    return lax.dot_general(left, right, (((1,), (1,)), ((), ())), preferred_element_type=f32)


def dot_first(left, right):
    return lax.dot_general(left, right, (((0,), (0,)), ((), ())), preferred_element_type=f32)


def sigmoid(v):
    return 1.0 / (1.0 + jnp.exp(-v))


def struct(shape, dtype):
    return jax.ShapeDtypeStruct(shape, dtype)


def vmem(count):
    return [pl.BlockSpec(memory_space=pltpu.VMEM)] * count


def params():
    return pltpu.CompilerParams(vmem_limit_bytes=VMEM_LIMIT)


def cost(flops, moved):
    return pl.CostEstimate(flops=int(flops), bytes_accessed=int(moved), transcendentals=0)


def beside(rows):
    half = rows.shape[0] // 2
    return jnp.concatenate([rows[:half], rows[half:]], axis=1)


def apart(wide):
    rank = wide.shape[1] // 2
    return jnp.concatenate([wide[:, :rank], wide[:, rank:]], axis=0)


def near_kernel(here_ref, tokens_ref, factor_ref, router_ref, tokens_out, factor_out, route_out, router_near, sems):
    pairs = ((tokens_ref, tokens_out), (factor_ref, factor_out), (router_ref, router_near))
    copies = [pltpu.make_async_copy(*pair, sems.at[i]) for i, pair in enumerate(pairs)]
    for copy in copies:
        copy.start()
    for copy in copies:
        copy.wait()
    picked = lax.broadcasted_iota(jnp.int32, (router_near.shape[0], 1), 0) == here_ref[1]
    route_out[...] = jnp.sum(jnp.where(picked, router_near[...].astype(f32), 0.0), axis=0, keepdims=True)


def brought_near(tokens, factor, router, here):
    return pl.pallas_call(
        near_kernel,
        in_specs=[pl.BlockSpec(memory_space=pltpu.SMEM)] + [pl.BlockSpec(memory_space=pl.ANY)] * 3,
        out_specs=vmem(3),
        out_shape=[
            struct(tokens.shape, bf16),
            struct(factor.shape, bf16),
            struct((1, router.shape[1]), f32),
        ],
        scratch_shapes=[pltpu.VMEM(router.shape, bf16), pltpu.SemaphoreType.DMA((3,))],
        compiler_params=params(),
        name="near",
    )(here, *[pltpu.with_memory_space_constraint(array, pltpu.HBM) for array in (tokens, factor, router)])


def pack_kernel(n_blocks, placer_ref, *refs):
    blocks = refs[:n_blocks]
    outs = refs[n_blocks:]
    capacity, width = outs[0].shape
    chunk = width // 6
    for k in range(6):
        at = slice(k * chunk, (k + 1) * chunk)
        rows = jnp.concatenate([block[:, at] for block in blocks], axis=0)
        packed = dot(placer_ref[...], rows).astype(bf16)
        for step, out in enumerate(outs):
            out[:, at] = packed[step * capacity : (step + 1) * capacity]


def pack(placer, blocks, capacity):
    count, width = placer.shape[0], blocks[0].shape[1]
    return pl.pallas_call(
        functools.partial(pack_kernel, len(blocks)),
        in_specs=vmem(1 + len(blocks)),
        out_specs=vmem(count // capacity),
        out_shape=[struct((capacity, width), bf16)] * (count // capacity),
        compiler_params=params(),
        name="pack",
    )(placer, *blocks)


def low_kernel(n_parts, place_ref, *refs):
    parts, factor_ref, out_ref = refs[:n_parts], refs[n_parts], refs[n_parts + 1]
    depth = factor_ref.shape[1]
    if depth < parts[0].shape[1]:
        at = pl.ds(pl.multiple_of(place_ref[0] * depth, depth), depth)
    else:
        at = slice(None)
    capacity = parts[0].shape[0]
    rows = dot_last(jnp.concatenate([r[:, at] for r in parts], axis=0), factor_ref[...])
    for step in range(n_parts):
        piece = beside(rows[step * capacity : (step + 1) * capacity])
        group = lax.rem(place_ref[1] + step, n_parts)
        for i in range(out_ref.shape[0] // (2 * n_parts)):
            spot = (i * n_parts + group) * 2
            out_ref[spot] = piece
            out_ref[spot + 1] = piece


def low_pieces(parts, factor, here, place, n_dp):
    rank, depth = factor.shape
    capacity = parts[0].shape[0]
    if depth % 128:
        parts = [lax.dynamic_slice_in_dim(part, place * depth, depth, 1) for part in parts]
    return pl.pallas_call(
        functools.partial(low_kernel, len(parts)),
        in_specs=[pl.BlockSpec(memory_space=pltpu.SMEM)] + vmem(len(parts) + 1),
        out_specs=vmem(1)[0],
        out_shape=struct((n_dp * len(parts) * 2, capacity // 2, 2 * rank), f32),
        compiler_params=params(),
        name="low_pieces",
    )(here, *parts, factor)


def lift_kernel(n_parts, *refs):
    parts = refs[:n_parts]
    weight_ref, up_ref, route_ref, pre_ref, lifted_ref, gate_ref, weight, up, sems = refs[n_parts:]
    width = parts[0].shape[1]
    steps = sems.shape[1]
    chunk = width // steps
    copies = []
    for k in range(steps):
        at = pl.ds(k * chunk, chunk)
        copies.append(
            (
                pltpu.make_async_copy(weight_ref.at[at], weight.at[at], sems.at[0, k]),
                pltpu.make_async_copy(up_ref.at[at], up.at[at], sems.at[1, k]),
            )
        )
    ahead = 4
    for pair in copies[:ahead]:
        pair[0].start()
        pair[1].start()
    pre = lifted = logit = 0.0
    for k in range(steps):
        at = slice(k * chunk, (k + 1) * chunk)
        for i in (0, 1):
            copies[k][i].wait()
            if k + ahead < steps:
                copies[k + ahead][i].start()
        rows = jnp.concatenate([r[:, at] for r in parts], axis=0)
        pre = pre + dot(rows, weight[at])
        lifted = lifted + dot(rows, up[at])
        logit = logit + jnp.sum(rows.astype(f32) * route_ref[:, at], axis=1, keepdims=True)
    pre_ref[...] = pre
    lifted_ref[...] = lifted
    gate_ref[...] = sigmoid(logit)


def lift(parts, gate_weight, up_weight, route):
    capacity, width = parts[0].shape
    units = gate_weight.shape[1]
    count = capacity * len(parts)
    return pl.pallas_call(
        functools.partial(lift_kernel, len(parts)),
        in_specs=vmem(len(parts))
        + [pl.BlockSpec(memory_space=pl.ANY)] * 2
        + vmem(1),
        out_specs=vmem(3),
        scratch_shapes=[
            pltpu.VMEM(gate_weight.shape, bf16),
            pltpu.VMEM(up_weight.shape, bf16),
            pltpu.SemaphoreType.DMA((2, 12)),
        ],
        out_shape=(
            struct((count, units), f32),
            struct((count, units), f32),
            struct((count, 1), f32),
        ),
        cost_estimate=cost(4 * count * width * units, 4 * width * units),
        compiler_params=params(),
        name="lift",
    )(
        *parts,
        pltpu.with_memory_space_constraint(gate_weight, pltpu.HBM),
        pltpu.with_memory_space_constraint(up_weight, pltpu.HBM),
        route,
    )


def bring(source, target, sems, starts):
    copies = []
    for k, start in enumerate(starts):
        at = pl.ds(start, target.shape[2])
        copies.append(pltpu.make_async_copy(source.at[:, at], target.at[k], sems.at[k]))
    for copy in copies:
        copy.start()
    return copies


def down_kernel(
    place_ref, base_ref, lifted_ref, low_ref, factor_ref, weight_ref, own_ref, other_ref, pre_ref, low_out, down_ref, sems
):
    blocks, half, wide = own_ref.shape
    copies = bring(weight_ref, down_ref, sems, [k * wide for k in range(blocks)])
    groups = low_ref.shape[1]
    sums = []
    for core in (place_ref[2], 1 - place_ref[2]):
        for step in range(groups):
            group = lax.rem(place_ref[1] - step + groups, groups)
            sums.append(apart(jnp.sum(low_ref[:, group, core], axis=0)))
    low = jnp.concatenate(sums, axis=0).astype(bf16)
    pre = base_ref[...] + adapter_scale * dot(low, factor_ref[...])
    low_out[...] = low
    pre_ref[...] = pre
    hidden = (pre * sigmoid(pre) * lifted_ref[...]).astype(bf16)
    for k in range(blocks):
        if k % 2 == 0:
            copies[k].wait()
            copies[k + 1].wait()
        partial = dot(hidden, down_ref[k]).astype(bf16)
        own_ref[k] = partial[:half]
        other_ref[k] = partial[half:]


def down(base, lifted, low_parts, factor, down_weight, blocks, here):
    count, units = base.shape
    half, width = count // 2, down_weight.shape[1]
    shape = struct((blocks, half, width // blocks), bf16)
    *outs, kept = pl.pallas_call(
        down_kernel,
        in_specs=[pl.BlockSpec(memory_space=pltpu.SMEM)] + vmem(4) + [pl.BlockSpec(memory_space=pl.ANY)],
        out_specs=vmem(5),
        scratch_shapes=[pltpu.SemaphoreType.DMA((blocks,))],
        out_shape=(
            shape,
            shape,
            struct((count, units), f32),
            struct((count, factor.shape[0]), bf16),
            pltpu.VMEM((blocks, units, width // blocks), bf16),
        ),
        cost_estimate=cost(2 * count * width * units, 2 * width * units),
        compiler_params=params(),
        name="down",
    )(
        here,
        base,
        lifted,
        low_parts,
        factor,
        pltpu.with_memory_space_constraint(down_weight, pltpu.HBM),
    )
    return *outs, pltpu.with_memory_space_constraint(kept, pltpu.VMEM)


def fold_core_kernel(place_ref, own_ref, got_ref, keep_ref, far_ref, near_ref):
    line, bit = place_ref[0] // 2, lax.rem(place_ref[0], 2)

    def folded(at):
        return (own_ref[at].astype(f32) + got_ref[at].astype(f32)).astype(bf16)

    for k in range(4):
        at = 2 * lax.bitwise_xor(line, k)
        keep_ref[k] = folded(at + bit)
        out_ref = near_ref if k < 2 else far_ref
        out_ref[k % 2] = folded(at + 1 - bit)


def fold_core(own, got, here):
    shapes = [struct((count, *own.shape[1:]), bf16) for count in (4, 2, 2)]
    return pl.pallas_call(
        fold_core_kernel,
        in_specs=[pl.BlockSpec(memory_space=pltpu.SMEM)] + vmem(2),
        out_specs=vmem(3),
        out_shape=shapes,
        compiler_params=params(),
        name="fold_core",
    )(here, own, got)


def fold_near_kernel(first, keep_ref, got_ref, *out_refs):
    for k, out_ref in enumerate(out_refs):
        out_ref[...] = (keep_ref[first + k].astype(f32) + got_ref[k].astype(f32)).astype(bf16)


def fold_near(keep, got, first):
    return pl.pallas_call(
        functools.partial(fold_near_kernel, first),
        in_specs=vmem(2),
        out_specs=vmem(2),
        out_shape=[struct(keep.shape[1:], bf16)] * 2,
        compiler_params=params(),
        name="fold_near",
    )(keep, got)


def mix_kernel(n_terms, *refs):
    gate_ref, out_ref = refs[n_terms:]
    total = refs[0][...].astype(f32)
    for term in refs[1:n_terms]:
        total = total + term[...].astype(f32)
    out_ref[...] = (gate_ref[: out_ref.shape[0]] * total).astype(bf16)


def mix(terms, gate):
    return pl.pallas_call(
        functools.partial(mix_kernel, len(terms)),
        in_specs=vmem(len(terms) + 1),
        out_specs=vmem(1)[0],
        out_shape=struct(terms[0].shape, bf16),
        compiler_params=params(),
        name="mix",
    )(*terms, gate)


def back_sum(parts, owns, others, order, gate_ref, down_ref, loss_factor):
    wide = owns[0].shape[1]
    scale = loss_factor * gate_ref[...]
    total = 0.0
    for block, own, other in zip(order, owns, others):
        start = block * wide
        at = pl.ds(start if isinstance(start, int) else pl.multiple_of(start, wide), wide)
        mixed = jnp.concatenate([own[...], other[...]], axis=0).astype(f32)
        rows = jnp.concatenate([r[:, at] for r in parts], axis=0).astype(f32)
        back = (scale * (mixed - rows)).astype(bf16)
        total = total + dot_last(down_ref[block], back)
    return total


def back_first_kernel(n_parts, n_blocks, eight, loss_factor, here_ref, *refs):
    parts, refs = refs[:n_parts], refs[n_parts:]
    owns, others, refs = refs[:n_blocks], refs[n_blocks : 2 * n_blocks], refs[2 * n_blocks :]
    gate_ref, down_ref, out_ref = refs
    order = order_of(here_ref[0], n_blocks, eight)
    out_ref[...] = back_sum(parts, owns, others, order, gate_ref, down_ref, loss_factor)


def back_last_kernel(n_parts, n_blocks, eight, loss_factor, here_ref, *refs):
    parts, refs = refs[:n_parts], refs[n_parts:]
    owns, refs = refs[: 2 * n_blocks], refs[2 * n_blocks :]
    others, refs = refs[:n_blocks], refs[n_blocks:]
    gate_ref, down_ref, first_ref, pre_ref, lifted_ref, low_ref, factor_ref = refs[:7]
    low_out, grad_ref, *homes = refs[7:]
    half, wide = owns[0].shape
    capacity = half // len(homes)
    order = order_of(here_ref[0], 2 * n_blocks, eight)
    pre = pre_ref[...]
    sig = sigmoid(pre)
    slope = lifted_ref[...] * (sig * (1.0 + pre * (1.0 - sig)))
    total = first_ref[...] + back_sum(
        parts, owns[n_blocks:], others, order[n_blocks:], gate_ref, down_ref, loss_factor
    )
    back_pre = (total.T * slope).astype(bf16)
    back_low = beside(adapter_scale * dot_last(back_pre, factor_ref[...])).astype(bf16)
    for i in range(low_out.shape[0]):
        low_out[i] = back_low
    grad_ref[...] = adapter_scale * dot_first(low_ref[...], back_pre)
    for block, own in zip(order, owns):
        start = block * wide
        at = pl.ds(start if isinstance(start, int) else pl.multiple_of(start, wide), wide)
        for step, home in enumerate(homes):
            home[:, at] = own[step * capacity : (step + 1) * capacity]


def back_first(parts, owns, others, here, eight, gate, kept, loss_factor):
    units = kept.shape[1]
    count, blocks, wide = gate.shape[0], len(owns), owns[0].shape[1]
    return pl.pallas_call(
        functools.partial(back_first_kernel, len(parts), blocks, eight, loss_factor),
        in_specs=[pl.BlockSpec(memory_space=pltpu.SMEM)] + vmem(len(parts) + 2 * blocks + 2),
        out_specs=vmem(1)[0],
        out_shape=struct((units, count), f32),
        cost_estimate=cost(2 * count * blocks * wide * units, 2 * blocks * wide * units),
        compiler_params=params(),
        name="back_first",
    )(here, *parts, *owns, *others, gate, kept)


def back_last(parts, owns, others, here, eight, gate, kept, first, pre, lifted, low, factor, loss_factor, copies):
    capacity, width = parts[0].shape
    half, wide = owns[0].shape
    count, units = pre.shape
    rank, blocks = factor.shape[0], len(others)
    homes = half // capacity
    return pl.pallas_call(
        functools.partial(back_last_kernel, len(parts), blocks, eight, loss_factor),
        in_specs=[pl.BlockSpec(memory_space=pltpu.SMEM)] + vmem(len(parts) + 3 * blocks + 7),
        out_specs=vmem(2 + homes),
        out_shape=(
            struct((copies, half, 2 * rank), bf16),
            struct((rank, units), f32),
            *[struct((capacity, width), bf16)] * homes,
        ),
        cost_estimate=cost(2 * count * blocks * wide * units, 2 * blocks * wide * units),
        compiler_params=params(),
        name="back_last",
    )(here, *parts, *owns, *others, gate, kept, first, pre, lifted, low, factor)


def factor_kernel(place_ref, low_ref, piece_ref, out_ref):
    rank, share = out_ref.shape
    groups = piece_ref.shape[0]
    group, core = place_ref[1], place_ref[2]
    lows, rows = [], []
    for step in range(groups):
        source = lax.rem(group - step + groups, groups)
        mine = jnp.sum(low_ref[:, source, core].astype(f32), axis=0)
        theirs = jnp.sum(low_ref[:, source, 1 - core].astype(f32), axis=0)
        lows += [mine[:, :rank] + theirs[:, rank:], mine[:, rank:] + theirs[:, :rank]]
        rows.append(piece_ref[step, :, :share])
    low = jnp.concatenate(lows, axis=0)
    high = low.astype(bf16)
    rest = (low - high.astype(f32)).astype(bf16)
    out_ref[...] = dot_first(jnp.concatenate([high, rest], axis=0), jnp.concatenate(rows + rows, axis=0))


def factor_gradient(lows, pieces, share, here):
    rank = lows.shape[-1] // 2
    return pl.pallas_call(
        factor_kernel,
        in_specs=[pl.BlockSpec(memory_space=pltpu.SMEM)] + vmem(2),
        out_specs=vmem(1)[0],
        out_shape=struct((rank, share), f32),
        compiler_params=params(),
        name="factor_gradient",
    )(here, lows, pieces)


def shards(
    tokens,
    expert_choice_table,
    gate_weight,
    up_weight,
    down_weight,
    adapter_down_shared,
    adapter_gate_factor,
    router,
):
    tok_rows, width = tokens.shape
    n_dp = lax.axis_size("dp")
    groups = lax.axis_size("x")
    place = lax.axis_index("dp")
    group = lax.axis_index("x")
    core = lax.axis_index("core")
    col_rows = n_dp * tok_rows
    capacity = col_rows // groups
    half = groups * capacity
    wide = width // n_dp
    rank = adapter_down_shared.shape[1]
    devices = n_dp * groups * 2
    share = width // devices
    loss_factor = math.sqrt(groups / (tok_rows * devices))
    blocks = 8
    eight = n_dp == blocks

    here = jnp.stack([place, group, core])

    labels = expert_choice_table[0]
    index = jnp.arange(col_rows, dtype=jnp.int32)
    number = index
    if eight:
        order = lax.bitwise_xor(jnp.array(NEAR, jnp.int32), place)
        number = (order[:, None] * tok_rows + jnp.arange(tok_rows)[None, :]).reshape(col_rows)
        labels = jnp.sum(jnp.where(number[:, None] == index[None, :], labels[None, :], 0), axis=1)
    before = (labels[None, :] == labels[:, None]) & (number[None, :] < number[:, None])
    ordinal = jnp.sum(before.astype(jnp.int32), axis=1)
    ahead = lax.rem(labels - group + groups, groups)
    target = ahead * capacity + ordinal
    placer = (index[:, None] == target[None, :]).astype(bf16)
    tokens_near, factor, own_route = brought_near(tokens, adapter_down_shared.T, router.T, here)
    if eight:
        column, placer, tokens_near, factor, own_route = gather_eight(
            tokens, placer, tokens_near, factor, own_route
        )
        column[0] = tokens_near
        column, placer, factor = lax.optimization_barrier((column, placer, factor))
        own_target = target[:tok_rows]
    else:
        column = exchange(jnp.broadcast_to(tokens[None], (n_dp, tok_rows, width)), "dp")
        column = [column.reshape(col_rows, width)]
        own_target = lax.dynamic_slice_in_dim(target, place * tok_rows, tok_rows, 0)
    packed = pack(placer, column, capacity)
    parts = [packed[0]]
    for step in range(1, groups):
        route = [(i, (i + step) % groups) for i in range(groups)]
        parts.append(lax.ppermute(packed[step], "x", route))
    parts = parts + [swap(part, "core") for part in parts]

    low_parts = low_pieces(packed, factor, here, place, n_dp)
    low_parts = exchange(low_parts, every).reshape(n_dp, groups, 2, capacity // 2, 2 * rank)
    base, lifted, gate = lift(parts, gate_weight, up_weight, own_route)
    low_parts, gate = lax.optimization_barrier((low_parts, gate))
    own, other, pre, low, kept = down(
        base, lifted, low_parts, adapter_gate_factor, down_weight, blocks, here
    )

    rows = jnp.concatenate(parts, axis=0)
    numbers = jnp.broadcast_to(own_target.astype(bf16)[None], (2 * half, tok_rows))
    pieces = []
    for step in range(groups):
        to = lax.rem(group + step, groups)
        at = ((place * groups + to) * 2 + core) * share
        piece = jnp.concatenate([lax.dynamic_slice_in_dim(rows, at, share, 1), numbers], axis=1)
        route = [(i, (i + step) % groups) for i in range(groups)]
        pieces.append(lax.ppermute(piece, "x", route) if step else piece)
    pieces = jnp.stack(pieces)

    got = swap(other, "core")
    if eight:
        keep, far, near = fold_core(own, got, here)
        far, near = across(far, "dp", 1), across(near, "dp", 1)
        two, three = fold_near(keep, far, 2)
        mine, one = fold_near(keep, near, 0)
        terms = [mine, across(one, "dp", 2), across(two, "dp", 4), across(three, "dp", 6)]
        terms, pieces = lax.optimization_barrier((terms, pieces))
        (owns,) = gather_eight(mix(terms, gate))
    else:
        summed = (own.astype(f32) + got.astype(f32)).astype(bf16)
        summed = summed.transpose(1, 0, 2).reshape(half, n_dp, wide).transpose(1, 0, 2)
        summed = exchange(summed, "dp")
        mixed = mix([summed[i] for i in range(n_dp)], gate)
        mixed = exchange(jnp.broadcast_to(mixed[None], (n_dp, half, wide)), "dp")
        mixed = mixed.transpose(1, 0, 2).reshape(half, width)
        owns = [mixed[:, i * (width // blocks) : (i + 1) * (width // blocks)] for i in range(blocks)]
    others = [swap(block, "core") for block in owns]

    first = back_first(
        parts, owns[: blocks // 2], others[: blocks // 2], here, eight, gate, kept, loss_factor
    )
    back_low, grad_b, *homes = back_last(
        parts,
        owns,
        others[blocks // 2 :],
        here,
        eight,
        gate,
        kept,
        first,
        pre,
        lifted,
        low,
        adapter_gate_factor,
        loss_factor,
        devices,
    )
    lows = exchange(back_low, every).reshape(n_dp, groups, 2, half, 2 * rank)

    result = jnp.zeros((tok_rows, width), f32)
    for step in range(groups):
        spot = index[step * capacity : (step + 1) * capacity]
        wanted = pieces[step, 0, share:].astype(jnp.int32)
        chooser = (wanted[:, None] == spot[None, :]).astype(bf16)
        chosen = dot(chooser, homes[step])
        if step:
            route = [(i, (i - step) % groups) for i in range(groups)]
            chosen = lax.ppermute(chosen.astype(bf16), "x", route).astype(f32)
        result = result + chosen

    grad_a = factor_gradient(lows, pieces, share, here)
    return (result.astype(bf16), grad_a.T, grad_b.T)


def solution(mesh):
    n_dp, n_expert = mesh.shape["dp"], mesh.shape["expert"]
    split = Mesh(mesh.devices.reshape(n_dp, n_expert // 2, 2), every)
    return jax.shard_map(
        shards,
        mesh=split,
        in_specs=(
            P(every, None),
            P(("x", "core"), None),
            P(None, every),
            P(None, every),
            P(every, None),
            P("dp", None),
            P(None, every),
            P(),
        ),
        out_specs=(P(every, None), P(every, None), P(every, None)),
        check_vma=False,
    )
```

```python
import functools
import math

import jax
import jax.numpy as jnp
from jax import lax
from jax.experimental import pallas as pl
from jax.experimental.pallas import tpu as pltpu
from jax.sharding import Mesh, PartitionSpec as P

adapter_scale = 0.25
bf16, f32 = jnp.bfloat16, jnp.float32
VMEM_LIMIT = 20 * 2**20
every = ("dp", "x", "core")
NEAR = (0, 2, 4, 6, 1, 3, 5, 7)


def swap(block, axis):
    return lax.ppermute(block, axis, [(0, 1), (1, 0)])


def across(block, axis, apart_by):
    count = lax.axis_size(axis)
    return lax.ppermute(block, axis, [(i, i ^ apart_by) for i in range(count)])


def gather_eight(block, *meanwhile):
    near = across(block, "dp", 1)
    far = [across(block, "dp", bits) for bits in NEAR[1:4]]
    if meanwhile:
        far[0], meanwhile = lax.optimization_barrier((far[0], meanwhile))
    return [block, *far, near, *[across(other, "dp", 1) for other in far]], *meanwhile


def order_of(place, blocks, eight, first=0):
    return [lax.bitwise_xor(place, NEAR[k]) if eight else k for k in range(first, first + blocks)]


def exchange(blocks, axis):
    return lax.all_to_all(blocks, axis, 0, 0, tiled=True)


def dot(left, right):
    return jnp.dot(left, right, preferred_element_type=f32)


def dot_last(left, right):
    return lax.dot_general(left, right, (((1,), (1,)), ((), ())), preferred_element_type=f32)


def dot_first(left, right):
    return lax.dot_general(left, right, (((0,), (0,)), ((), ())), preferred_element_type=f32)


def sigmoid(v):
    return 1.0 / (1.0 + jnp.exp(-v))


def struct(shape, dtype):
    return jax.ShapeDtypeStruct(shape, dtype)


def vmem(count):
    return [pl.BlockSpec(memory_space=pltpu.VMEM)] * count


def params():
    return pltpu.CompilerParams(vmem_limit_bytes=VMEM_LIMIT)


def cost(flops, moved):
    return pl.CostEstimate(flops=int(flops), bytes_accessed=int(moved), transcendentals=0)


def beside(rows):
    half = rows.shape[0] // 2
    return jnp.concatenate([rows[:half], rows[half:]], axis=1)


def apart(wide):
    rank = wide.shape[1] // 2
    return jnp.concatenate([wide[:, :rank], wide[:, rank:]], axis=0)


def near_kernel(here_ref, tokens_ref, factor_ref, router_ref, tokens_out, factor_out, route_out, router_near, sems):
    pairs = ((tokens_ref, tokens_out), (factor_ref, factor_out), (router_ref, router_near))
    copies = [pltpu.make_async_copy(*pair, sems.at[i]) for i, pair in enumerate(pairs)]
    for copy in copies:
        copy.start()
    for copy in copies:
        copy.wait()
    picked = lax.broadcasted_iota(jnp.int32, (router_near.shape[0], 1), 0) == here_ref[1]
    route_out[...] = jnp.sum(jnp.where(picked, router_near[...].astype(f32), 0.0), axis=0, keepdims=True)


def brought_near(tokens, factor, router, here):
    return pl.pallas_call(
        near_kernel,
        in_specs=[pl.BlockSpec(memory_space=pltpu.SMEM)] + [pl.BlockSpec(memory_space=pl.ANY)] * 3,
        out_specs=vmem(3),
        out_shape=[
            struct(tokens.shape, bf16),
            struct(factor.shape, bf16),
            struct((1, router.shape[1]), f32),
        ],
        scratch_shapes=[pltpu.VMEM(router.shape, bf16), pltpu.SemaphoreType.DMA((3,))],
        compiler_params=params(),
        name="near",
    )(here, *[pltpu.with_memory_space_constraint(array, pltpu.HBM) for array in (tokens, factor, router)])


def pack_kernel(n_blocks, placer_ref, *refs):
    blocks = refs[:n_blocks]
    outs = refs[n_blocks:]
    capacity, width = outs[0].shape
    chunk = width // 6
    for k in range(6):
        at = slice(k * chunk, (k + 1) * chunk)
        rows = jnp.concatenate([block[:, at] for block in blocks], axis=0)
        packed = dot(placer_ref[...], rows).astype(bf16)
        for step, out in enumerate(outs):
            out[:, at] = packed[step * capacity : (step + 1) * capacity]


def pack(placer, blocks, capacity):
    count, width = placer.shape[0], blocks[0].shape[1]
    return pl.pallas_call(
        functools.partial(pack_kernel, len(blocks)),
        in_specs=vmem(1 + len(blocks)),
        out_specs=vmem(count // capacity),
        out_shape=[struct((capacity, width), bf16)] * (count // capacity),
        compiler_params=params(),
        name="pack",
    )(placer, *blocks)


def low_kernel(n_parts, place_ref, *refs):
    parts, factor_ref, out_ref = refs[:n_parts], refs[n_parts], refs[n_parts + 1]
    depth = factor_ref.shape[1]
    if depth < parts[0].shape[1]:
        at = pl.ds(pl.multiple_of(place_ref[0] * depth, depth), depth)
    else:
        at = slice(None)
    capacity = parts[0].shape[0]
    rows = dot_last(jnp.concatenate([r[:, at] for r in parts], axis=0), factor_ref[...])
    for step in range(n_parts):
        piece = beside(rows[step * capacity : (step + 1) * capacity]).astype(bf16)
        group = lax.rem(place_ref[1] + step, n_parts)
        for i in range(out_ref.shape[0] // (2 * n_parts)):
            spot = (i * n_parts + group) * 2
            out_ref[spot] = piece
            out_ref[spot + 1] = piece


def low_pieces(parts, factor, here, place, n_dp):
    rank, depth = factor.shape
    capacity = parts[0].shape[0]
    if depth % 128:
        parts = [lax.dynamic_slice_in_dim(part, place * depth, depth, 1) for part in parts]
    return pl.pallas_call(
        functools.partial(low_kernel, len(parts)),
        in_specs=[pl.BlockSpec(memory_space=pltpu.SMEM)] + vmem(len(parts) + 1),
        out_specs=vmem(1)[0],
        out_shape=struct((n_dp * len(parts) * 2, capacity // 2, 2 * rank), bf16),
        compiler_params=params(),
        name="low_pieces",
    )(here, *parts, factor)


def lift_kernel(n_parts, *refs):
    parts = refs[:n_parts]
    weight_ref, up_ref, route_ref, pre_ref, lifted_ref, gate_ref, weight, up, sems = refs[n_parts:]
    width = parts[0].shape[1]
    steps = sems.shape[1]
    chunk = width // steps
    copies = []
    for k in range(steps):
        at = pl.ds(k * chunk, chunk)
        copies.append(
            (
                pltpu.make_async_copy(weight_ref.at[at], weight.at[at], sems.at[0, k]),
                pltpu.make_async_copy(up_ref.at[at], up.at[at], sems.at[1, k]),
            )
        )
    ahead = 4
    for pair in copies[:ahead]:
        pair[0].start()
        pair[1].start()
    pre = lifted = logit = 0.0
    for k in range(steps):
        at = slice(k * chunk, (k + 1) * chunk)
        for i in (0, 1):
            copies[k][i].wait()
            if k + ahead < steps:
                copies[k + ahead][i].start()
        rows = jnp.concatenate([r[:, at] for r in parts], axis=0)
        pre = pre + dot(rows, weight[at])
        lifted = lifted + dot(rows, up[at])
        logit = logit + jnp.sum(rows.astype(f32) * route_ref[:, at], axis=1, keepdims=True)
    pre_ref[...] = pre
    lifted_ref[...] = lifted
    gate_ref[...] = sigmoid(logit)


def lift(parts, gate_weight, up_weight, route):
    capacity, width = parts[0].shape
    units = gate_weight.shape[1]
    count = capacity * len(parts)
    return pl.pallas_call(
        functools.partial(lift_kernel, len(parts)),
        in_specs=vmem(len(parts))
        + [pl.BlockSpec(memory_space=pl.ANY)] * 2
        + vmem(1),
        out_specs=vmem(3),
        scratch_shapes=[
            pltpu.VMEM(gate_weight.shape, bf16),
            pltpu.VMEM(up_weight.shape, bf16),
            pltpu.SemaphoreType.DMA((2, 12)),
        ],
        out_shape=(
            struct((count, units), f32),
            struct((count, units), f32),
            struct((count, 1), f32),
        ),
        cost_estimate=cost(4 * count * width * units, 4 * width * units),
        compiler_params=params(),
        name="lift",
    )(
        *parts,
        pltpu.with_memory_space_constraint(gate_weight, pltpu.HBM),
        pltpu.with_memory_space_constraint(up_weight, pltpu.HBM),
        route,
    )


def bring(source, target, sems, starts):
    copies = []
    for k, start in enumerate(starts):
        at = pl.ds(start, target.shape[2])
        copies.append(pltpu.make_async_copy(source.at[:, at], target.at[k], sems.at[k]))
    for copy in copies:
        copy.start()
    return copies


def down_kernel(
    place_ref, base_ref, lifted_ref, low_ref, factor_ref, weight_ref, own_ref, other_ref, slope_ref, low_out, down_ref, sems
):
    blocks, half, wide = own_ref.shape
    copies = bring(weight_ref, down_ref, sems, [k * wide for k in range(blocks)])
    groups = low_ref.shape[1]
    sums = []
    for core in (place_ref[2], 1 - place_ref[2]):
        for step in range(groups):
            group = lax.rem(place_ref[1] - step + groups, groups)
            sums.append(apart(jnp.sum(low_ref[:, group, core].astype(f32), axis=0)))
    low = jnp.concatenate(sums, axis=0).astype(bf16)
    pre = base_ref[...] + adapter_scale * dot(low, factor_ref[...])
    low_out[...] = low
    lifted = lifted_ref[...]
    sig = sigmoid(pre)
    slope_ref[...] = (lifted * (sig * (1.0 + pre * (1.0 - sig)))).T
    hidden = (pre * sig * lifted).astype(bf16)
    for k in range(blocks):
        if k % 2 == 0:
            copies[k].wait()
            copies[k + 1].wait()
        partial = dot(hidden, down_ref[k]).astype(bf16)
        own_ref[k] = partial[:half]
        other_ref[k] = partial[half:]


def down(base, lifted, low_parts, factor, down_weight, blocks, here):
    count, units = base.shape
    half, width = count // 2, down_weight.shape[1]
    shape = struct((blocks, half, width // blocks), bf16)
    *outs, kept = pl.pallas_call(
        down_kernel,
        in_specs=[pl.BlockSpec(memory_space=pltpu.SMEM)] + vmem(4) + [pl.BlockSpec(memory_space=pl.ANY)],
        out_specs=vmem(5),
        scratch_shapes=[pltpu.SemaphoreType.DMA((blocks,))],
        out_shape=(
            shape,
            shape,
            struct((units, count), f32),
            struct((count, factor.shape[0]), bf16),
            pltpu.VMEM((blocks, units, width // blocks), bf16),
        ),
        cost_estimate=cost(2 * count * width * units, 2 * width * units),
        compiler_params=params(),
        name="down",
    )(
        here,
        base,
        lifted,
        low_parts,
        factor,
        pltpu.with_memory_space_constraint(down_weight, pltpu.HBM),
    )
    return *outs, pltpu.with_memory_space_constraint(kept, pltpu.VMEM)


def fold_core_kernel(place_ref, own_ref, got_ref, keep_ref, far_ref, near_ref):
    line, bit = place_ref[0] // 2, lax.rem(place_ref[0], 2)

    def folded(at):
        return (own_ref[at].astype(f32) + got_ref[at].astype(f32)).astype(bf16)

    for k in range(4):
        at = 2 * lax.bitwise_xor(line, k)
        keep_ref[k] = folded(at + bit)
        out_ref = near_ref if k < 2 else far_ref
        out_ref[k % 2] = folded(at + 1 - bit)


def fold_core(own, got, here):
    shapes = [struct((count, *own.shape[1:]), bf16) for count in (4, 2, 2)]
    return pl.pallas_call(
        fold_core_kernel,
        in_specs=[pl.BlockSpec(memory_space=pltpu.SMEM)] + vmem(2),
        out_specs=vmem(3),
        out_shape=shapes,
        compiler_params=params(),
        name="fold_core",
    )(here, own, got)


def fold_near_kernel(first, keep_ref, got_ref, *out_refs):
    for k, out_ref in enumerate(out_refs):
        out_ref[...] = (keep_ref[first + k].astype(f32) + got_ref[k].astype(f32)).astype(bf16)


def fold_near(keep, got, first):
    return pl.pallas_call(
        functools.partial(fold_near_kernel, first),
        in_specs=vmem(2),
        out_specs=vmem(2),
        out_shape=[struct(keep.shape[1:], bf16)] * 2,
        compiler_params=params(),
        name="fold_near",
    )(keep, got)


def mix_kernel(n_terms, *refs):
    gate_ref, out_ref = refs[n_terms:]
    total = refs[0][...].astype(f32)
    for term in refs[1:n_terms]:
        total = total + term[...].astype(f32)
    out_ref[...] = (gate_ref[: out_ref.shape[0]] * total).astype(bf16)


def mix(terms, gate):
    return pl.pallas_call(
        functools.partial(mix_kernel, len(terms)),
        in_specs=vmem(len(terms) + 1),
        out_specs=vmem(1)[0],
        out_shape=struct(terms[0].shape, bf16),
        compiler_params=params(),
        name="mix",
    )(*terms, gate)


def back_sum(parts, owns, others, order, gate_ref, down_ref, loss_factor):
    wide = owns[0].shape[1]
    scale = loss_factor * gate_ref[...]
    total = 0.0
    for block, own, other in zip(order, owns, others):
        start = block * wide
        at = pl.ds(start if isinstance(start, int) else pl.multiple_of(start, wide), wide)
        mixed = jnp.concatenate([own[...], other[...]], axis=0).astype(f32)
        rows = jnp.concatenate([r[:, at] for r in parts], axis=0).astype(f32)
        back = (scale * (mixed - rows)).astype(bf16)
        total = total + dot_last(down_ref[block], back)
    return total


def back_first_kernel(n_parts, n_blocks, eight, loss_factor, here_ref, *refs):
    parts, refs = refs[:n_parts], refs[n_parts:]
    owns, others, refs = refs[:n_blocks], refs[n_blocks : 2 * n_blocks], refs[2 * n_blocks :]
    gate_ref, down_ref, out_ref = refs
    order = order_of(here_ref[0], n_blocks, eight)
    out_ref[...] = back_sum(parts, owns, others, order, gate_ref, down_ref, loss_factor)


def back_last_kernel(n_parts, n_blocks, eight, loss_factor, here_ref, *refs):
    parts, refs = refs[:n_parts], refs[n_parts:]
    owns, others, refs = refs[:n_blocks], refs[n_blocks : 2 * n_blocks], refs[2 * n_blocks :]
    gate_ref, down_ref, first_ref, slope_ref, factor_ref, low_out, back_out = refs
    order = order_of(here_ref[0], n_blocks, eight, n_blocks)
    total = first_ref[...] + back_sum(parts, owns, others, order, gate_ref, down_ref, loss_factor)
    back_pre = (total * slope_ref[...]).astype(bf16)
    back_low = beside(adapter_scale * dot(factor_ref[...], back_pre)).astype(bf16)
    for i in range(low_out.shape[0]):
        low_out[i] = back_low
    back_out[...] = back_pre


def rest_kernel(n_blocks, eight, here_ref, *refs):
    owns, (back_ref, low_ref, grad_ref, *homes) = refs[:n_blocks], refs[n_blocks:]
    half, wide = owns[0].shape
    capacity = half // len(homes)
    grad_ref[...] = adapter_scale * lax.dot_general(
        low_ref[...], back_ref[...], (((0,), (1,)), ((), ())), preferred_element_type=f32
    )
    for block, own in zip(order_of(here_ref[0], n_blocks, eight), owns):
        start = block * wide
        at = pl.ds(start if isinstance(start, int) else pl.multiple_of(start, wide), wide)
        for step, home in enumerate(homes):
            home[:, at] = own[step * capacity : (step + 1) * capacity]


def rest(owns, here, eight, back_pre, low, capacity):
    half, wide = owns[0].shape
    homes = half // capacity
    return pl.pallas_call(
        functools.partial(rest_kernel, len(owns), eight),
        in_specs=[pl.BlockSpec(memory_space=pltpu.SMEM)] + vmem(len(owns) + 2),
        out_specs=vmem(1 + homes),
        out_shape=(
            struct((low.shape[1], back_pre.shape[0]), f32),
            *[struct((capacity, wide * len(owns)), bf16)] * homes,
        ),
        compiler_params=params(),
        name="rest",
    )(here, *owns, back_pre, low)


def back_first(parts, owns, others, here, eight, gate, kept, loss_factor):
    units = kept.shape[1]
    count, blocks, wide = gate.shape[0], len(owns), owns[0].shape[1]
    return pl.pallas_call(
        functools.partial(back_first_kernel, len(parts), blocks, eight, loss_factor),
        in_specs=[pl.BlockSpec(memory_space=pltpu.SMEM)] + vmem(len(parts) + 2 * blocks + 2),
        out_specs=vmem(1)[0],
        out_shape=struct((units, count), f32),
        cost_estimate=cost(2 * count * blocks * wide * units, 2 * blocks * wide * units),
        compiler_params=params(),
        name="back_first",
    )(here, *parts, *owns, *others, gate, kept)


def back_last(parts, owns, others, here, eight, gate, kept, first, slope, factor, loss_factor, copies):
    wide = owns[0].shape[1]
    units, count = slope.shape
    rank, blocks = factor.shape[0], len(others)
    return pl.pallas_call(
        functools.partial(back_last_kernel, len(parts), blocks, eight, loss_factor),
        in_specs=[pl.BlockSpec(memory_space=pltpu.SMEM)] + vmem(len(parts) + 2 * blocks + 5),
        out_specs=vmem(2),
        out_shape=(struct((copies, rank // 2, 2 * count), bf16), struct((units, count), bf16)),
        cost_estimate=cost(2 * count * blocks * wide * units, 2 * blocks * wide * units),
        compiler_params=params(),
        name="back_last",
    )(here, *parts, *owns, *others, gate, kept, first, slope, factor)


def factor_kernel(place_ref, low_ref, piece_ref, out_ref):
    share = out_ref.shape[1]
    groups, count = piece_ref.shape[:2]
    half = count // 2
    group, core = place_ref[1], place_ref[2]
    lows, rows = [], []
    for step in range(groups):
        source = lax.rem(group - step + groups, groups)
        mine = apart(jnp.sum(low_ref[:, source, core].astype(f32), axis=0))
        theirs = apart(jnp.sum(low_ref[:, source, 1 - core].astype(f32), axis=0))
        lows.append(mine + jnp.concatenate([theirs[:, half:], theirs[:, :half]], axis=1))
        rows.append(piece_ref[step, :, :share])
    low = jnp.concatenate(lows, axis=1)
    high = low.astype(bf16)
    rest = (low - high.astype(f32)).astype(bf16)
    out_ref[...] = dot(jnp.concatenate([high, rest], axis=1), jnp.concatenate(rows + rows, axis=0))


def factor_gradient(lows, pieces, share, here):
    rank = 2 * lows.shape[3]
    return pl.pallas_call(
        factor_kernel,
        in_specs=[pl.BlockSpec(memory_space=pltpu.SMEM)] + vmem(2),
        out_specs=vmem(1)[0],
        out_shape=struct((rank, share), f32),
        compiler_params=params(),
        name="factor_gradient",
    )(here, lows, pieces)


def shards(
    tokens,
    expert_choice_table,
    gate_weight,
    up_weight,
    down_weight,
    adapter_down_shared,
    adapter_gate_factor,
    router,
):
    tok_rows, width = tokens.shape
    n_dp = lax.axis_size("dp")
    groups = lax.axis_size("x")
    place = lax.axis_index("dp")
    group = lax.axis_index("x")
    core = lax.axis_index("core")
    col_rows = n_dp * tok_rows
    capacity = col_rows // groups
    half = groups * capacity
    wide = width // n_dp
    rank = adapter_down_shared.shape[1]
    devices = n_dp * groups * 2
    share = width // devices
    loss_factor = math.sqrt(groups / (tok_rows * devices))
    blocks = 8
    eight = n_dp == blocks

    here = jnp.stack([place, group, core])

    labels = expert_choice_table[0]
    index = jnp.arange(col_rows, dtype=jnp.int32)
    number = index
    if eight:
        order = lax.bitwise_xor(jnp.array(NEAR, jnp.int32), place)
        number = (order[:, None] * tok_rows + jnp.arange(tok_rows)[None, :]).reshape(col_rows)
        labels = jnp.sum(jnp.where(number[:, None] == index[None, :], labels[None, :], 0), axis=1)
    before = (labels[None, :] == labels[:, None]) & (number[None, :] < number[:, None])
    ordinal = jnp.sum(before.astype(jnp.int32), axis=1)
    ahead = lax.rem(labels - group + groups, groups)
    target = ahead * capacity + ordinal
    placer = (index[:, None] == target[None, :]).astype(bf16)
    tokens_near, factor, own_route = brought_near(tokens, adapter_down_shared.T, router.T, here)
    if eight:
        column, placer = gather_eight(tokens, placer)
        column[0] = tokens_near
        column, placer, factor, own_route = lax.optimization_barrier((column, placer, factor, own_route))
        own_target = target[:tok_rows]
    else:
        column = exchange(jnp.broadcast_to(tokens[None], (n_dp, tok_rows, width)), "dp")
        column = [column.reshape(col_rows, width)]
        own_target = lax.dynamic_slice_in_dim(target, place * tok_rows, tok_rows, 0)
    packed = pack(placer, column, capacity)
    parts = [packed[0]]
    for step in range(1, groups):
        route = [(i, (i + step) % groups) for i in range(groups)]
        parts.append(lax.ppermute(packed[step], "x", route))
    parts = parts + [swap(part, "core") for part in parts]

    low_parts = low_pieces(packed, factor, here, place, n_dp)
    low_parts = exchange(low_parts, every).reshape(n_dp, groups, 2, capacity // 2, 2 * rank)
    base, lifted, gate = lift(parts, gate_weight, up_weight, own_route)
    low_parts, gate = lax.optimization_barrier((low_parts, gate))
    own, other, slope, low, kept = down(
        base, lifted, low_parts, adapter_gate_factor, down_weight, blocks, here
    )

    rows = jnp.concatenate(parts, axis=0)
    numbers = jnp.broadcast_to(own_target.astype(bf16)[None], (2 * half, tok_rows))
    pieces = []
    for step in range(groups):
        to = lax.rem(group + step, groups)
        at = ((place * groups + to) * 2 + core) * share
        piece = jnp.concatenate([lax.dynamic_slice_in_dim(rows, at, share, 1), numbers], axis=1)
        route = [(i, (i + step) % groups) for i in range(groups)]
        pieces.append(lax.ppermute(piece, "x", route) if step else piece)
    pieces = jnp.stack(pieces)

    got = swap(other, "core")
    if eight:
        keep, far, near = fold_core(own, got, here)
        far, near = across(far, "dp", 1), across(near, "dp", 1)
        two, three = fold_near(keep, far, 2)
        mine, one = fold_near(keep, near, 0)
        terms = [mine, across(one, "dp", 2), across(two, "dp", 4), across(three, "dp", 6)]
        terms, pieces = lax.optimization_barrier((terms, pieces))
        (owns,) = gather_eight(mix(terms, gate))
    else:
        summed = (own.astype(f32) + got.astype(f32)).astype(bf16)
        summed = summed.transpose(1, 0, 2).reshape(half, n_dp, wide).transpose(1, 0, 2)
        summed = exchange(summed, "dp")
        mixed = mix([summed[i] for i in range(n_dp)], gate)
        mixed = exchange(jnp.broadcast_to(mixed[None], (n_dp, half, wide)), "dp")
        mixed = mixed.transpose(1, 0, 2).reshape(half, width)
        owns = [mixed[:, i * (width // blocks) : (i + 1) * (width // blocks)] for i in range(blocks)]
    others = [swap(block, "core") for block in owns]

    first = back_first(
        parts, owns[: blocks // 2], others[: blocks // 2], here, eight, gate, kept, loss_factor
    )
    back_low, back_pre = back_last(
        parts,
        owns[blocks // 2 :],
        others[blocks // 2 :],
        here,
        eight,
        gate,
        kept,
        first,
        slope,
        adapter_gate_factor,
        loss_factor,
        devices,
    )
    lows = exchange(back_low, every).reshape(n_dp, groups, 2, rank // 2, 4 * half)
    grad_b, *homes = rest(owns, here, eight, back_pre, low, capacity)

    result = jnp.zeros((tok_rows, width), f32)
    for step in range(groups):
        spot = index[step * capacity : (step + 1) * capacity]
        wanted = pieces[step, 0, share:].astype(jnp.int32)
        chooser = (wanted[:, None] == spot[None, :]).astype(bf16)
        chosen = dot(chooser, homes[step])
        if step:
            route = [(i, (i - step) % groups) for i in range(groups)]
            chosen = lax.ppermute(chosen.astype(bf16), "x", route).astype(f32)
        result = result + chosen

    grad_a = factor_gradient(lows, pieces, share, here)
    return (result.astype(bf16), grad_a.T, grad_b.T)


def solution(mesh):
    n_dp, n_expert = mesh.shape["dp"], mesh.shape["expert"]
    split = Mesh(mesh.devices.reshape(n_dp, n_expert // 2, 2), every)
    return jax.shard_map(
        shards,
        mesh=split,
        in_specs=(
            P(every, None),
            P(("x", "core"), None),
            P(None, every),
            P(None, every),
            P(every, None),
            P("dp", None),
            P(None, every),
            P(),
        ),
        out_specs=(P(every, None), P(every, None), P(every, None)),
        check_vma=False,
    )
```

```python
import functools
import math

import jax
import jax.numpy as jnp
from jax import lax
from jax.experimental import pallas as pl
from jax.experimental.pallas import tpu as pltpu
from jax.sharding import Mesh, PartitionSpec as P

adapter_scale = 0.25
bf16, f32 = jnp.bfloat16, jnp.float32
VMEM_LIMIT = 20 * 2**20
every = ("dp", "x", "core")
NEAR = (0, 2, 4, 6, 1, 3, 5, 7)


def swap(block, axis):
    return lax.ppermute(block, axis, [(0, 1), (1, 0)])


def across(block, axis, apart_by):
    count = lax.axis_size(axis)
    return lax.ppermute(block, axis, [(i, i ^ apart_by) for i in range(count)])


def gather_eight(block, *meanwhile):
    near = across(block, "dp", 1)
    far = [across(block, "dp", bits) for bits in NEAR[1:4]]
    if meanwhile:
        far[0], meanwhile = lax.optimization_barrier((far[0], meanwhile))
    return [block, *far, near, *[across(other, "dp", 1) for other in far]], *meanwhile


def order_of(place, blocks, eight, first=0):
    return [lax.bitwise_xor(place, NEAR[k]) if eight else k for k in range(first, first + blocks)]


def exchange(blocks, axis):
    return lax.all_to_all(blocks, axis, 0, 0, tiled=True)


def dot(left, right):
    return jnp.dot(left, right, preferred_element_type=f32)


def dot_last(left, right):
    return lax.dot_general(left, right, (((1,), (1,)), ((), ())), preferred_element_type=f32)


def dot_first(left, right):
    return lax.dot_general(left, right, (((0,), (0,)), ((), ())), preferred_element_type=f32)


def sigmoid(v):
    return 1.0 / (1.0 + jnp.exp(-v))


def struct(shape, dtype):
    return jax.ShapeDtypeStruct(shape, dtype)


def vmem(count):
    return [pl.BlockSpec(memory_space=pltpu.VMEM)] * count


class Here:
    def __init__(self, refs):
        self.refs = refs

    def __getitem__(self, which):
        return self.refs[which][0]


def seated(kernel):
    def run(place_ref, group_ref, core_ref, *refs):
        kernel(Here((place_ref, group_ref, core_ref)), *refs)

    return run


def params():
    return pltpu.CompilerParams(vmem_limit_bytes=VMEM_LIMIT)


def cost(flops, moved):
    return pl.CostEstimate(flops=int(flops), bytes_accessed=int(moved), transcendentals=0)


def beside(rows):
    half = rows.shape[0] // 2
    return jnp.concatenate([rows[:half], rows[half:]], axis=1)


def apart(wide):
    rank = wide.shape[1] // 2
    return jnp.concatenate([wide[:, :rank], wide[:, rank:]], axis=0)


def near_kernel(here_ref, tokens_ref, factor_ref, router_ref, tokens_out, factor_out, route_out, router_near, sems):
    pairs = ((tokens_ref, tokens_out), (factor_ref, factor_out), (router_ref, router_near))
    copies = [pltpu.make_async_copy(*pair, sems.at[i]) for i, pair in enumerate(pairs)]
    for copy in copies:
        copy.start()
    for copy in copies:
        copy.wait()
    picked = lax.broadcasted_iota(jnp.int32, (router_near.shape[0], 1), 0) == here_ref[1]
    route_out[...] = jnp.sum(jnp.where(picked, router_near[...].astype(f32), 0.0), axis=0, keepdims=True)


def brought_near(tokens, factor, router, here):
    return pl.pallas_call(
        seated(near_kernel),
        in_specs=[pl.BlockSpec(memory_space=pltpu.SMEM)] * 3 + [pl.BlockSpec(memory_space=pl.ANY)] * 3,
        out_specs=vmem(3),
        out_shape=[
            struct(tokens.shape, bf16),
            struct(factor.shape, bf16),
            struct((1, router.shape[1]), f32),
        ],
        scratch_shapes=[pltpu.VMEM(router.shape, bf16), pltpu.SemaphoreType.DMA((3,))],
        compiler_params=params(),
        name="near",
    )(*here, *[pltpu.with_memory_space_constraint(array, pltpu.HBM) for array in (tokens, factor, router)])


def pack_kernel(n_blocks, placer_ref, *refs):
    blocks = refs[:n_blocks]
    outs = refs[n_blocks:]
    capacity, width = outs[0].shape
    chunk = width // 6
    for k in range(6):
        at = slice(k * chunk, (k + 1) * chunk)
        rows = jnp.concatenate([block[:, at] for block in blocks], axis=0)
        packed = dot(placer_ref[...], rows).astype(bf16)
        for step, out in enumerate(outs):
            out[:, at] = packed[step * capacity : (step + 1) * capacity]


def pack(placer, blocks, capacity):
    count, width = placer.shape[0], blocks[0].shape[1]
    return pl.pallas_call(
        functools.partial(pack_kernel, len(blocks)),
        in_specs=vmem(1 + len(blocks)),
        out_specs=vmem(count // capacity),
        out_shape=[struct((capacity, width), bf16)] * (count // capacity),
        compiler_params=params(),
        name="pack",
    )(placer, *blocks)


def low_kernel(n_parts, place_ref, *refs):
    parts, factor_ref, out_ref = refs[:n_parts], refs[n_parts], refs[n_parts + 1]
    depth = factor_ref.shape[1]
    if depth < parts[0].shape[1]:
        at = pl.ds(pl.multiple_of(place_ref[0] * depth, depth), depth)
    else:
        at = slice(None)
    capacity = parts[0].shape[0]
    rows = dot_last(jnp.concatenate([r[:, at] for r in parts], axis=0), factor_ref[...])
    for step in range(n_parts):
        piece = beside(rows[step * capacity : (step + 1) * capacity]).astype(bf16)
        group = lax.rem(place_ref[1] + step, n_parts)
        for i in range(out_ref.shape[0] // (2 * n_parts)):
            spot = (i * n_parts + group) * 2
            out_ref[spot] = piece
            out_ref[spot + 1] = piece


def low_pieces(parts, factor, here, place, n_dp):
    rank, depth = factor.shape
    capacity = parts[0].shape[0]
    if depth % 128:
        parts = [lax.dynamic_slice_in_dim(part, place * depth, depth, 1) for part in parts]
    return pl.pallas_call(
        seated(functools.partial(low_kernel, len(parts))),
        in_specs=[pl.BlockSpec(memory_space=pltpu.SMEM)] * 3 + vmem(len(parts) + 1),
        out_specs=vmem(1)[0],
        out_shape=struct((n_dp * len(parts) * 2, capacity // 2, 2 * rank), bf16),
        compiler_params=params(),
        name="low_pieces",
    )(*here, *parts, factor)


def lift_kernel(n_parts, *refs):
    parts = refs[:n_parts]
    weight_ref, up_ref, route_ref, pre_ref, lifted_ref, gate_ref, weight, up, sems = refs[n_parts:]
    width = parts[0].shape[1]
    steps = sems.shape[1]
    chunk = width // steps
    copies = []
    for k in range(steps):
        at = pl.ds(k * chunk, chunk)
        copies.append(
            (
                pltpu.make_async_copy(weight_ref.at[at], weight.at[at], sems.at[0, k]),
                pltpu.make_async_copy(up_ref.at[at], up.at[at], sems.at[1, k]),
            )
        )
    ahead = 4
    for pair in copies[:ahead]:
        pair[0].start()
        pair[1].start()
    pre = lifted = logit = 0.0
    for k in range(steps):
        at = slice(k * chunk, (k + 1) * chunk)
        for i in (0, 1):
            copies[k][i].wait()
            if k + ahead < steps:
                copies[k + ahead][i].start()
        rows = jnp.concatenate([r[:, at] for r in parts], axis=0)
        pre = pre + dot(rows, weight[at])
        lifted = lifted + dot(rows, up[at])
        logit = logit + jnp.sum(rows.astype(f32) * route_ref[:, at], axis=1, keepdims=True)
    pre_ref[...] = pre
    lifted_ref[...] = lifted
    gate_ref[...] = sigmoid(logit)


def lift(parts, gate_weight, up_weight, route):
    capacity, width = parts[0].shape
    units = gate_weight.shape[1]
    count = capacity * len(parts)
    return pl.pallas_call(
        functools.partial(lift_kernel, len(parts)),
        in_specs=vmem(len(parts))
        + [pl.BlockSpec(memory_space=pl.ANY)] * 2
        + vmem(1),
        out_specs=vmem(3),
        scratch_shapes=[
            pltpu.VMEM(gate_weight.shape, bf16),
            pltpu.VMEM(up_weight.shape, bf16),
            pltpu.SemaphoreType.DMA((2, 12)),
        ],
        out_shape=(
            struct((count, units), f32),
            struct((count, units), f32),
            struct((count, 1), f32),
        ),
        cost_estimate=cost(4 * count * width * units, 4 * width * units),
        compiler_params=params(),
        name="lift",
    )(
        *parts,
        pltpu.with_memory_space_constraint(gate_weight, pltpu.HBM),
        pltpu.with_memory_space_constraint(up_weight, pltpu.HBM),
        route,
    )


def bring(source, target, sems, starts):
    copies = []
    for k, start in enumerate(starts):
        at = pl.ds(start, target.shape[2])
        copies.append(pltpu.make_async_copy(source.at[:, at], target.at[k], sems.at[k]))
    for copy in copies:
        copy.start()
    return copies


def down_kernel(
    place_ref, base_ref, lifted_ref, low_ref, factor_ref, weight_ref, own_ref, other_ref, slope_ref, low_out, down_ref, sems
):
    blocks, half, wide = own_ref.shape
    copies = bring(weight_ref, down_ref, sems, [k * wide for k in range(blocks)])
    groups = low_ref.shape[1]
    sums = []
    for core in (place_ref[2], 1 - place_ref[2]):
        for step in range(groups):
            group = lax.rem(place_ref[1] - step + groups, groups)
            sums.append(apart(jnp.sum(low_ref[:, group, core].astype(f32), axis=0)))
    low = jnp.concatenate(sums, axis=0).astype(bf16)
    pre = base_ref[...] + adapter_scale * dot(low, factor_ref[...])
    low_out[...] = low
    lifted = lifted_ref[...]
    sig = sigmoid(pre)
    slope_ref[...] = (lifted * (sig * (1.0 + pre * (1.0 - sig)))).T
    hidden = (pre * sig * lifted).astype(bf16)
    for k in range(blocks):
        if k % 2 == 0:
            copies[k].wait()
            copies[k + 1].wait()
        partial = dot(hidden, down_ref[k]).astype(bf16)
        own_ref[k] = partial[:half]
        other_ref[k] = partial[half:]


def down(base, lifted, low_parts, factor, down_weight, blocks, here):
    count, units = base.shape
    half, width = count // 2, down_weight.shape[1]
    shape = struct((blocks, half, width // blocks), bf16)
    *outs, kept = pl.pallas_call(
        seated(down_kernel),
        in_specs=[pl.BlockSpec(memory_space=pltpu.SMEM)] * 3 + vmem(4) + [pl.BlockSpec(memory_space=pl.ANY)],
        out_specs=vmem(5),
        scratch_shapes=[pltpu.SemaphoreType.DMA((blocks,))],
        out_shape=(
            shape,
            shape,
            struct((units, count), f32),
            struct((count, factor.shape[0]), bf16),
            pltpu.VMEM((blocks, units, width // blocks), bf16),
        ),
        cost_estimate=cost(2 * count * width * units, 2 * width * units),
        compiler_params=params(),
        name="down",
    )(
        *here,
        base,
        lifted,
        low_parts,
        factor,
        pltpu.with_memory_space_constraint(down_weight, pltpu.HBM),
    )
    return *outs, pltpu.with_memory_space_constraint(kept, pltpu.VMEM)


def fold_core_kernel(place_ref, own_ref, got_ref, keep_ref, far_ref, near_ref):
    line, bit = place_ref[0] // 2, lax.rem(place_ref[0], 2)

    def folded(at):
        return (own_ref[at].astype(f32) + got_ref[at].astype(f32)).astype(bf16)

    for k in range(4):
        at = 2 * lax.bitwise_xor(line, k)
        keep_ref[k] = folded(at + bit)
        out_ref = near_ref if k < 2 else far_ref
        out_ref[k % 2] = folded(at + 1 - bit)


def fold_core(own, got, here):
    shapes = [struct((count, *own.shape[1:]), bf16) for count in (4, 2, 2)]
    return pl.pallas_call(
        seated(fold_core_kernel),
        in_specs=[pl.BlockSpec(memory_space=pltpu.SMEM)] * 3 + vmem(2),
        out_specs=vmem(3),
        out_shape=shapes,
        compiler_params=params(),
        name="fold_core",
    )(*here, own, got)


def fold_near_kernel(first, keep_ref, got_ref, *out_refs):
    for k, out_ref in enumerate(out_refs):
        out_ref[...] = (keep_ref[first + k].astype(f32) + got_ref[k].astype(f32)).astype(bf16)


def fold_near(keep, got, first):
    return pl.pallas_call(
        functools.partial(fold_near_kernel, first),
        in_specs=vmem(2),
        out_specs=vmem(2),
        out_shape=[struct(keep.shape[1:], bf16)] * 2,
        compiler_params=params(),
        name="fold_near",
    )(keep, got)


def mix_kernel(n_terms, *refs):
    gate_ref, out_ref = refs[n_terms:]
    total = refs[0][...].astype(f32)
    for term in refs[1:n_terms]:
        total = total + term[...].astype(f32)
    out_ref[...] = (gate_ref[: out_ref.shape[0]] * total).astype(bf16)


def mix(terms, gate):
    return pl.pallas_call(
        functools.partial(mix_kernel, len(terms)),
        in_specs=vmem(len(terms) + 1),
        out_specs=vmem(1)[0],
        out_shape=struct(terms[0].shape, bf16),
        compiler_params=params(),
        name="mix",
    )(*terms, gate)


def back_sum(parts, owns, others, order, gate_ref, down_ref, loss_factor):
    wide = owns[0].shape[1]
    scale = loss_factor * gate_ref[...]
    total = 0.0
    for block, own, other in zip(order, owns, others):
        start = block * wide
        at = pl.ds(start if isinstance(start, int) else pl.multiple_of(start, wide), wide)
        mixed = jnp.concatenate([own[...], other[...]], axis=0).astype(f32)
        rows = jnp.concatenate([r[:, at] for r in parts], axis=0).astype(f32)
        back = (scale * (mixed - rows)).astype(bf16)
        total = total + dot_last(down_ref[block], back)
    return total


def back_first_kernel(n_parts, n_blocks, eight, loss_factor, here_ref, *refs):
    parts, refs = refs[:n_parts], refs[n_parts:]
    owns, others, refs = refs[:n_blocks], refs[n_blocks : 2 * n_blocks], refs[2 * n_blocks :]
    gate_ref, down_ref, out_ref = refs
    order = order_of(here_ref[0], n_blocks, eight)
    out_ref[...] = back_sum(parts, owns, others, order, gate_ref, down_ref, loss_factor)


def back_last_kernel(n_parts, n_blocks, eight, loss_factor, here_ref, *refs):
    parts, refs = refs[:n_parts], refs[n_parts:]
    owns, others, refs = refs[:n_blocks], refs[n_blocks : 2 * n_blocks], refs[2 * n_blocks :]
    gate_ref, down_ref, first_ref, slope_ref, factor_ref, low_out, back_out = refs
    order = order_of(here_ref[0], n_blocks, eight, n_blocks)
    total = first_ref[...] + back_sum(parts, owns, others, order, gate_ref, down_ref, loss_factor)
    back_pre = (total * slope_ref[...]).astype(bf16)
    back_low = beside(adapter_scale * dot(factor_ref[...], back_pre)).astype(bf16)
    for i in range(low_out.shape[0]):
        low_out[i] = back_low
    back_out[...] = back_pre


def rest_kernel(n_blocks, eight, here_ref, *refs):
    owns, (back_ref, low_ref, grad_ref, *homes) = refs[:n_blocks], refs[n_blocks:]
    half, wide = owns[0].shape
    capacity = half // len(homes)
    grad_ref[...] = adapter_scale * lax.dot_general(
        low_ref[...], back_ref[...], (((0,), (1,)), ((), ())), preferred_element_type=f32
    )
    for block, own in zip(order_of(here_ref[0], n_blocks, eight), owns):
        start = block * wide
        at = pl.ds(start if isinstance(start, int) else pl.multiple_of(start, wide), wide)
        for step, home in enumerate(homes):
            home[:, at] = own[step * capacity : (step + 1) * capacity]


def rest(owns, here, eight, back_pre, low, capacity):
    half, wide = owns[0].shape
    homes = half // capacity
    return pl.pallas_call(
        seated(functools.partial(rest_kernel, len(owns), eight)),
        in_specs=[pl.BlockSpec(memory_space=pltpu.SMEM)] * 3 + vmem(len(owns) + 2),
        out_specs=vmem(1 + homes),
        out_shape=(
            struct((low.shape[1], back_pre.shape[0]), f32),
            *[struct((capacity, wide * len(owns)), bf16)] * homes,
        ),
        compiler_params=params(),
        name="rest",
    )(*here, *owns, back_pre, low)


def back_first(parts, owns, others, here, eight, gate, kept, loss_factor):
    units = kept.shape[1]
    count, blocks, wide = gate.shape[0], len(owns), owns[0].shape[1]
    return pl.pallas_call(
        seated(functools.partial(back_first_kernel, len(parts), blocks, eight, loss_factor)),
        in_specs=[pl.BlockSpec(memory_space=pltpu.SMEM)] * 3 + vmem(len(parts) + 2 * blocks + 2),
        out_specs=vmem(1)[0],
        out_shape=struct((units, count), f32),
        cost_estimate=cost(2 * count * blocks * wide * units, 2 * blocks * wide * units),
        compiler_params=params(),
        name="back_first",
    )(*here, *parts, *owns, *others, gate, kept)


def back_last(parts, owns, others, here, eight, gate, kept, first, slope, factor, loss_factor, copies):
    wide = owns[0].shape[1]
    units, count = slope.shape
    rank, blocks = factor.shape[0], len(others)
    return pl.pallas_call(
        seated(functools.partial(back_last_kernel, len(parts), blocks, eight, loss_factor)),
        in_specs=[pl.BlockSpec(memory_space=pltpu.SMEM)] * 3 + vmem(len(parts) + 2 * blocks + 5),
        out_specs=vmem(2),
        out_shape=(struct((copies, rank // 2, 2 * count), bf16), struct((units, count), bf16)),
        cost_estimate=cost(2 * count * blocks * wide * units, 2 * blocks * wide * units),
        compiler_params=params(),
        name="back_last",
    )(*here, *parts, *owns, *others, gate, kept, first, slope, factor)


def factor_kernel(place_ref, low_ref, piece_ref, out_ref):
    share = out_ref.shape[1]
    groups, count = piece_ref.shape[:2]
    half = count // 2
    group, core = place_ref[1], place_ref[2]
    lows, rows = [], []
    for step in range(groups):
        source = lax.rem(group - step + groups, groups)
        mine = apart(jnp.sum(low_ref[:, source, core].astype(f32), axis=0))
        theirs = apart(jnp.sum(low_ref[:, source, 1 - core].astype(f32), axis=0))
        lows.append(mine + jnp.concatenate([theirs[:, half:], theirs[:, :half]], axis=1))
        rows.append(piece_ref[step, :, :share])
    low = jnp.concatenate(lows, axis=1)
    high = low.astype(bf16)
    rest = (low - high.astype(f32)).astype(bf16)
    out_ref[...] = dot(jnp.concatenate([high, rest], axis=1), jnp.concatenate(rows + rows, axis=0))


def factor_gradient(lows, pieces, share, here):
    rank = 2 * lows.shape[3]
    return pl.pallas_call(
        seated(factor_kernel),
        in_specs=[pl.BlockSpec(memory_space=pltpu.SMEM)] * 3 + vmem(2),
        out_specs=vmem(1)[0],
        out_shape=struct((rank, share), f32),
        compiler_params=params(),
        name="factor_gradient",
    )(*here, lows, pieces)


def shards(
    tokens,
    expert_choice_table,
    gate_weight,
    up_weight,
    down_weight,
    adapter_down_shared,
    adapter_gate_factor,
    router,
):
    tok_rows, width = tokens.shape
    n_dp = lax.axis_size("dp")
    groups = lax.axis_size("x")
    place = lax.axis_index("dp")
    group = lax.axis_index("x")
    core = lax.axis_index("core")
    col_rows = n_dp * tok_rows
    capacity = col_rows // groups
    half = groups * capacity
    wide = width // n_dp
    rank = adapter_down_shared.shape[1]
    devices = n_dp * groups * 2
    share = width // devices
    loss_factor = math.sqrt(groups / (tok_rows * devices))
    blocks = 8
    eight = n_dp == blocks

    here = (place.reshape(1), group.reshape(1), core.reshape(1))

    labels = expert_choice_table[0]
    index = jnp.arange(col_rows, dtype=jnp.int32)
    number = index
    if eight:
        order = lax.bitwise_xor(jnp.array(NEAR, jnp.int32), place)
        number = (order[:, None] * tok_rows + jnp.arange(tok_rows)[None, :]).reshape(col_rows)
        labels = jnp.sum(jnp.where(number[:, None] == index[None, :], labels[None, :], 0), axis=1)
    before = (labels[None, :] == labels[:, None]) & (number[None, :] < number[:, None])
    ordinal = jnp.sum(before.astype(jnp.int32), axis=1)
    ahead = lax.rem(labels - group + groups, groups)
    target = ahead * capacity + ordinal
    placer = (index[:, None] == target[None, :]).astype(bf16)
    tokens_near, factor, own_route = brought_near(tokens, adapter_down_shared.T, router.T, here)
    if eight:
        column, placer = gather_eight(tokens, placer)
        column[0] = tokens_near
        column, placer, factor, own_route = lax.optimization_barrier((column, placer, factor, own_route))
        own_target = target[:tok_rows]
    else:
        column = exchange(jnp.broadcast_to(tokens[None], (n_dp, tok_rows, width)), "dp")
        column = [column.reshape(col_rows, width)]
        own_target = lax.dynamic_slice_in_dim(target, place * tok_rows, tok_rows, 0)
    packed = pack(placer, column, capacity)
    parts = [packed[0]]
    for step in range(1, groups):
        route = [(i, (i + step) % groups) for i in range(groups)]
        parts.append(lax.ppermute(packed[step], "x", route))
    parts = parts + [swap(part, "core") for part in parts]

    low_parts = low_pieces(packed, factor, here, place, n_dp)
    low_parts = exchange(low_parts, every).reshape(n_dp, groups, 2, capacity // 2, 2 * rank)
    base, lifted, gate = lift(parts, gate_weight, up_weight, own_route)
    low_parts, gate = lax.optimization_barrier((low_parts, gate))
    own, other, slope, low, kept = down(
        base, lifted, low_parts, adapter_gate_factor, down_weight, blocks, here
    )

    rows = jnp.concatenate(parts, axis=0)
    numbers = jnp.broadcast_to(own_target.astype(bf16)[None], (2 * half, tok_rows))
    pieces = []
    for step in range(groups):
        to = lax.rem(group + step, groups)
        at = ((place * groups + to) * 2 + core) * share
        piece = jnp.concatenate([lax.dynamic_slice_in_dim(rows, at, share, 1), numbers], axis=1)
        route = [(i, (i + step) % groups) for i in range(groups)]
        pieces.append(lax.ppermute(piece, "x", route) if step else piece)
    pieces = jnp.stack(pieces)

    got = swap(other, "core")
    if eight:
        keep, far, near = fold_core(own, got, here)
        far, near = across(far, "dp", 1), across(near, "dp", 1)
        two, three = fold_near(keep, far, 2)
        mine, one = fold_near(keep, near, 0)
        terms = [mine, across(one, "dp", 2), across(two, "dp", 4), across(three, "dp", 6)]
        terms, pieces = lax.optimization_barrier((terms, pieces))
        (owns,) = gather_eight(mix(terms, gate))
    else:
        summed = (own.astype(f32) + got.astype(f32)).astype(bf16)
        summed = summed.transpose(1, 0, 2).reshape(half, n_dp, wide).transpose(1, 0, 2)
        summed = exchange(summed, "dp")
        mixed = mix([summed[i] for i in range(n_dp)], gate)
        mixed = exchange(jnp.broadcast_to(mixed[None], (n_dp, half, wide)), "dp")
        mixed = mixed.transpose(1, 0, 2).reshape(half, width)
        owns = [mixed[:, i * (width // blocks) : (i + 1) * (width // blocks)] for i in range(blocks)]
    others = [swap(block, "core") for block in owns]

    first = back_first(
        parts, owns[: blocks // 2], others[: blocks // 2], here, eight, gate, kept, loss_factor
    )
    back_low, back_pre = back_last(
        parts,
        owns[blocks // 2 :],
        others[blocks // 2 :],
        here,
        eight,
        gate,
        kept,
        first,
        slope,
        adapter_gate_factor,
        loss_factor,
        devices,
    )
    lows = exchange(back_low, every).reshape(n_dp, groups, 2, rank // 2, 4 * half)
    grad_b, *homes = rest(owns, here, eight, back_pre, low, capacity)

    result = jnp.zeros((tok_rows, width), f32)
    for step in range(groups):
        spot = index[step * capacity : (step + 1) * capacity]
        wanted = pieces[step, 0, share:].astype(jnp.int32)
        chooser = (wanted[:, None] == spot[None, :]).astype(bf16)
        chosen = dot(chooser, homes[step])
        if step:
            route = [(i, (i - step) % groups) for i in range(groups)]
            chosen = lax.ppermute(chosen.astype(bf16), "x", route).astype(f32)
        result = result + chosen

    grad_a = factor_gradient(lows, pieces, share, here)
    return (result.astype(bf16), grad_a.T, grad_b.T)


def solution(mesh):
    n_dp, n_expert = mesh.shape["dp"], mesh.shape["expert"]
    split = Mesh(mesh.devices.reshape(n_dp, n_expert // 2, 2), every)
    return jax.shard_map(
        shards,
        mesh=split,
        in_specs=(
            P(every, None),
            P(("x", "core"), None),
            P(None, every),
            P(None, every),
            P(every, None),
            P("dp", None),
            P(None, every),
            P(),
        ),
        out_specs=(P(every, None), P(every, None), P(every, None)),
        check_vma=False,
    )
```

```python
import functools
import math

import jax
import jax.numpy as jnp
from jax import lax
from jax.experimental import pallas as pl
from jax.experimental.pallas import tpu as pltpu
from jax.sharding import Mesh, PartitionSpec as P

adapter_scale = 0.25
bf16, f32 = jnp.bfloat16, jnp.float32
VMEM_LIMIT = 20 * 2**20
every = ("dp", "x", "core")
NEAR = (0, 2, 4, 6, 1, 3, 5, 7)


def swap(block, axis):
    return lax.ppermute(block, axis, [(0, 1), (1, 0)])


def across(block, axis, apart_by):
    count = lax.axis_size(axis)
    return lax.ppermute(block, axis, [(i, i ^ apart_by) for i in range(count)])


def gather_eight(block, *meanwhile):
    near = across(block, "dp", 1)
    far = [across(block, "dp", bits) for bits in NEAR[3:0:-1]][::-1]
    if meanwhile:
        far[0], meanwhile = lax.optimization_barrier((far[0], meanwhile))
    return [block, *far, near, *[across(other, "dp", 1) for other in far]], *meanwhile


def order_of(place, blocks, eight, first=0):
    return [lax.bitwise_xor(place, NEAR[k]) if eight else k for k in range(first, first + blocks)]


def exchange(blocks, axis):
    return lax.all_to_all(blocks, axis, 0, 0, tiled=True)


def dot(left, right):
    return jnp.dot(left, right, preferred_element_type=f32)


def dot_last(left, right):
    return lax.dot_general(left, right, (((1,), (1,)), ((), ())), preferred_element_type=f32)


def dot_first(left, right):
    return lax.dot_general(left, right, (((0,), (0,)), ((), ())), preferred_element_type=f32)


def sigmoid(v):
    return 1.0 / (1.0 + jnp.exp(-v))


def struct(shape, dtype):
    return jax.ShapeDtypeStruct(shape, dtype)


def vmem(count):
    return [pl.BlockSpec(memory_space=pltpu.VMEM)] * count


class Here:
    def __init__(self, refs):
        self.refs = refs

    def __getitem__(self, which):
        return self.refs[which][0]


def seated(kernel):
    def run(place_ref, group_ref, core_ref, *refs):
        kernel(Here((place_ref, group_ref, core_ref)), *refs)

    return run


def params():
    return pltpu.CompilerParams(vmem_limit_bytes=VMEM_LIMIT)


def cost(flops, moved):
    return pl.CostEstimate(flops=int(flops), bytes_accessed=int(moved), transcendentals=0)


def beside(rows):
    half = rows.shape[0] // 2
    return jnp.concatenate([rows[:half], rows[half:]], axis=1)


def apart(wide):
    rank = wide.shape[1] // 2
    return jnp.concatenate([wide[:, :rank], wide[:, rank:]], axis=0)


def near_kernel(here_ref, tokens_ref, factor_ref, router_ref, tokens_out, factor_out, route_out, router_near, sems):
    pairs = ((tokens_ref, tokens_out), (factor_ref, factor_out), (router_ref, router_near))
    copies = [pltpu.make_async_copy(*pair, sems.at[i]) for i, pair in enumerate(pairs)]
    for copy in copies:
        copy.start()
    for copy in copies:
        copy.wait()
    picked = lax.broadcasted_iota(jnp.int32, (router_near.shape[0], 1), 0) == here_ref[1]
    route_out[...] = jnp.sum(jnp.where(picked, router_near[...].astype(f32), 0.0), axis=0, keepdims=True)


def brought_near(tokens, factor, router, here):
    return pl.pallas_call(
        seated(near_kernel),
        in_specs=[pl.BlockSpec(memory_space=pltpu.SMEM)] * 3 + [pl.BlockSpec(memory_space=pl.ANY)] * 3,
        out_specs=vmem(3),
        out_shape=[
            struct(tokens.shape, bf16),
            struct(factor.shape, bf16),
            struct((1, router.shape[1]), f32),
        ],
        scratch_shapes=[pltpu.VMEM(router.shape, bf16), pltpu.SemaphoreType.DMA((3,))],
        compiler_params=params(),
        name="near",
    )(*here, *[pltpu.with_memory_space_constraint(array, pltpu.HBM) for array in (tokens, factor, router)])


def pack_kernel(n_blocks, placer_ref, *refs):
    blocks = refs[:n_blocks]
    outs = refs[n_blocks:]
    capacity, width = outs[0].shape
    chunk = width // 6
    for k in range(6):
        at = slice(k * chunk, (k + 1) * chunk)
        rows = jnp.concatenate([block[:, at] for block in blocks], axis=0)
        packed = dot(placer_ref[...], rows).astype(bf16)
        for step, out in enumerate(outs):
            out[:, at] = packed[step * capacity : (step + 1) * capacity]


def pack(placer, blocks, capacity):
    count, width = placer.shape[0], blocks[0].shape[1]
    return pl.pallas_call(
        functools.partial(pack_kernel, len(blocks)),
        in_specs=vmem(1 + len(blocks)),
        out_specs=vmem(count // capacity),
        out_shape=[struct((capacity, width), bf16)] * (count // capacity),
        compiler_params=params(),
        name="pack",
    )(placer, *blocks)


def low_kernel(n_parts, place_ref, *refs):
    parts, factor_ref, out_ref = refs[:n_parts], refs[n_parts], refs[n_parts + 1]
    depth = factor_ref.shape[1]
    if depth < parts[0].shape[1]:
        at = pl.ds(pl.multiple_of(place_ref[0] * depth, depth), depth)
    else:
        at = slice(None)
    capacity = parts[0].shape[0]
    rows = dot_last(jnp.concatenate([r[:, at] for r in parts], axis=0), factor_ref[...])
    for step in range(n_parts):
        piece = beside(rows[step * capacity : (step + 1) * capacity]).astype(bf16)
        group = lax.rem(place_ref[1] + step, n_parts)
        for i in range(out_ref.shape[0] // (2 * n_parts)):
            spot = (i * n_parts + group) * 2
            out_ref[spot] = piece
            out_ref[spot + 1] = piece


def low_pieces(parts, factor, here, place, n_dp):
    rank, depth = factor.shape
    capacity = parts[0].shape[0]
    if depth % 128:
        parts = [lax.dynamic_slice_in_dim(part, place * depth, depth, 1) for part in parts]
    return pl.pallas_call(
        seated(functools.partial(low_kernel, len(parts))),
        in_specs=[pl.BlockSpec(memory_space=pltpu.SMEM)] * 3 + vmem(len(parts) + 1),
        out_specs=vmem(1)[0],
        out_shape=struct((n_dp * len(parts) * 2, capacity // 2, 2 * rank), bf16),
        compiler_params=params(),
        name="low_pieces",
    )(*here, *parts, factor)


def lift_kernel(n_parts, *refs):
    parts = refs[:n_parts]
    weight_ref, up_ref, route_ref, pre_ref, lifted_ref, gate_ref, weight, up, sems = refs[n_parts:]
    width = parts[0].shape[1]
    steps = sems.shape[1]
    chunk = width // steps
    copies = []
    for k in range(steps):
        at = pl.ds(k * chunk, chunk)
        copies.append(
            (
                pltpu.make_async_copy(weight_ref.at[at], weight.at[at], sems.at[0, k]),
                pltpu.make_async_copy(up_ref.at[at], up.at[at], sems.at[1, k]),
            )
        )
    for pair in copies:
        pair[0].start()
        pair[1].start()
    pre = lifted = logit = 0.0
    for k in range(steps):
        at = slice(k * chunk, (k + 1) * chunk)
        copies[k][0].wait()
        copies[k][1].wait()
        rows = jnp.concatenate([r[:, at] for r in parts], axis=0)
        pre = pre + dot(rows, weight[at])
        lifted = lifted + dot(rows, up[at])
        logit = logit + jnp.sum(rows.astype(f32) * route_ref[:, at], axis=1, keepdims=True)
    pre_ref[...] = pre
    lifted_ref[...] = lifted
    gate_ref[...] = sigmoid(logit)


def lift(parts, gate_weight, up_weight, route):
    capacity, width = parts[0].shape
    units = gate_weight.shape[1]
    count = capacity * len(parts)
    return pl.pallas_call(
        functools.partial(lift_kernel, len(parts)),
        in_specs=vmem(len(parts))
        + [pl.BlockSpec(memory_space=pl.ANY)] * 2
        + vmem(1),
        out_specs=vmem(3),
        scratch_shapes=[
            pltpu.VMEM(gate_weight.shape, bf16),
            pltpu.VMEM(up_weight.shape, bf16),
            pltpu.SemaphoreType.DMA((2, 12)),
        ],
        out_shape=(
            struct((count, units), f32),
            struct((count, units), f32),
            struct((count, 1), f32),
        ),
        cost_estimate=cost(4 * count * width * units, 4 * width * units),
        compiler_params=params(),
        name="lift",
    )(
        *parts,
        pltpu.with_memory_space_constraint(gate_weight, pltpu.HBM),
        pltpu.with_memory_space_constraint(up_weight, pltpu.HBM),
        route,
    )


def bring(source, target, sems, starts):
    copies = []
    for k, start in enumerate(starts):
        at = pl.ds(start, target.shape[2])
        copies.append(pltpu.make_async_copy(source.at[:, at], target.at[k], sems.at[k]))
    for copy in copies:
        copy.start()
    return copies


def down_kernel(
    place_ref, base_ref, lifted_ref, low_ref, factor_ref, weight_ref, own_ref, other_ref, slope_ref, low_out, down_ref, sems
):
    blocks, half, wide = own_ref.shape
    copies = bring(weight_ref, down_ref, sems, [k * wide for k in range(blocks)])
    groups = low_ref.shape[1]
    sums = []
    for core in (place_ref[2], 1 - place_ref[2]):
        for step in range(groups):
            group = lax.rem(place_ref[1] - step + groups, groups)
            sums.append(apart(jnp.sum(low_ref[:, group, core].astype(f32), axis=0)))
    low = jnp.concatenate(sums, axis=0).astype(bf16)
    pre = base_ref[...] + adapter_scale * dot(low, factor_ref[...])
    low_out[...] = low
    lifted = lifted_ref[...]
    sig = sigmoid(pre)
    slope_ref[...] = (lifted * (sig * (1.0 + pre * (1.0 - sig)))).T
    hidden = (pre * sig * lifted).astype(bf16)
    for k in range(blocks):
        if k % 2 == 0:
            copies[k].wait()
            copies[k + 1].wait()
        partial = dot(hidden, down_ref[k]).astype(bf16)
        own_ref[k] = partial[:half]
        other_ref[k] = partial[half:]


def down(base, lifted, low_parts, factor, down_weight, blocks, here):
    count, units = base.shape
    half, width = count // 2, down_weight.shape[1]
    shape = struct((blocks, half, width // blocks), bf16)
    *outs, kept = pl.pallas_call(
        seated(down_kernel),
        in_specs=[pl.BlockSpec(memory_space=pltpu.SMEM)] * 3 + vmem(4) + [pl.BlockSpec(memory_space=pl.ANY)],
        out_specs=vmem(5),
        scratch_shapes=[pltpu.SemaphoreType.DMA((blocks,))],
        out_shape=(
            shape,
            shape,
            struct((units, count), f32),
            struct((count, factor.shape[0]), bf16),
            pltpu.VMEM((blocks, units, width // blocks), bf16),
        ),
        cost_estimate=cost(2 * count * width * units, 2 * width * units),
        compiler_params=params(),
        name="down",
    )(
        *here,
        base,
        lifted,
        low_parts,
        factor,
        pltpu.with_memory_space_constraint(down_weight, pltpu.HBM),
    )
    return *outs, pltpu.with_memory_space_constraint(kept, pltpu.VMEM)


def fold_core_kernel(place_ref, own_ref, got_ref, keep_ref, far_ref, near_ref):
    line, bit = place_ref[0] // 2, lax.rem(place_ref[0], 2)

    def folded(at):
        return (own_ref[at].astype(f32) + got_ref[at].astype(f32)).astype(bf16)

    for k in range(4):
        at = 2 * lax.bitwise_xor(line, k)
        keep_ref[k] = folded(at + bit)
        out_ref = near_ref if k < 2 else far_ref
        out_ref[k % 2] = folded(at + 1 - bit)


def fold_core(own, got, here):
    shapes = [struct((count, *own.shape[1:]), bf16) for count in (4, 2, 2)]
    return pl.pallas_call(
        seated(fold_core_kernel),
        in_specs=[pl.BlockSpec(memory_space=pltpu.SMEM)] * 3 + vmem(2),
        out_specs=vmem(3),
        out_shape=shapes,
        compiler_params=params(),
        name="fold_core",
    )(*here, own, got)


def fold_near_kernel(first, keep_ref, got_ref, *out_refs):
    for k, out_ref in enumerate(out_refs):
        out_ref[...] = (keep_ref[first + k].astype(f32) + got_ref[k].astype(f32)).astype(bf16)


def fold_near(keep, got, first):
    return pl.pallas_call(
        functools.partial(fold_near_kernel, first),
        in_specs=vmem(2),
        out_specs=vmem(2),
        out_shape=[struct(keep.shape[1:], bf16)] * 2,
        compiler_params=params(),
        name="fold_near",
    )(keep, got)


def mix_kernel(n_terms, *refs):
    gate_ref, out_ref = refs[n_terms:]
    total = refs[0][...].astype(f32)
    for term in refs[1:n_terms]:
        total = total + term[...].astype(f32)
    out_ref[...] = (gate_ref[: out_ref.shape[0]] * total).astype(bf16)


def mix(terms, gate):
    return pl.pallas_call(
        functools.partial(mix_kernel, len(terms)),
        in_specs=vmem(len(terms) + 1),
        out_specs=vmem(1)[0],
        out_shape=struct(terms[0].shape, bf16),
        compiler_params=params(),
        name="mix",
    )(*terms, gate)


def back_sum(parts, owns, others, order, gate_ref, down_ref, loss_factor):
    wide = owns[0].shape[1]
    scale = loss_factor * gate_ref[...]
    total = 0.0
    for block, own, other in zip(order, owns, others):
        start = block * wide
        at = pl.ds(start if isinstance(start, int) else pl.multiple_of(start, wide), wide)
        mixed = jnp.concatenate([own[...], other[...]], axis=0).astype(f32)
        rows = jnp.concatenate([r[:, at] for r in parts], axis=0).astype(f32)
        back = (scale * (mixed - rows)).astype(bf16)
        total = total + dot_last(down_ref[block], back)
    return total


def back_first_kernel(n_parts, n_blocks, eight, loss_factor, here_ref, *refs):
    parts, refs = refs[:n_parts], refs[n_parts:]
    owns, others, refs = refs[:n_blocks], refs[n_blocks : 2 * n_blocks], refs[2 * n_blocks :]
    gate_ref, down_ref, out_ref = refs
    order = order_of(here_ref[0], n_blocks, eight)
    out_ref[...] = back_sum(parts, owns, others, order, gate_ref, down_ref, loss_factor)


def back_last_kernel(n_parts, n_blocks, eight, loss_factor, here_ref, *refs):
    parts, refs = refs[:n_parts], refs[n_parts:]
    owns, others, refs = refs[:n_blocks], refs[n_blocks : 2 * n_blocks], refs[2 * n_blocks :]
    gate_ref, down_ref, first_ref, slope_ref, factor_ref, low_out, back_out = refs
    order = order_of(here_ref[0], n_blocks, eight, n_blocks)
    total = first_ref[...] + back_sum(parts, owns, others, order, gate_ref, down_ref, loss_factor)
    back_pre = (total * slope_ref[...]).astype(bf16)
    back_low = beside(adapter_scale * dot(factor_ref[...], back_pre)).astype(bf16)
    for i in range(low_out.shape[0]):
        low_out[i] = back_low
    back_out[...] = back_pre


def rest_kernel(n_blocks, eight, here_ref, *refs):
    owns, (back_ref, low_ref, grad_ref, *homes) = refs[:n_blocks], refs[n_blocks:]
    half, wide = owns[0].shape
    capacity = half // len(homes)
    grad_ref[...] = adapter_scale * lax.dot_general(
        low_ref[...], back_ref[...], (((0,), (1,)), ((), ())), preferred_element_type=f32
    )
    for block, own in zip(order_of(here_ref[0], n_blocks, eight), owns):
        start = block * wide
        at = pl.ds(start if isinstance(start, int) else pl.multiple_of(start, wide), wide)
        for step, home in enumerate(homes):
            home[:, at] = own[step * capacity : (step + 1) * capacity]


def rest(owns, here, eight, back_pre, low, capacity):
    half, wide = owns[0].shape
    homes = half // capacity
    return pl.pallas_call(
        seated(functools.partial(rest_kernel, len(owns), eight)),
        in_specs=[pl.BlockSpec(memory_space=pltpu.SMEM)] * 3 + vmem(len(owns) + 2),
        out_specs=vmem(1 + homes),
        out_shape=(
            struct((low.shape[1], back_pre.shape[0]), f32),
            *[struct((capacity, wide * len(owns)), bf16)] * homes,
        ),
        compiler_params=params(),
        name="rest",
    )(*here, *owns, back_pre, low)


def back_first(parts, owns, others, here, eight, gate, kept, loss_factor):
    units = kept.shape[1]
    count, blocks, wide = gate.shape[0], len(owns), owns[0].shape[1]
    return pl.pallas_call(
        seated(functools.partial(back_first_kernel, len(parts), blocks, eight, loss_factor)),
        in_specs=[pl.BlockSpec(memory_space=pltpu.SMEM)] * 3 + vmem(len(parts) + 2 * blocks + 2),
        out_specs=vmem(1)[0],
        out_shape=struct((units, count), f32),
        cost_estimate=cost(2 * count * blocks * wide * units, 2 * blocks * wide * units),
        compiler_params=params(),
        name="back_first",
    )(*here, *parts, *owns, *others, gate, kept)


def back_last(parts, owns, others, here, eight, gate, kept, first, slope, factor, loss_factor, copies):
    wide = owns[0].shape[1]
    units, count = slope.shape
    rank, blocks = factor.shape[0], len(others)
    return pl.pallas_call(
        seated(functools.partial(back_last_kernel, len(parts), blocks, eight, loss_factor)),
        in_specs=[pl.BlockSpec(memory_space=pltpu.SMEM)] * 3 + vmem(len(parts) + 2 * blocks + 5),
        out_specs=vmem(2),
        out_shape=(struct((copies, rank // 2, 2 * count), bf16), struct((units, count), bf16)),
        cost_estimate=cost(2 * count * blocks * wide * units, 2 * blocks * wide * units),
        compiler_params=params(),
        name="back_last",
    )(*here, *parts, *owns, *others, gate, kept, first, slope, factor)


def factor_kernel(place_ref, low_ref, piece_ref, out_ref):
    share = out_ref.shape[1]
    groups, count = piece_ref.shape[:2]
    half = count // 2
    group, core = place_ref[1], place_ref[2]
    lows, rows = [], []
    for step in range(groups):
        source = lax.rem(group - step + groups, groups)
        mine = apart(jnp.sum(low_ref[:, source, core].astype(f32), axis=0))
        theirs = apart(jnp.sum(low_ref[:, source, 1 - core].astype(f32), axis=0))
        lows.append(mine + jnp.concatenate([theirs[:, half:], theirs[:, :half]], axis=1))
        rows.append(piece_ref[step, :, :share])
    low = jnp.concatenate(lows, axis=1)
    high = low.astype(bf16)
    rest = (low - high.astype(f32)).astype(bf16)
    out_ref[...] = dot(jnp.concatenate([high, rest], axis=1), jnp.concatenate(rows + rows, axis=0))


def factor_gradient(lows, pieces, share, here):
    rank = 2 * lows.shape[3]
    return pl.pallas_call(
        seated(factor_kernel),
        in_specs=[pl.BlockSpec(memory_space=pltpu.SMEM)] * 3 + vmem(2),
        out_specs=vmem(1)[0],
        out_shape=struct((rank, share), f32),
        compiler_params=params(),
        name="factor_gradient",
    )(*here, lows, pieces)


def shards(
    tokens,
    expert_choice_table,
    gate_weight,
    up_weight,
    down_weight,
    adapter_down_shared,
    adapter_gate_factor,
    router,
):
    tok_rows, width = tokens.shape
    n_dp = lax.axis_size("dp")
    groups = lax.axis_size("x")
    place = lax.axis_index("dp")
    group = lax.axis_index("x")
    core = lax.axis_index("core")
    col_rows = n_dp * tok_rows
    capacity = col_rows // groups
    half = groups * capacity
    wide = width // n_dp
    rank = adapter_down_shared.shape[1]
    devices = n_dp * groups * 2
    share = width // devices
    loss_factor = math.sqrt(groups / (tok_rows * devices))
    blocks = 8
    eight = n_dp == blocks

    here = (place.reshape(1), group.reshape(1), core.reshape(1))

    labels = expert_choice_table[0]
    index = jnp.arange(col_rows, dtype=jnp.int32)
    number = index
    if eight:
        order = lax.bitwise_xor(jnp.array(NEAR, jnp.int32), place)
        number = (order[:, None] * tok_rows + jnp.arange(tok_rows)[None, :]).reshape(col_rows)
        labels = jnp.sum(jnp.where(number[:, None] == index[None, :], labels[None, :], 0), axis=1)
    before = (labels[None, :] == labels[:, None]) & (number[None, :] < number[:, None])
    ordinal = jnp.sum(before.astype(jnp.int32), axis=1)
    ahead = lax.rem(labels - group + groups, groups)
    target = ahead * capacity + ordinal
    placer = (index[:, None] == target[None, :]).astype(bf16)
    tokens_near, factor, own_route = brought_near(tokens, adapter_down_shared.T, router.T, here)
    if eight:
        column, placer = gather_eight(tokens, placer)
        column[0] = tokens_near
        column, placer, factor, own_route = lax.optimization_barrier((column, placer, factor, own_route))
        own_target = target[:tok_rows]
    else:
        column = exchange(jnp.broadcast_to(tokens[None], (n_dp, tok_rows, width)), "dp")
        column = [column.reshape(col_rows, width)]
        own_target = lax.dynamic_slice_in_dim(target, place * tok_rows, tok_rows, 0)
    packed = pack(placer, column, capacity)
    low_parts = low_pieces(packed, factor, here, place, n_dp)
    packed, low_parts = lax.optimization_barrier((packed, low_parts))
    parts = [packed[0]]
    for step in range(1, groups):
        route = [(i, (i + step) % groups) for i in range(groups)]
        parts.append(lax.ppermute(packed[step], "x", route))
    parts = parts + [swap(part, "core") for part in parts]

    low_parts = exchange(low_parts, every).reshape(n_dp, groups, 2, capacity // 2, 2 * rank)
    base, lifted, gate = lift(parts, gate_weight, up_weight, own_route)
    low_parts, gate = lax.optimization_barrier((low_parts, gate))
    own, other, slope, low, kept = down(
        base, lifted, low_parts, adapter_gate_factor, down_weight, blocks, here
    )

    rows = jnp.concatenate(parts, axis=0)
    numbers = jnp.broadcast_to(own_target.astype(bf16)[None], (2 * half, tok_rows))
    pieces = []
    for step in range(groups):
        to = lax.rem(group + step, groups)
        at = ((place * groups + to) * 2 + core) * share
        piece = jnp.concatenate([lax.dynamic_slice_in_dim(rows, at, share, 1), numbers], axis=1)
        route = [(i, (i + step) % groups) for i in range(groups)]
        pieces.append(lax.ppermute(piece, "x", route) if step else piece)
    pieces = jnp.stack(pieces)

    got = swap(other, "core")
    if eight:
        keep, far, near = fold_core(own, got, here)
        far, near, pieces = lax.optimization_barrier((across(far, "dp", 1), near, pieces))
        near = across(near, "dp", 1)
        two, three = fold_near(keep, far, 2)
        mine, one = fold_near(keep, near, 0)
        terms = [mine, across(one, "dp", 2), across(two, "dp", 4), across(three, "dp", 6)]
        (owns,) = gather_eight(mix(terms, gate))
    else:
        summed = (own.astype(f32) + got.astype(f32)).astype(bf16)
        summed = summed.transpose(1, 0, 2).reshape(half, n_dp, wide).transpose(1, 0, 2)
        summed = exchange(summed, "dp")
        mixed = mix([summed[i] for i in range(n_dp)], gate)
        mixed = exchange(jnp.broadcast_to(mixed[None], (n_dp, half, wide)), "dp")
        mixed = mixed.transpose(1, 0, 2).reshape(half, width)
        owns = [mixed[:, i * (width // blocks) : (i + 1) * (width // blocks)] for i in range(blocks)]
    others = [swap(block, "core") for block in owns]

    first = back_first(
        parts, owns[: blocks // 2], others[: blocks // 2], here, eight, gate, kept, loss_factor
    )
    back_low, back_pre = back_last(
        parts,
        owns[blocks // 2 :],
        others[blocks // 2 :],
        here,
        eight,
        gate,
        kept,
        first,
        slope,
        adapter_gate_factor,
        loss_factor,
        devices,
    )
    lows = exchange(back_low, every).reshape(n_dp, groups, 2, rank // 2, 4 * half)
    grad_b, *homes = rest(owns, here, eight, back_pre, low, capacity)

    result = jnp.zeros((tok_rows, width), f32)
    for step in range(groups):
        spot = index[step * capacity : (step + 1) * capacity]
        wanted = pieces[step, 0, share:].astype(jnp.int32)
        chooser = (wanted[:, None] == spot[None, :]).astype(bf16)
        chosen = dot(chooser, homes[step])
        if step:
            route = [(i, (i - step) % groups) for i in range(groups)]
            chosen = lax.ppermute(chosen.astype(bf16), "x", route).astype(f32)
        result = result + chosen

    grad_a = factor_gradient(lows, pieces, share, here)
    return (result.astype(bf16), grad_a.T, grad_b.T)


def solution(mesh):
    n_dp, n_expert = mesh.shape["dp"], mesh.shape["expert"]
    split = Mesh(mesh.devices.reshape(n_dp, n_expert // 2, 2), every)
    return jax.shard_map(
        shards,
        mesh=split,
        in_specs=(
            P(every, None),
            P(("x", "core"), None),
            P(None, every),
            P(None, every),
            P(every, None),
            P("dp", None),
            P(None, every),
            P(),
        ),
        out_specs=(P(every, None), P(every, None), P(every, None)),
        check_vma=False,
    )
```

```python
import functools
import math

import jax
import jax.numpy as jnp
from jax import lax
from jax.experimental import pallas as pl
from jax.experimental.pallas import tpu as pltpu
from jax.sharding import Mesh, PartitionSpec as P

adapter_scale = 0.25
bf16, f32 = jnp.bfloat16, jnp.float32
VMEM_LIMIT = 20 * 2**20
every = ("dp", "x", "core")
NEAR = (0, 2, 4, 6, 1, 3, 5, 7)


def swap(block, axis):
    return lax.ppermute(block, axis, [(0, 1), (1, 0)])


def across(block, axis, apart_by):
    count = lax.axis_size(axis)
    return lax.ppermute(block, axis, [(i, i ^ apart_by) for i in range(count)])


def gather_eight(block, *meanwhile):
    near = across(block, "dp", 1)
    far = [across(block, "dp", bits) for bits in NEAR[3:0:-1]][::-1]
    if meanwhile:
        far[0], meanwhile = lax.optimization_barrier((far[0], meanwhile))
    return [block, *far, near, *[across(other, "dp", 1) for other in far]], *meanwhile


def gather_pairs(block):
    near = across(block, "dp", 1)
    line = stack_three([across(block, "dp", bits) for bits in NEAR[3:0:-1]][::-1])
    return (block, line), (near, across(line, "dp", 1))


def views(single, line):
    return [single, *[line.at[k] for k in range(line.shape[0])]]


def order_of(place, blocks, eight, first=0):
    return [lax.bitwise_xor(place, NEAR[k]) if eight else k for k in range(first, first + blocks)]


def exchange(blocks, axis):
    return lax.all_to_all(blocks, axis, 0, 0, tiled=True)


def dot(left, right):
    return jnp.dot(left, right, preferred_element_type=f32)


def dot_last(left, right):
    return lax.dot_general(left, right, (((1,), (1,)), ((), ())), preferred_element_type=f32)


def dot_first(left, right):
    return lax.dot_general(left, right, (((0,), (0,)), ((), ())), preferred_element_type=f32)


def sigmoid(v):
    return 1.0 / (1.0 + jnp.exp(-v))


def struct(shape, dtype):
    return jax.ShapeDtypeStruct(shape, dtype)


def vmem(count):
    return [pl.BlockSpec(memory_space=pltpu.VMEM)] * count


class Here:
    def __init__(self, refs):
        self.refs = refs

    def __getitem__(self, which):
        return self.refs[which][0]


def seated(kernel):
    def run(place_ref, group_ref, core_ref, *refs):
        kernel(Here((place_ref, group_ref, core_ref)), *refs)

    return run


def params():
    return pltpu.CompilerParams(vmem_limit_bytes=VMEM_LIMIT)


def cost(flops, moved):
    return pl.CostEstimate(flops=int(flops), bytes_accessed=int(moved), transcendentals=0)


def beside(rows):
    half = rows.shape[0] // 2
    return jnp.concatenate([rows[:half], rows[half:]], axis=1)


def apart(wide):
    rank = wide.shape[1] // 2
    return jnp.concatenate([wide[:, :rank], wide[:, rank:]], axis=0)


def near_kernel(here_ref, tokens_ref, factor_ref, router_ref, tokens_out, factor_out, route_out, router_near, sems):
    pairs = ((tokens_ref, tokens_out), (factor_ref, factor_out), (router_ref, router_near))
    copies = [pltpu.make_async_copy(*pair, sems.at[i]) for i, pair in enumerate(pairs)]
    for copy in copies:
        copy.start()
    for copy in copies:
        copy.wait()
    picked = lax.broadcasted_iota(jnp.int32, (router_near.shape[0], 1), 0) == here_ref[1]
    route_out[...] = jnp.sum(jnp.where(picked, router_near[...].astype(f32), 0.0), axis=0, keepdims=True)


def brought_near(tokens, factor, router, here):
    return pl.pallas_call(
        seated(near_kernel),
        in_specs=[pl.BlockSpec(memory_space=pltpu.SMEM)] * 3 + [pl.BlockSpec(memory_space=pl.ANY)] * 3,
        out_specs=vmem(3),
        out_shape=[
            struct(tokens.shape, bf16),
            struct(factor.shape, bf16),
            struct((1, router.shape[1]), f32),
        ],
        scratch_shapes=[pltpu.VMEM(router.shape, bf16), pltpu.SemaphoreType.DMA((3,))],
        compiler_params=params(),
        name="near",
    )(*here, *[pltpu.with_memory_space_constraint(array, pltpu.HBM) for array in (tokens, factor, router)])


def pack_kernel(n_blocks, placer_ref, *refs):
    blocks = refs[:n_blocks]
    outs = refs[n_blocks:]
    capacity, width = outs[0].shape
    chunk = width // 6
    for k in range(6):
        at = slice(k * chunk, (k + 1) * chunk)
        rows = jnp.concatenate([block[:, at] for block in blocks], axis=0)
        packed = dot(placer_ref[...], rows).astype(bf16)
        for step, out in enumerate(outs):
            out[:, at] = packed[step * capacity : (step + 1) * capacity]


def pack(placer, blocks, capacity):
    count, width = placer.shape[0], blocks[0].shape[1]
    return pl.pallas_call(
        functools.partial(pack_kernel, len(blocks)),
        in_specs=vmem(1 + len(blocks)),
        out_specs=vmem(count // capacity),
        out_shape=[struct((capacity, width), bf16)] * (count // capacity),
        compiler_params=params(),
        name="pack",
    )(placer, *blocks)


def low_kernel(n_parts, place_ref, *refs):
    parts, factor_ref, out_ref = refs[:n_parts], refs[n_parts], refs[n_parts + 1]
    depth = factor_ref.shape[1]
    if depth < parts[0].shape[1]:
        at = pl.ds(pl.multiple_of(place_ref[0] * depth, depth), depth)
    else:
        at = slice(None)
    capacity = parts[0].shape[0]
    rows = dot_last(jnp.concatenate([r[:, at] for r in parts], axis=0), factor_ref[...])
    for step in range(n_parts):
        piece = beside(rows[step * capacity : (step + 1) * capacity]).astype(bf16)
        group = lax.rem(place_ref[1] + step, n_parts)
        for i in range(out_ref.shape[0] // (2 * n_parts)):
            spot = (i * n_parts + group) * 2
            out_ref[spot] = piece
            out_ref[spot + 1] = piece


def low_pieces(parts, factor, here, place, n_dp):
    rank, depth = factor.shape
    capacity = parts[0].shape[0]
    if depth % 128:
        parts = [lax.dynamic_slice_in_dim(part, place * depth, depth, 1) for part in parts]
    return pl.pallas_call(
        seated(functools.partial(low_kernel, len(parts))),
        in_specs=[pl.BlockSpec(memory_space=pltpu.SMEM)] * 3 + vmem(len(parts) + 1),
        out_specs=vmem(1)[0],
        out_shape=struct((n_dp * len(parts) * 2, capacity // 2, 2 * rank), bf16),
        compiler_params=params(),
        name="low_pieces",
    )(*here, *parts, factor)


def lift_kernel(n_parts, *refs):
    parts = refs[:n_parts]
    weight_ref, up_ref, route_ref, pre_ref, lifted_ref, gate_ref, weight, up, sems = refs[n_parts:]
    width = parts[0].shape[1]
    steps = sems.shape[1]
    chunk = width // steps
    copies = []
    for k in range(steps):
        at = pl.ds(k * chunk, chunk)
        copies.append(
            (
                pltpu.make_async_copy(weight_ref.at[at], weight.at[at], sems.at[0, k]),
                pltpu.make_async_copy(up_ref.at[at], up.at[at], sems.at[1, k]),
            )
        )
    for pair in copies:
        pair[0].start()
        pair[1].start()
    pre = lifted = logit = 0.0
    for k in range(steps):
        at = slice(k * chunk, (k + 1) * chunk)
        copies[k][0].wait()
        copies[k][1].wait()
        rows = jnp.concatenate([r[:, at] for r in parts], axis=0)
        pre = pre + dot(rows, weight[at])
        lifted = lifted + dot(rows, up[at])
        logit = logit + jnp.sum(rows.astype(f32) * route_ref[:, at], axis=1, keepdims=True)
    pre_ref[...] = pre
    lifted_ref[...] = lifted
    gate_ref[...] = sigmoid(logit)


def lift(parts, gate_weight, up_weight, route):
    capacity, width = parts[0].shape
    units = gate_weight.shape[1]
    count = capacity * len(parts)
    return pl.pallas_call(
        functools.partial(lift_kernel, len(parts)),
        in_specs=vmem(len(parts))
        + [pl.BlockSpec(memory_space=pl.ANY)] * 2
        + vmem(1),
        out_specs=vmem(3),
        scratch_shapes=[
            pltpu.VMEM(gate_weight.shape, bf16),
            pltpu.VMEM(up_weight.shape, bf16),
            pltpu.SemaphoreType.DMA((2, 12)),
        ],
        out_shape=(
            struct((count, units), f32),
            struct((count, units), f32),
            struct((count, 1), f32),
        ),
        cost_estimate=cost(4 * count * width * units, 4 * width * units),
        compiler_params=params(),
        name="lift",
    )(
        *parts,
        pltpu.with_memory_space_constraint(gate_weight, pltpu.HBM),
        pltpu.with_memory_space_constraint(up_weight, pltpu.HBM),
        route,
    )


def bring(source, target, sems, starts):
    copies = []
    for k, start in enumerate(starts):
        at = pl.ds(start, target.shape[2])
        copies.append(pltpu.make_async_copy(source.at[:, at], target.at[k], sems.at[k]))
    for copy in copies:
        copy.start()
    return copies


def down_kernel(
    place_ref, base_ref, lifted_ref, low_ref, factor_ref, weight_ref, own_ref, other_ref, slope_ref, low_out, down_ref, sems
):
    blocks, half, wide = own_ref.shape
    copies = bring(weight_ref, down_ref, sems, [k * wide for k in range(blocks)])
    groups = low_ref.shape[1]
    sums = []
    for core in (place_ref[2], 1 - place_ref[2]):
        for step in range(groups):
            group = lax.rem(place_ref[1] - step + groups, groups)
            sums.append(apart(jnp.sum(low_ref[:, group, core].astype(f32), axis=0)))
    low = jnp.concatenate(sums, axis=0).astype(bf16)
    pre = base_ref[...] + adapter_scale * dot(low, factor_ref[...])
    low_out[...] = low
    lifted = lifted_ref[...]
    sig = sigmoid(pre)
    slope_ref[...] = (lifted * (sig * (1.0 + pre * (1.0 - sig)))).T
    hidden = (pre * sig * lifted).astype(bf16)
    for k in range(blocks):
        if k % 2 == 0:
            copies[k].wait()
            copies[k + 1].wait()
        partial = dot(hidden, down_ref[k]).astype(bf16)
        own_ref[k] = partial[:half]
        other_ref[k] = partial[half:]


def down(base, lifted, low_parts, factor, down_weight, blocks, here):
    count, units = base.shape
    half, width = count // 2, down_weight.shape[1]
    shape = struct((blocks, half, width // blocks), bf16)
    *outs, kept = pl.pallas_call(
        seated(down_kernel),
        in_specs=[pl.BlockSpec(memory_space=pltpu.SMEM)] * 3 + vmem(4) + [pl.BlockSpec(memory_space=pl.ANY)],
        out_specs=vmem(5),
        scratch_shapes=[pltpu.SemaphoreType.DMA((blocks,))],
        out_shape=(
            shape,
            shape,
            struct((units, count), f32),
            struct((count, factor.shape[0]), bf16),
            pltpu.VMEM((blocks, units, width // blocks), bf16),
        ),
        cost_estimate=cost(2 * count * width * units, 2 * width * units),
        compiler_params=params(),
        name="down",
    )(
        *here,
        base,
        lifted,
        low_parts,
        factor,
        pltpu.with_memory_space_constraint(down_weight, pltpu.HBM),
    )
    return *outs, pltpu.with_memory_space_constraint(kept, pltpu.VMEM)


def fold_core_kernel(place_ref, own_ref, got_ref, keep_ref, far_ref, near_ref):
    line, bit = place_ref[0] // 2, lax.rem(place_ref[0], 2)

    def folded(at):
        return (own_ref[at].astype(f32) + got_ref[at].astype(f32)).astype(bf16)

    for k in range(4):
        at = 2 * lax.bitwise_xor(line, k)
        keep_ref[k] = folded(at + bit)
        out_ref = near_ref if k < 2 else far_ref
        out_ref[k % 2] = folded(at + 1 - bit)


def fold_core(own, got, here):
    shapes = [struct((count, *own.shape[1:]), bf16) for count in (4, 2, 2)]
    return pl.pallas_call(
        seated(fold_core_kernel),
        in_specs=[pl.BlockSpec(memory_space=pltpu.SMEM)] * 3 + vmem(2),
        out_specs=vmem(3),
        out_shape=shapes,
        compiler_params=params(),
        name="fold_core",
    )(*here, own, got)


def fold_near_kernel(first, keep_ref, got_ref, *out_refs):
    for k, out_ref in enumerate(out_refs):
        out_ref[...] = (keep_ref[first + k].astype(f32) + got_ref[k].astype(f32)).astype(bf16)


def fold_near(keep, got, first):
    return pl.pallas_call(
        functools.partial(fold_near_kernel, first),
        in_specs=vmem(2),
        out_specs=vmem(2),
        out_shape=[struct(keep.shape[1:], bf16)] * 2,
        compiler_params=params(),
        name="fold_near",
    )(keep, got)


def stack_kernel(*refs):
    for k, ref in enumerate(refs[:-1]):
        refs[-1][k] = ref[...]


def stack_three(arrays):
    return pl.pallas_call(
        stack_kernel,
        in_specs=vmem(len(arrays)),
        out_specs=vmem(1)[0],
        out_shape=struct((len(arrays), *arrays[0].shape), bf16),
        compiler_params=params(),
        name="stack",
    )(*arrays)


def mix_kernel(n_terms, *refs):
    gate_ref, out_ref = refs[n_terms:]
    total = refs[0][...].astype(f32)
    for term in refs[1:n_terms]:
        total = total + term[...].astype(f32)
    out_ref[...] = (gate_ref[: out_ref.shape[0]] * total).astype(bf16)


def mix(terms, gate):
    return pl.pallas_call(
        functools.partial(mix_kernel, len(terms)),
        in_specs=vmem(len(terms) + 1),
        out_specs=vmem(1)[0],
        out_shape=struct(terms[0].shape, bf16),
        compiler_params=params(),
        name="mix",
    )(*terms, gate)


def back_sum(parts, owns, others, order, gate_ref, down_ref, loss_factor):
    wide = owns[0].shape[1]
    scale = loss_factor * gate_ref[...]
    total = 0.0
    for block, own, other in zip(order, owns, others):
        start = block * wide
        at = pl.ds(start if isinstance(start, int) else pl.multiple_of(start, wide), wide)
        mixed = jnp.concatenate([own[...], other[...]], axis=0).astype(f32)
        rows = jnp.concatenate([r[:, at] for r in parts], axis=0).astype(f32)
        back = (scale * (mixed - rows)).astype(bf16)
        total = total + dot_last(down_ref[block], back)
    return total


def back_first_kernel(n_parts, n_blocks, eight, loss_factor, here_ref, *refs):
    parts, refs = refs[:n_parts], refs[n_parts:]
    owns, others, refs = views(*refs[:2]), views(*refs[2:4]), refs[4:]
    gate_ref, down_ref, out_ref = refs
    order = order_of(here_ref[0], n_blocks, eight)
    out_ref[...] = back_sum(parts, owns, others, order, gate_ref, down_ref, loss_factor)


def back_last_kernel(n_parts, n_blocks, eight, loss_factor, here_ref, *refs):
    parts, refs = refs[:n_parts], refs[n_parts:]
    owns, others, refs = views(*refs[:2]), views(*refs[2:4]), refs[4:]
    gate_ref, down_ref, first_ref, slope_ref, factor_ref, low_out, back_out = refs
    order = order_of(here_ref[0], n_blocks, eight, n_blocks)
    total = first_ref[...] + back_sum(parts, owns, others, order, gate_ref, down_ref, loss_factor)
    back_pre = (total * slope_ref[...]).astype(bf16)
    back_low = beside(adapter_scale * dot(factor_ref[...], back_pre)).astype(bf16)
    for i in range(low_out.shape[0]):
        low_out[i] = back_low
    back_out[...] = back_pre


def rest_kernel(n_blocks, eight, here_ref, *refs):
    owns = views(*refs[:2]) + views(*refs[2:4])
    back_ref, low_ref, grad_ref, *homes = refs[4:]
    half, wide = owns[0].shape
    capacity = half // len(homes)
    grad_ref[...] = adapter_scale * lax.dot_general(
        low_ref[...], back_ref[...], (((0,), (1,)), ((), ())), preferred_element_type=f32
    )
    for block, own in zip(order_of(here_ref[0], n_blocks, eight), owns):
        start = block * wide
        at = pl.ds(start if isinstance(start, int) else pl.multiple_of(start, wide), wide)
        for step, home in enumerate(homes):
            home[:, at] = own[step * capacity : (step + 1) * capacity]


def rest(owns, here, eight, back_pre, low, capacity):
    half, wide = owns[0].shape
    homes, blocks = half // capacity, 2 * (1 + owns[1].shape[0])
    return pl.pallas_call(
        seated(functools.partial(rest_kernel, blocks, eight)),
        in_specs=[pl.BlockSpec(memory_space=pltpu.SMEM)] * 3 + vmem(len(owns) + 2),
        out_specs=vmem(1 + homes),
        out_shape=(
            struct((low.shape[1], back_pre.shape[0]), f32),
            *[struct((capacity, wide * blocks), bf16)] * homes,
        ),
        compiler_params=params(),
        name="rest",
    )(*here, *owns, back_pre, low)


def back_first(parts, owns, others, here, eight, gate, kept, loss_factor):
    units = kept.shape[1]
    count, blocks, wide = gate.shape[0], 1 + owns[1].shape[0], owns[0].shape[1]
    return pl.pallas_call(
        seated(functools.partial(back_first_kernel, len(parts), blocks, eight, loss_factor)),
        in_specs=[pl.BlockSpec(memory_space=pltpu.SMEM)] * 3 + vmem(len(parts) + 6),
        out_specs=vmem(1)[0],
        out_shape=struct((units, count), f32),
        cost_estimate=cost(2 * count * blocks * wide * units, 2 * blocks * wide * units),
        compiler_params=params(),
        name="back_first",
    )(*here, *parts, *owns, *others, gate, kept)


def back_last(parts, owns, others, here, eight, gate, kept, first, slope, factor, loss_factor, copies):
    wide = owns[0].shape[1]
    units, count = slope.shape
    rank, blocks = factor.shape[0], 1 + others[1].shape[0]
    return pl.pallas_call(
        seated(functools.partial(back_last_kernel, len(parts), blocks, eight, loss_factor)),
        in_specs=[pl.BlockSpec(memory_space=pltpu.SMEM)] * 3 + vmem(len(parts) + 9),
        out_specs=vmem(2),
        out_shape=(struct((copies, rank // 2, 2 * count), bf16), struct((units, count), bf16)),
        cost_estimate=cost(2 * count * blocks * wide * units, 2 * blocks * wide * units),
        compiler_params=params(),
        name="back_last",
    )(*here, *parts, *owns, *others, gate, kept, first, slope, factor)


def factor_kernel(place_ref, low_ref, piece_ref, out_ref):
    share = out_ref.shape[1]
    groups, count = piece_ref.shape[:2]
    half = count // 2
    group, core = place_ref[1], place_ref[2]
    lows, rows = [], []
    for step in range(groups):
        source = lax.rem(group - step + groups, groups)
        mine = apart(jnp.sum(low_ref[:, source, core].astype(f32), axis=0))
        theirs = apart(jnp.sum(low_ref[:, source, 1 - core].astype(f32), axis=0))
        lows.append(mine + jnp.concatenate([theirs[:, half:], theirs[:, :half]], axis=1))
        rows.append(piece_ref[step, :, :share])
    low = jnp.concatenate(lows, axis=1)
    high = low.astype(bf16)
    rest = (low - high.astype(f32)).astype(bf16)
    out_ref[...] = dot(jnp.concatenate([high, rest], axis=1), jnp.concatenate(rows + rows, axis=0))


def factor_gradient(lows, pieces, share, here):
    rank = 2 * lows.shape[3]
    return pl.pallas_call(
        seated(factor_kernel),
        in_specs=[pl.BlockSpec(memory_space=pltpu.SMEM)] * 3 + vmem(2),
        out_specs=vmem(1)[0],
        out_shape=struct((rank, share), f32),
        compiler_params=params(),
        name="factor_gradient",
    )(*here, lows, pieces)


def shards(
    tokens,
    expert_choice_table,
    gate_weight,
    up_weight,
    down_weight,
    adapter_down_shared,
    adapter_gate_factor,
    router,
):
    tok_rows, width = tokens.shape
    n_dp = lax.axis_size("dp")
    groups = lax.axis_size("x")
    place = lax.axis_index("dp")
    group = lax.axis_index("x")
    core = lax.axis_index("core")
    col_rows = n_dp * tok_rows
    capacity = col_rows // groups
    half = groups * capacity
    wide = width // n_dp
    rank = adapter_down_shared.shape[1]
    devices = n_dp * groups * 2
    share = width // devices
    loss_factor = math.sqrt(groups / (tok_rows * devices))
    blocks = 8
    eight = n_dp == blocks

    here = (place.reshape(1), group.reshape(1), core.reshape(1))

    labels = expert_choice_table[0]
    index = jnp.arange(col_rows, dtype=jnp.int32)
    number = index
    if eight:
        order = lax.bitwise_xor(jnp.array(NEAR, jnp.int32), place)
        number = (order[:, None] * tok_rows + jnp.arange(tok_rows)[None, :]).reshape(col_rows)
        labels = jnp.sum(jnp.where(number[:, None] == index[None, :], labels[None, :], 0), axis=1)
    before = (labels[None, :] == labels[:, None]) & (number[None, :] < number[:, None])
    ordinal = jnp.sum(before.astype(jnp.int32), axis=1)
    ahead = lax.rem(labels - group + groups, groups)
    target = ahead * capacity + ordinal
    placer = (index[:, None] == target[None, :]).astype(bf16)
    tokens_near, factor, own_route = brought_near(tokens, adapter_down_shared.T, router.T, here)
    if eight:
        column, placer = gather_eight(tokens, placer)
        column[0] = tokens_near
        column, placer, factor, own_route = lax.optimization_barrier((column, placer, factor, own_route))
        own_target = target[:tok_rows]
    else:
        column = exchange(jnp.broadcast_to(tokens[None], (n_dp, tok_rows, width)), "dp")
        column = [column.reshape(col_rows, width)]
        own_target = lax.dynamic_slice_in_dim(target, place * tok_rows, tok_rows, 0)
    packed = pack(placer, column, capacity)
    low_parts = low_pieces(packed, factor, here, place, n_dp)
    packed, low_parts = lax.optimization_barrier((packed, low_parts))
    parts = [packed[0]]
    for step in range(1, groups):
        route = [(i, (i + step) % groups) for i in range(groups)]
        parts.append(lax.ppermute(packed[step], "x", route))
    parts = parts + [swap(part, "core") for part in parts]

    low_parts = exchange(low_parts, every).reshape(n_dp, groups, 2, capacity // 2, 2 * rank)
    base, lifted, gate = lift(parts, gate_weight, up_weight, own_route)
    low_parts, gate = lax.optimization_barrier((low_parts, gate))
    own, other, slope, low, kept = down(
        base, lifted, low_parts, adapter_gate_factor, down_weight, blocks, here
    )

    rows = jnp.concatenate(parts, axis=0)
    numbers = jnp.broadcast_to(own_target.astype(bf16)[None], (2 * half, tok_rows))
    pieces = []
    for step in range(groups):
        to = lax.rem(group + step, groups)
        at = ((place * groups + to) * 2 + core) * share
        piece = jnp.concatenate([lax.dynamic_slice_in_dim(rows, at, share, 1), numbers], axis=1)
        route = [(i, (i + step) % groups) for i in range(groups)]
        pieces.append(lax.ppermute(piece, "x", route) if step else piece)
    pieces = jnp.stack(pieces)

    got = swap(other, "core")
    if eight:
        keep, far, near = fold_core(own, got, here)
        far, near, pieces = lax.optimization_barrier((across(far, "dp", 1), near, pieces))
        near = across(near, "dp", 1)
        two, three = fold_near(keep, far, 2)
        mine, one = fold_near(keep, near, 0)
        terms = [mine, across(one, "dp", 2), across(two, "dp", 4), across(three, "dp", 6)]
        owns = gather_pairs(mix(terms, gate))
    else:
        summed = (own.astype(f32) + got.astype(f32)).astype(bf16)
        summed = summed.transpose(1, 0, 2).reshape(half, n_dp, wide).transpose(1, 0, 2)
        summed = exchange(summed, "dp")
        mixed = mix([summed[i] for i in range(n_dp)], gate)
        mixed = exchange(jnp.broadcast_to(mixed[None], (n_dp, half, wide)), "dp")
        mixed = mixed.transpose(1, 0, 2).reshape(half, width)
        owns = [mixed[:, i * (width // blocks) : (i + 1) * (width // blocks)] for i in range(blocks)]
        owns = [(owns[k], jnp.stack(owns[k + 1 : k + blocks // 2])) for k in (0, blocks // 2)]
    others = [[swap(block, "core") for block in pair] for pair in owns]

    first = back_first(
        parts, owns[0], others[0], here, eight, gate, kept, loss_factor
    )
    back_low, back_pre = back_last(
        parts,
        owns[1],
        others[1],
        here,
        eight,
        gate,
        kept,
        first,
        slope,
        adapter_gate_factor,
        loss_factor,
        devices,
    )
    lows = exchange(back_low, every).reshape(n_dp, groups, 2, rank // 2, 4 * half)
    grad_b, *homes = rest([*owns[0], *owns[1]], here, eight, back_pre, low, capacity)

    result = jnp.zeros((tok_rows, width), f32)
    for step in range(groups):
        spot = index[step * capacity : (step + 1) * capacity]
        wanted = pieces[step, 0, share:].astype(jnp.int32)
        chooser = (wanted[:, None] == spot[None, :]).astype(bf16)
        chosen = dot(chooser, homes[step])
        if step:
            route = [(i, (i - step) % groups) for i in range(groups)]
            chosen = lax.ppermute(chosen.astype(bf16), "x", route).astype(f32)
        result = result + chosen

    grad_a = factor_gradient(lows, pieces, share, here)
    return (result.astype(bf16), grad_a.T, grad_b.T)


def solution(mesh):
    n_dp, n_expert = mesh.shape["dp"], mesh.shape["expert"]
    split = Mesh(mesh.devices.reshape(n_dp, n_expert // 2, 2), every)
    return jax.shard_map(
        shards,
        mesh=split,
        in_specs=(
            P(every, None),
            P(("x", "core"), None),
            P(None, every),
            P(None, every),
            P(every, None),
            P("dp", None),
            P(None, every),
            P(),
        ),
        out_specs=(P(every, None), P(every, None), P(every, None)),
        check_vma=False,
    )
```

```python
import functools
import math

import jax
import jax.numpy as jnp
from jax import lax
from jax.experimental import pallas as pl
from jax.experimental.pallas import tpu as pltpu
from jax.sharding import Mesh, PartitionSpec as P

adapter_scale = 0.25
bf16, f32 = jnp.bfloat16, jnp.float32
VMEM_LIMIT = 20 * 2**20
every = ("dp", "x", "core")
NEAR = (0, 2, 4, 6, 1, 3, 5, 7)


def swap(block, axis):
    return lax.ppermute(block, axis, [(0, 1), (1, 0)])


def across(block, axis, apart_by):
    count = lax.axis_size(axis)
    return lax.ppermute(block, axis, [(i, i ^ apart_by) for i in range(count)])


def gather_eight(block, *meanwhile):
    near = across(block, "dp", 1)
    far = [across(block, "dp", bits) for bits in NEAR[3:0:-1]][::-1]
    if meanwhile:
        far[0], meanwhile = lax.optimization_barrier((far[0], meanwhile))
    return [block, *far, near, *[across(other, "dp", 1) for other in far]], *meanwhile


def gather_pairs(block):
    near = across(block, "dp", 1)
    line = stack_three([across(block, "dp", bits) for bits in NEAR[3:0:-1]][::-1])
    return (block, line), (near, across(line, "dp", 1))


def views(single, line):
    return [single, *[line.at[k] for k in range(line.shape[0])]]


def order_of(place, blocks, eight, first=0):
    return [lax.bitwise_xor(place, NEAR[k]) if eight else k for k in range(first, first + blocks)]


def exchange(blocks, axis):
    return lax.all_to_all(blocks, axis, 0, 0, tiled=True)


def dot(left, right):
    return jnp.dot(left, right, preferred_element_type=f32)


def dot_last(left, right):
    return lax.dot_general(left, right, (((1,), (1,)), ((), ())), preferred_element_type=f32)


def dot_first(left, right):
    return lax.dot_general(left, right, (((0,), (0,)), ((), ())), preferred_element_type=f32)


def sigmoid(v):
    return 1.0 / (1.0 + jnp.exp(-v))


def struct(shape, dtype):
    return jax.ShapeDtypeStruct(shape, dtype)


def vmem(count):
    return [pl.BlockSpec(memory_space=pltpu.VMEM)] * count


class Here:
    def __init__(self, refs):
        self.refs = refs

    def __getitem__(self, which):
        return self.refs[which][0]


def seated(kernel):
    def run(place_ref, group_ref, core_ref, *refs):
        kernel(Here((place_ref, group_ref, core_ref)), *refs)

    return run


def params():
    return pltpu.CompilerParams(vmem_limit_bytes=VMEM_LIMIT)


def cost(flops, moved):
    return pl.CostEstimate(flops=int(flops), bytes_accessed=int(moved), transcendentals=0)


def beside(rows):
    half = rows.shape[0] // 2
    return jnp.concatenate([rows[:half], rows[half:]], axis=1)


def apart(wide):
    rank = wide.shape[1] // 2
    return jnp.concatenate([wide[:, :rank], wide[:, rank:]], axis=0)


def near_kernel(here_ref, tokens_ref, factor_ref, router_ref, tokens_out, factor_out, route_out, router_near, sems):
    pairs = ((tokens_ref, tokens_out), (factor_ref, factor_out), (router_ref, router_near))
    copies = [pltpu.make_async_copy(*pair, sems.at[i]) for i, pair in enumerate(pairs)]
    for copy in copies:
        copy.start()
    for copy in copies:
        copy.wait()
    picked = lax.broadcasted_iota(jnp.int32, (router_near.shape[0], 1), 0) == here_ref[1]
    route_out[...] = jnp.sum(jnp.where(picked, router_near[...].astype(f32), 0.0), axis=0, keepdims=True)


def brought_near(tokens, factor, router, here):
    return pl.pallas_call(
        seated(near_kernel),
        in_specs=[pl.BlockSpec(memory_space=pltpu.SMEM)] * 3 + [pl.BlockSpec(memory_space=pl.ANY)] * 3,
        out_specs=vmem(3),
        out_shape=[
            struct(tokens.shape, bf16),
            struct(factor.shape, bf16),
            struct((1, router.shape[1]), f32),
        ],
        scratch_shapes=[pltpu.VMEM(router.shape, bf16), pltpu.SemaphoreType.DMA((3,))],
        compiler_params=params(),
        name="near",
    )(*here, *[pltpu.with_memory_space_constraint(array, pltpu.HBM) for array in (tokens, factor, router)])


def pack_kernel(n_blocks, placer_ref, *refs):
    blocks = refs[:n_blocks]
    outs = refs[n_blocks:]
    capacity, width = outs[0].shape
    chunk = width // 6
    for k in range(6):
        at = slice(k * chunk, (k + 1) * chunk)
        rows = jnp.concatenate([block[:, at] for block in blocks], axis=0)
        packed = dot(placer_ref[...], rows).astype(bf16)
        for step, out in enumerate(outs):
            out[:, at] = packed[step * capacity : (step + 1) * capacity]


def pack(placer, blocks, capacity):
    count, width = placer.shape[0], blocks[0].shape[1]
    return pl.pallas_call(
        functools.partial(pack_kernel, len(blocks)),
        in_specs=vmem(1 + len(blocks)),
        out_specs=vmem(count // capacity),
        out_shape=[struct((capacity, width), bf16)] * (count // capacity),
        compiler_params=params(),
        name="pack",
    )(placer, *blocks)


def low_kernel(n_parts, place_ref, *refs):
    parts, factor_ref, out_ref = refs[:n_parts], refs[n_parts], refs[n_parts + 1]
    depth = factor_ref.shape[1]
    if depth < parts[0].shape[1]:
        at = pl.ds(pl.multiple_of(place_ref[0] * depth, depth), depth)
    else:
        at = slice(None)
    capacity = parts[0].shape[0]
    rows = dot_last(jnp.concatenate([r[:, at] for r in parts], axis=0), factor_ref[...])
    for step in range(n_parts):
        piece = beside(rows[step * capacity : (step + 1) * capacity]).astype(bf16)
        group = lax.rem(place_ref[1] + step, n_parts)
        for i in range(out_ref.shape[0] // (2 * n_parts)):
            spot = (i * n_parts + group) * 2
            out_ref[spot] = piece
            out_ref[spot + 1] = piece


def low_pieces(parts, factor, here, place, n_dp):
    rank, depth = factor.shape
    capacity = parts[0].shape[0]
    if depth % 128:
        parts = [lax.dynamic_slice_in_dim(part, place * depth, depth, 1) for part in parts]
    return pl.pallas_call(
        seated(functools.partial(low_kernel, len(parts))),
        in_specs=[pl.BlockSpec(memory_space=pltpu.SMEM)] * 3 + vmem(len(parts) + 1),
        out_specs=vmem(1)[0],
        out_shape=struct((n_dp * len(parts) * 2, capacity // 2, 2 * rank), bf16),
        compiler_params=params(),
        name="low_pieces",
    )(*here, *parts, factor)


def lift_kernel(n_parts, *refs):
    parts = refs[:n_parts]
    weight_ref, up_ref, route_ref, pre_ref, lifted_ref, gate_ref, weight, up, sems = refs[n_parts:]
    width = parts[0].shape[1]
    steps = sems.shape[1]
    chunk = width // steps
    copies = []
    for k in range(steps):
        at = pl.ds(k * chunk, chunk)
        copies.append(
            (
                pltpu.make_async_copy(weight_ref.at[at], weight.at[at], sems.at[0, k]),
                pltpu.make_async_copy(up_ref.at[at], up.at[at], sems.at[1, k]),
            )
        )
    for pair in copies:
        pair[0].start()
        pair[1].start()
    pre = lifted = logit = 0.0
    for k in range(steps):
        at = slice(k * chunk, (k + 1) * chunk)
        copies[k][0].wait()
        copies[k][1].wait()
        rows = jnp.concatenate([r[:, at] for r in parts], axis=0)
        pre = pre + dot(rows, weight[at])
        lifted = lifted + dot(rows, up[at])
        logit = logit + jnp.sum(rows.astype(f32) * route_ref[:, at], axis=1, keepdims=True)
    pre_ref[...] = pre
    lifted_ref[...] = lifted
    gate_ref[...] = sigmoid(logit)


def lift(parts, gate_weight, up_weight, route):
    capacity, width = parts[0].shape
    units = gate_weight.shape[1]
    count = capacity * len(parts)
    return pl.pallas_call(
        functools.partial(lift_kernel, len(parts)),
        in_specs=vmem(len(parts))
        + [pl.BlockSpec(memory_space=pl.ANY)] * 2
        + vmem(1),
        out_specs=vmem(3),
        scratch_shapes=[
            pltpu.VMEM(gate_weight.shape, bf16),
            pltpu.VMEM(up_weight.shape, bf16),
            pltpu.SemaphoreType.DMA((2, 8)),
        ],
        out_shape=(
            struct((count, units), f32),
            struct((count, units), f32),
            struct((count, 1), f32),
        ),
        cost_estimate=cost(4 * count * width * units, 4 * width * units),
        compiler_params=params(),
        name="lift",
    )(
        *parts,
        pltpu.with_memory_space_constraint(gate_weight, pltpu.HBM),
        pltpu.with_memory_space_constraint(up_weight, pltpu.HBM),
        route,
    )


def bring(source, target, sems, starts):
    copies = []
    for k, start in enumerate(starts):
        at = pl.ds(start, target.shape[2])
        copies.append(pltpu.make_async_copy(source.at[:, at], target.at[k], sems.at[k]))
    for copy in copies:
        copy.start()
    return copies


def down_kernel(
    place_ref, base_ref, lifted_ref, low_ref, factor_ref, weight_ref, own_ref, other_ref, slope_ref, low_out, down_ref, sems
):
    blocks, half, wide = own_ref.shape
    copies = bring(weight_ref, down_ref, sems, [k * wide for k in range(blocks)])
    groups = low_ref.shape[1]
    sums = []
    for core in (place_ref[2], 1 - place_ref[2]):
        for step in range(groups):
            group = lax.rem(place_ref[1] - step + groups, groups)
            sums.append(apart(jnp.sum(low_ref[:, group, core].astype(f32), axis=0)))
    low = jnp.concatenate(sums, axis=0).astype(bf16)
    pre = base_ref[...] + adapter_scale * dot(low, factor_ref[...])
    low_out[...] = low
    lifted = lifted_ref[...]
    sig = sigmoid(pre)
    slope_ref[...] = (lifted * (sig * (1.0 + pre * (1.0 - sig)))).T
    hidden = (pre * sig * lifted).astype(bf16)
    for k in range(blocks):
        if k % 2 == 0:
            copies[k].wait()
            copies[k + 1].wait()
        partial = dot(hidden, down_ref[k]).astype(bf16)
        own_ref[k] = partial[:half]
        other_ref[k] = partial[half:]


def down(base, lifted, low_parts, factor, down_weight, blocks, here):
    count, units = base.shape
    half, width = count // 2, down_weight.shape[1]
    shape = struct((blocks, half, width // blocks), bf16)
    *outs, kept = pl.pallas_call(
        seated(down_kernel),
        in_specs=[pl.BlockSpec(memory_space=pltpu.SMEM)] * 3 + vmem(4) + [pl.BlockSpec(memory_space=pl.ANY)],
        out_specs=vmem(5),
        scratch_shapes=[pltpu.SemaphoreType.DMA((blocks,))],
        out_shape=(
            shape,
            shape,
            struct((units, count), f32),
            struct((count, factor.shape[0]), bf16),
            pltpu.VMEM((blocks, units, width // blocks), bf16),
        ),
        cost_estimate=cost(2 * count * width * units, 2 * width * units),
        compiler_params=params(),
        name="down",
    )(
        *here,
        base,
        lifted,
        low_parts,
        factor,
        pltpu.with_memory_space_constraint(down_weight, pltpu.HBM),
    )
    return *outs, pltpu.with_memory_space_constraint(kept, pltpu.VMEM)


def fold_core_kernel(place_ref, own_ref, got_ref, keep_ref, far_ref, near_ref):
    line, bit = place_ref[0] // 2, lax.rem(place_ref[0], 2)

    def folded(at):
        return (own_ref[at].astype(f32) + got_ref[at].astype(f32)).astype(bf16)

    for k in range(4):
        at = 2 * lax.bitwise_xor(line, k)
        keep_ref[k] = folded(at + bit)
        out_ref = near_ref if k < 2 else far_ref
        out_ref[k % 2] = folded(at + 1 - bit)


def fold_core(own, got, here):
    shapes = [struct((count, *own.shape[1:]), bf16) for count in (4, 2, 2)]
    return pl.pallas_call(
        seated(fold_core_kernel),
        in_specs=[pl.BlockSpec(memory_space=pltpu.SMEM)] * 3 + vmem(2),
        out_specs=vmem(3),
        out_shape=shapes,
        compiler_params=params(),
        name="fold_core",
    )(*here, own, got)


def fold_near_kernel(first, keep_ref, got_ref, *out_refs):
    for k, out_ref in enumerate(out_refs):
        out_ref[...] = (keep_ref[first + k].astype(f32) + got_ref[k].astype(f32)).astype(bf16)


def fold_near(keep, got, first):
    return pl.pallas_call(
        functools.partial(fold_near_kernel, first),
        in_specs=vmem(2),
        out_specs=vmem(2),
        out_shape=[struct(keep.shape[1:], bf16)] * 2,
        compiler_params=params(),
        name="fold_near",
    )(keep, got)


def stack_kernel(*refs):
    for k, ref in enumerate(refs[:-1]):
        refs[-1][k] = ref[...]


def stack_three(arrays):
    return pl.pallas_call(
        stack_kernel,
        in_specs=vmem(len(arrays)),
        out_specs=vmem(1)[0],
        out_shape=struct((len(arrays), *arrays[0].shape), bf16),
        compiler_params=params(),
        name="stack",
    )(*arrays)


def mix_kernel(n_terms, *refs):
    gate_ref, out_ref = refs[n_terms:]
    total = refs[0][...].astype(f32)
    for term in refs[1:n_terms]:
        total = total + term[...].astype(f32)
    out_ref[...] = (gate_ref[: out_ref.shape[0]] * total).astype(bf16)


def mix(terms, gate):
    return pl.pallas_call(
        functools.partial(mix_kernel, len(terms)),
        in_specs=vmem(len(terms) + 1),
        out_specs=vmem(1)[0],
        out_shape=struct(terms[0].shape, bf16),
        compiler_params=params(),
        name="mix",
    )(*terms, gate)


def back_sum(parts, owns, others, order, gate_ref, down_ref, loss_factor):
    wide = owns[0].shape[1]
    scale = loss_factor * gate_ref[...]
    total = 0.0
    for block, own, other in zip(order, owns, others):
        start = block * wide
        at = pl.ds(start if isinstance(start, int) else pl.multiple_of(start, wide), wide)
        mixed = jnp.concatenate([own[...], other[...]], axis=0).astype(f32)
        rows = jnp.concatenate([r[:, at] for r in parts], axis=0).astype(f32)
        back = (scale * (mixed - rows)).astype(bf16)
        total = total + dot_last(down_ref[block], back)
    return total


def back_first_kernel(n_parts, n_blocks, eight, loss_factor, here_ref, *refs):
    parts, refs = refs[:n_parts], refs[n_parts:]
    owns, others, refs = views(*refs[:2]), views(*refs[2:4]), refs[4:]
    gate_ref, down_ref, out_ref = refs
    order = order_of(here_ref[0], n_blocks, eight)
    out_ref[...] = back_sum(parts, owns, others, order, gate_ref, down_ref, loss_factor)


def back_last_kernel(n_parts, n_blocks, eight, loss_factor, here_ref, *refs):
    parts, refs = refs[:n_parts], refs[n_parts:]
    owns, others, refs = views(*refs[:2]), views(*refs[2:4]), refs[4:]
    gate_ref, down_ref, first_ref, slope_ref, factor_ref, low_out, back_out = refs
    order = order_of(here_ref[0], n_blocks, eight, n_blocks)
    total = first_ref[...] + back_sum(parts, owns, others, order, gate_ref, down_ref, loss_factor)
    back_pre = (total * slope_ref[...]).astype(bf16)
    back_low = beside(adapter_scale * dot(factor_ref[...], back_pre)).astype(bf16)
    for i in range(low_out.shape[0]):
        low_out[i] = back_low
    back_out[...] = back_pre


def rest_kernel(n_blocks, eight, here_ref, *refs):
    owns = views(*refs[:2]) + views(*refs[2:4])
    back_ref, low_ref, grad_ref, *homes = refs[4:]
    half, wide = owns[0].shape
    capacity = half // len(homes)
    grad_ref[...] = adapter_scale * lax.dot_general(
        low_ref[...], back_ref[...], (((0,), (1,)), ((), ())), preferred_element_type=f32
    )
    for block, own in zip(order_of(here_ref[0], n_blocks, eight), owns):
        start = block * wide
        at = pl.ds(start if isinstance(start, int) else pl.multiple_of(start, wide), wide)
        for step, home in enumerate(homes):
            home[:, at] = own[step * capacity : (step + 1) * capacity]


def rest(owns, here, eight, back_pre, low, capacity):
    half, wide = owns[0].shape
    homes, blocks = half // capacity, 2 * (1 + owns[1].shape[0])
    return pl.pallas_call(
        seated(functools.partial(rest_kernel, blocks, eight)),
        in_specs=[pl.BlockSpec(memory_space=pltpu.SMEM)] * 3 + vmem(len(owns) + 2),
        out_specs=vmem(1 + homes),
        out_shape=(
            struct((low.shape[1], back_pre.shape[0]), f32),
            *[struct((capacity, wide * blocks), bf16)] * homes,
        ),
        compiler_params=params(),
        name="rest",
    )(*here, *owns, back_pre, low)


def back_first(parts, owns, others, here, eight, gate, kept, loss_factor):
    units = kept.shape[1]
    count, blocks, wide = gate.shape[0], 1 + owns[1].shape[0], owns[0].shape[1]
    return pl.pallas_call(
        seated(functools.partial(back_first_kernel, len(parts), blocks, eight, loss_factor)),
        in_specs=[pl.BlockSpec(memory_space=pltpu.SMEM)] * 3 + vmem(len(parts) + 6),
        out_specs=vmem(1)[0],
        out_shape=struct((units, count), f32),
        cost_estimate=cost(2 * count * blocks * wide * units, 2 * blocks * wide * units),
        compiler_params=params(),
        name="back_first",
    )(*here, *parts, *owns, *others, gate, kept)


def back_last(parts, owns, others, here, eight, gate, kept, first, slope, factor, loss_factor, copies):
    wide = owns[0].shape[1]
    units, count = slope.shape
    rank, blocks = factor.shape[0], 1 + others[1].shape[0]
    return pl.pallas_call(
        seated(functools.partial(back_last_kernel, len(parts), blocks, eight, loss_factor)),
        in_specs=[pl.BlockSpec(memory_space=pltpu.SMEM)] * 3 + vmem(len(parts) + 9),
        out_specs=vmem(2),
        out_shape=(struct((copies, rank // 2, 2 * count), bf16), struct((units, count), bf16)),
        cost_estimate=cost(2 * count * blocks * wide * units, 2 * blocks * wide * units),
        compiler_params=params(),
        name="back_last",
    )(*here, *parts, *owns, *others, gate, kept, first, slope, factor)


def factor_kernel(place_ref, low_ref, piece_ref, out_ref):
    share = out_ref.shape[1]
    groups, count = piece_ref.shape[:2]
    half = count // 2
    group, core = place_ref[1], place_ref[2]
    lows, rows = [], []
    for step in range(groups):
        source = lax.rem(group - step + groups, groups)
        mine = apart(jnp.sum(low_ref[:, source, core].astype(f32), axis=0))
        theirs = apart(jnp.sum(low_ref[:, source, 1 - core].astype(f32), axis=0))
        lows.append(mine + jnp.concatenate([theirs[:, half:], theirs[:, :half]], axis=1))
        rows.append(piece_ref[step, :, :share])
    low = jnp.concatenate(lows, axis=1)
    high = low.astype(bf16)
    rest = (low - high.astype(f32)).astype(bf16)
    out_ref[...] = dot(jnp.concatenate([high, rest], axis=1), jnp.concatenate(rows + rows, axis=0))


def factor_gradient(lows, pieces, share, here):
    rank = 2 * lows.shape[3]
    return pl.pallas_call(
        seated(factor_kernel),
        in_specs=[pl.BlockSpec(memory_space=pltpu.SMEM)] * 3 + vmem(2),
        out_specs=vmem(1)[0],
        out_shape=struct((rank, share), f32),
        compiler_params=params(),
        name="factor_gradient",
    )(*here, lows, pieces)


def shards(
    tokens,
    expert_choice_table,
    gate_weight,
    up_weight,
    down_weight,
    adapter_down_shared,
    adapter_gate_factor,
    router,
):
    tok_rows, width = tokens.shape
    n_dp = lax.axis_size("dp")
    groups = lax.axis_size("x")
    place = lax.axis_index("dp")
    group = lax.axis_index("x")
    core = lax.axis_index("core")
    col_rows = n_dp * tok_rows
    capacity = col_rows // groups
    half = groups * capacity
    wide = width // n_dp
    rank = adapter_down_shared.shape[1]
    devices = n_dp * groups * 2
    share = width // devices
    loss_factor = math.sqrt(groups / (tok_rows * devices))
    blocks = 8
    eight = n_dp == blocks

    here = (place.reshape(1), group.reshape(1), core.reshape(1))

    labels = expert_choice_table[0]
    index = jnp.arange(col_rows, dtype=jnp.int32)
    number = index
    if eight:
        order = lax.bitwise_xor(jnp.array(NEAR, jnp.int32), place)
        number = (order[:, None] * tok_rows + jnp.arange(tok_rows)[None, :]).reshape(col_rows)
        labels = jnp.sum(jnp.where(number[:, None] == index[None, :], labels[None, :], 0), axis=1)
    before = (labels[None, :] == labels[:, None]) & (number[None, :] < number[:, None])
    ordinal = jnp.sum(before.astype(jnp.int32), axis=1)
    ahead = lax.rem(labels - group + groups, groups)
    target = ahead * capacity + ordinal
    placer = (index[:, None] == target[None, :]).astype(bf16)
    tokens_near, factor, own_route = brought_near(tokens, adapter_down_shared.T, router.T, here)
    if eight:
        column, placer = gather_eight(tokens, placer)
        column[0] = tokens_near
        column, placer, factor, own_route = lax.optimization_barrier((column, placer, factor, own_route))
        own_target = target[:tok_rows]
    else:
        column = exchange(jnp.broadcast_to(tokens[None], (n_dp, tok_rows, width)), "dp")
        column = [column.reshape(col_rows, width)]
        own_target = lax.dynamic_slice_in_dim(target, place * tok_rows, tok_rows, 0)
    packed = pack(placer, column, capacity)
    low_parts = low_pieces(packed, factor, here, place, n_dp)
    packed, low_parts = lax.optimization_barrier((packed, low_parts))
    parts = [packed[0]]
    for step in range(1, groups):
        route = [(i, (i + step) % groups) for i in range(groups)]
        parts.append(lax.ppermute(packed[step], "x", route))
    parts = parts + [swap(part, "core") for part in parts]

    low_parts = exchange(low_parts, every).reshape(n_dp, groups, 2, capacity // 2, 2 * rank)
    base, lifted, gate = lift(parts, gate_weight, up_weight, own_route)
    low_parts, gate = lax.optimization_barrier((low_parts, gate))
    own, other, slope, low, kept = down(
        base, lifted, low_parts, adapter_gate_factor, down_weight, blocks, here
    )

    rows = jnp.concatenate(parts, axis=0)
    numbers = jnp.broadcast_to(own_target.astype(bf16)[None], (2 * half, tok_rows))
    pieces = []
    for step in range(groups):
        to = lax.rem(group + step, groups)
        at = ((place * groups + to) * 2 + core) * share
        piece = jnp.concatenate([lax.dynamic_slice_in_dim(rows, at, share, 1), numbers], axis=1)
        route = [(i, (i + step) % groups) for i in range(groups)]
        pieces.append(lax.ppermute(piece, "x", route) if step else piece)
    pieces = jnp.stack(pieces)

    got = swap(other, "core")
    if eight:
        keep, far, near = fold_core(own, got, here)
        far, near, pieces = lax.optimization_barrier((across(far, "dp", 1), near, pieces))
        near = across(near, "dp", 1)
        two, three = fold_near(keep, far, 2)
        mine, one = fold_near(keep, near, 0)
        terms = [mine, across(one, "dp", 2), across(two, "dp", 4), across(three, "dp", 6)]
        owns = gather_pairs(mix(terms, gate))
    else:
        summed = (own.astype(f32) + got.astype(f32)).astype(bf16)
        summed = summed.transpose(1, 0, 2).reshape(half, n_dp, wide).transpose(1, 0, 2)
        summed = exchange(summed, "dp")
        mixed = mix([summed[i] for i in range(n_dp)], gate)
        mixed = exchange(jnp.broadcast_to(mixed[None], (n_dp, half, wide)), "dp")
        mixed = mixed.transpose(1, 0, 2).reshape(half, width)
        owns = [mixed[:, i * (width // blocks) : (i + 1) * (width // blocks)] for i in range(blocks)]
        owns = [(owns[k], jnp.stack(owns[k + 1 : k + blocks // 2])) for k in (0, blocks // 2)]
    others = [[swap(block, "core") for block in pair] for pair in owns]

    first = back_first(
        parts, owns[0], others[0], here, eight, gate, kept, loss_factor
    )
    back_low, back_pre = back_last(
        parts,
        owns[1],
        others[1],
        here,
        eight,
        gate,
        kept,
        first,
        slope,
        adapter_gate_factor,
        loss_factor,
        devices,
    )
    lows = exchange(back_low, every).reshape(n_dp, groups, 2, rank // 2, 4 * half)
    grad_b, *homes = rest([*owns[0], *owns[1]], here, eight, back_pre, low, capacity)

    result = jnp.zeros((tok_rows, width), f32)
    for step in range(groups):
        spot = index[step * capacity : (step + 1) * capacity]
        wanted = pieces[step, 0, share:].astype(jnp.int32)
        chooser = (wanted[:, None] == spot[None, :]).astype(bf16)
        chosen = dot(chooser, homes[step])
        if step:
            route = [(i, (i - step) % groups) for i in range(groups)]
            chosen = lax.ppermute(chosen.astype(bf16), "x", route).astype(f32)
        result = result + chosen

    grad_a = factor_gradient(lows, pieces, share, here)
    return (result.astype(bf16), grad_a.T, grad_b.T)


def solution(mesh):
    n_dp, n_expert = mesh.shape["dp"], mesh.shape["expert"]
    split = Mesh(mesh.devices.reshape(n_dp, n_expert // 2, 2), every)
    return jax.shard_map(
        shards,
        mesh=split,
        in_specs=(
            P(every, None),
            P(("x", "core"), None),
            P(None, every),
            P(None, every),
            P(every, None),
            P("dp", None),
            P(None, every),
            P(),
        ),
        out_specs=(P(every, None), P(every, None), P(every, None)),
        check_vma=False,
    )
```
